128 devices in a mesh: freq: 4 (over z), grid: 32 (over y, x, core).
Axes of the slice: x: 4, y: 4, z: 4, core: 2. Of those that a mesh axis runs over, the one named last changes fastest.
Arguments:
- green_spectra: bfloat16 [2, 8, 2048, 8192], P(None, 'freq', None, 'grid'), may hold values from -6 to 6
- source_psd: float32 [8, 8192], P('freq', 'grid'), may hold values from 0.2 to 5
- pair_list: int32 [64, 2], replicated, may hold values from 0 to 15, as said below
- owner_map: int32 [64], replicated, may hold values from 0 to 31, as said below
- observed: bfloat16 [64, 128, 128, 128], P('grid'), may hold values from -48 to 48
Outputs:
- gradient: float32 [8, 8192], P('freq', 'grid')
- misfit: float32 [64, 128], P('grid', 'freq')
The draws below stay inside these ranges and needn't reach their ends.
Inputs may be any that keep to these rules, and one draw needn't show every extreme that they name: `pair_list`: each row names two different station blocks, the smaller first; no pair of blocks is listed twice. `owner_map`: each owner appears exactly 2 times.
All inputs are finite; a program needn't handle non-finite values.
Results may differ from the reference program's by a relative error of at most 0.0014.
Values may be sent and summed in bfloat16 or wider, within the bound.
A program may use at most 128 MiB of HBM per device.

```python
import math
import jax
import jax.numpy as jnp
from jax import lax

STATIONS = 2048
STATION_BLOCK = 128
LAG_LENGTH = 128
PAIR_DEV = 2
FREQUENCY_COUNT = 8
GRID = 8192
PAIR_SLOTS = 64


def draw_pair_list(key, part):
    key = jax.random.fold_in(key, 17)
    block_count = STATIONS // STATION_BLOCK
    pair_count_total = block_count * (block_count - 1) // 2
    first_ids, second_ids = jnp.triu_indices(block_count, 1)
    first_ids = first_ids.astype(jnp.int32)
    second_ids = second_ids.astype(jnp.int32)
    selected_pairs = 1 + jax.random.permutation(key, pair_count_total - 2)[:PAIR_SLOTS - 2].astype(jnp.int32)
    chosen = jnp.concatenate([jnp.array([0, pair_count_total - 1], dtype=jnp.int32), selected_pairs])
    reorder_pairs = jax.random.permutation(jax.random.fold_in(key, 5), PAIR_SLOTS)
    chosen = chosen[reorder_pairs]
    return jnp.stack([first_ids[chosen], second_ids[chosen]], axis=1).astype(jnp.int32)


def draw_owner_map(key, part):
    key = jax.random.fold_in(key, 29)
    reordered_pairs = jax.random.permutation(key, PAIR_SLOTS).astype(jnp.int32)
    return (reordered_pairs // PAIR_DEV).astype(jnp.int32)


def shard_levels(stream_key, dims, cuts, smallest, largest):
    loudness, own = 1.0, jax.random.fold_in(stream_key, 6)
    for dim, shards_of in cuts:
        steps = jnp.exp(jax.random.uniform(jax.random.fold_in(own, dim), (shards_of,), jnp.float32, smallest / len(cuts), largest / len(cuts)))
        loudness = loudness * jnp.repeat(steps, dims[dim] // shards_of).reshape([-1 if axis == dim else 1 for axis in range(len(dims))])
    return loudness


def gaussian(key, extent, deviation, most, pieces=(), kind=jnp.bfloat16):
    result = deviation * jax.random.normal(key, extent, jnp.float32)
    if pieces:
        result = result * shard_levels(key, extent, pieces, -0.22, 0.18)
    return jnp.clip(result, -most, most).astype(kind)


def setup_inputs(seed: int = 0) -> dict:
    keys = jax.random.split(jax.random.key(seed), 6)
    return {
        "green_spectra": gaussian(keys[0], (2, FREQUENCY_COUNT, STATIONS, GRID), 1.0, 6.0, ((1, 4), (3, 32))),
        "source_psd": jnp.clip(jnp.exp(math.log(5.0) - 3.218876 * jax.random.uniform(keys[1], (FREQUENCY_COUNT, GRID), jnp.float32) ** shard_levels(keys[1], (FREQUENCY_COUNT, GRID), ((0, 4), (1, 32)), -0.2, 0.2)), 0.2, 5.0),
        "pair_list": draw_pair_list(jax.random.fold_in(keys[5], 71), 0),
        "owner_map": draw_owner_map(jax.random.fold_in(keys[5], 71), 0),
        "observed": gaussian(keys[4], (PAIR_SLOTS, STATION_BLOCK, STATION_BLOCK, LAG_LENGTH), 8.0, 48.0, ((0, 32),)),
    }


harmonic_step = 3

def phase_values(freq_total, lag_count):
    freq_ids = jnp.arange(freq_total, dtype=jnp.int32)[:, None]
    lag_ids = jnp.arange(lag_count, dtype=jnp.int32)[None, :]
    turns = (harmonic_step * (freq_ids + 1) * lag_ids % lag_count).astype(jnp.float32)
    angles = turns * jnp.float32(2.0 * math.pi / lag_count)
    return jnp.stack((jnp.cos(angles), -jnp.sin(angles)))

def reference(green_spectra, source_psd, pair_list, owner_map, observed):
    highest = lax.Precision.HIGHEST
    slot_order = jnp.argsort(owner_map, stable=True).astype(jnp.int32)
    first_blocks = pair_list[slot_order, 0]
    second_blocks = pair_list[slot_order, 1]
    block_pairs = jnp.stack((first_blocks, second_blocks), axis=1)
    block_count = STATIONS // STATION_BLOCK

    def cross_at(freq_id):
        spectra = green_spectra[:, freq_id]
        weighted = (spectra.astype(jnp.float32) * source_psd[freq_id][None, None, :]).astype(jnp.bfloat16)
        plain_blocks = spectra.reshape(2, block_count, STATION_BLOCK, GRID)
        weighted_blocks = weighted.reshape(2, block_count, STATION_BLOCK, GRID)

        def cross_slot(block_ids):
            left_block = weighted_blocks[:, block_ids[0]].astype(jnp.float32)
            right_block = plain_blocks[:, block_ids[1]].astype(jnp.float32)
            real_part = jnp.einsum('cix,cjx->ij', left_block, right_block, precision=highest)
            imag_part = jnp.einsum('ix,jx->ij', left_block[1], right_block[0], precision=highest) - jnp.einsum('ix,jx->ij', left_block[0], right_block[1], precision=highest)
            return jnp.stack((real_part, imag_part))
        return lax.map(cross_slot, block_pairs)
    cross = lax.map(cross_at, jnp.arange(FREQUENCY_COUNT, dtype=jnp.int32)) * jnp.float32(1.0 / math.sqrt(GRID))
    phases = phase_values(FREQUENCY_COUNT, LAG_LENGTH)
    modelled = jnp.einsum('fskij,kft->sijt', cross, phases, precision=highest)
    residual = modelled - observed.astype(jnp.float32)
    misfit = lax.optimization_barrier(jnp.sum(residual * residual, axis=(2, 3))) / jnp.float32(2.0 * STATION_BLOCK * LAG_LENGTH * FREQUENCY_COUNT)
    adjoint = (jnp.einsum('sijt,kft->fskij', residual, phases, precision=highest) / jnp.float32(LAG_LENGTH)).astype(jnp.bfloat16)

    def gradient_for(freq_id):
        plain_blocks = green_spectra[:, freq_id].reshape(2, block_count, STATION_BLOCK, GRID)

        def add_slot(running, inputs):
            block_ids, weights = inputs
            left_block = plain_blocks[:, block_ids[0]].astype(jnp.float32)
            right_block = plain_blocks[:, block_ids[1]].astype(jnp.float32)
            weights = weights.astype(jnp.float32)
            along_term = jnp.dot(weights[0], right_block[0], precision=highest) - jnp.dot(weights[1], right_block[1], precision=highest)
            across_term = jnp.dot(weights[0], right_block[1], precision=highest) + jnp.dot(weights[1], right_block[0], precision=highest)
            return (running + lax.optimization_barrier(jnp.sum(left_block[0] * along_term + left_block[1] * across_term, axis=0)), None)
        return lax.scan(add_slot, jnp.zeros((GRID,), jnp.float32), (block_pairs, adjoint[freq_id]))[0]
    gradient = lax.map(gradient_for, jnp.arange(FREQUENCY_COUNT, dtype=jnp.int32)) * jnp.float32(1.0 / (STATION_BLOCK * math.sqrt(PAIR_SLOTS)))
    return (gradient, misfit)
```

```python
import functools
import math

import jax
import jax.numpy as jnp
import ml_dtypes
import numpy as np
from jax import lax
from jax.experimental import pallas as pl
from jax.experimental.pallas import tpu as pltpu
from jax.sharding import PartitionSpec as P

harmonic_step = 3
side = 4
stages = 2
pieces = 3
group = 8
MESH = pl.DeviceIdType.MESH
f32 = jnp.float32
bf16 = jnp.bfloat16


def phase_table(freq_total, lag_count, freq_devices):
    freq_ids = np.arange(freq_total)[:, None]
    turns = harmonic_step * (freq_ids + 1) * np.arange(lag_count)[None, :] % lag_count
    angles = turns * (2.0 * math.pi / lag_count)
    exact = np.stack((np.cos(angles), -np.sin(angles)), axis=1)
    parts = []
    for unused in range(pieces):
        part = exact.astype(ml_dtypes.bfloat16)
        parts.append(part)
        exact = exact - part.astype(np.float64)
    table = np.stack(parts).reshape(pieces, freq_devices, 2, 2, lag_count)
    both = np.stack((table, table[:, :, ::-1]), axis=2)
    both = both.transpose(1, 2, 0, 3, 4, 5).reshape(freq_devices * 2, pieces * 4, lag_count)
    return np.repeat(both, group, axis=1)


def kernel(
    freq_devices,
    ids,
    psd,
    table,
    green,
    observed,
    gradient_out,
    misfit_out,
    gbuf,
    wbuf,
    psd_other,
    obs,
    phi,
    spread,
    ohat,
    ohat_send,
    energy,
    send1,
    recv1,
    send_a,
    recv_a,
    send_b,
    recv_b,
    keep,
    abuf,
    total,
    mis_own,
    mis_other,
    mis_pair,
    mis_freq,
    gsum,
    gsend,
    grecv,
    local_sem,
    core_send,
    core_recv,
    one_send,
    one_recv,
    a_send,
    a_recv,
    b_send,
    b_recv,
    g1_send,
    g1_recv,
    g1f_send,
    g1f_recv,
    g2_send,
    g2_recv,
    g2f_send,
    g2f_recv,
    z_send,
    z_recv,
):
    z = lax.axis_index("freq")
    g = lax.axis_index("grid")
    c = g % 2
    x = (g // 2) % side
    y = g // (2 * side)
    other = g + 1 - 2 * c
    points = psd.shape[1]
    pair_dev, block, unused_cols, lags = observed.shape
    freq_total = 2 * freq_devices
    slot_count = 2 * side * side * pair_dev
    root_scale = 1.0 / math.sqrt(points * 2 * side * side)

    def neighbour(axis, d):
        step = 1 + 2 * d
        nx = (x + (1 - axis) * step) % side
        ny = (y + axis * step) % side
        return (ny * side + nx) * 2 + c

    def slot_of(t, h, o, r):
        sx = (x + (1 - h) * o + h * r) % side
        sy = (y + h * o + (1 - h) * r) % side
        return (sy * side + sx) * 4 + h * 2 + t

    def lane(d, j):
        return (1 - d) * (2 - 2 * j) + d * (1 + 2 * j)

    def lane_place(r):
        return ((r + 1) // 2 + 1) % 2

    def remote(src, dst, send, recv, device):
        return pltpu.make_async_remote_copy(
            src_ref=src, dst_ref=dst, send_sem=send, recv_sem=recv,
            device_id={"grid": device}, device_id_type=MESH,
        )

    own_points = pl.ds(0, points)
    other_points = pl.ds(points, points)
    load_green = [
        pltpu.make_async_copy(green.at[k, c], gbuf.at[k, :, :, own_points], local_sem.at[k])
        for k in range(2)
    ]
    load_table = pltpu.make_async_copy(table.at[z * 2 + c], phi, local_sem.at[2])
    load_obs = pltpu.make_async_copy(observed, obs, local_sem.at[3])
    for copy in load_green:
        copy.start()
    load_table.start()
    load_obs.start()

    barrier = pltpu.get_barrier_semaphore()
    friends = [{"grid": other}]
    for axis in range(2):
        for d in range(2):
            friends.append({"grid": neighbour(axis, d)})
    for dz in range(1, freq_devices):
        friends.append({"freq": (z + dz) % freq_devices})
    for friend in friends:
        pl.semaphore_signal(barrier, inc=1, device_id=friend, device_id_type=MESH)
    pl.semaphore_wait(barrier, len(friends))

    swap_psd = remote(psd, psd_other, core_send.at[2], core_recv.at[2], other)
    swap_green = [
        remote(
            green.at[k, 1 - c], gbuf.at[k, :, :, other_points], core_send.at[k], core_recv.at[k], other
        )
        for k in range(2)
    ]
    swap_psd.start()
    for copy in swap_green:
        copy.start()

    def weigh(k, where, row):
        def body(b, carry):
            wbuf[k, b, :, where] = (gbuf[k, b, :, where].astype(f32) * row).astype(bf16)
            return carry

        lax.fori_loop(0, gbuf.shape[1], body, 0)

    own_row = psd[pl.ds(c, 1), :]
    for k in range(2):
        load_green[k].wait()
        weigh(k, own_points, own_row)
    swap_psd.wait_recv()
    other_row = psd_other[pl.ds(c, 1), :]
    for k in range(2):
        swap_green[k].wait_recv()
        weigh(k, other_points, other_row)

    load_table.wait()
    rows = phi.shape[0]
    row_in_group = lax.broadcasted_iota(jnp.int32, (rows, lags), 0) % group
    phi_values = phi[...].astype(f32)
    for i in range(group):
        spread[:, pl.ds(i * lags, lags)] = jnp.where(row_in_group == i, phi_values, 0.0).astype(bf16)

    def unit(slot):
        left = wbuf[:, ids[slot]].reshape(2 * block, 2 * points)
        right = gbuf[:, ids[slot_count + slot]].reshape(2 * block, 2 * points)
        acc = lax.dot_general(left, right, (((1,), (1,)), ((), ())), preferred_element_type=f32)
        real = acc[:block, :block] + acc[block:, block:]
        imag = acc[block:, :block] - acc[:block, block:]
        return real, imag

    def copy1(n):
        u = n % 8
        return remote(
            send1.at[n], recv1.at[n], one_send.at[n], one_recv.at[n], neighbour(u % 2, (u // 2) % 2)
        )

    def first_ring(low, high):
        def body(n, carry):
            t = n // 24
            role = (n % 24) // 8
            u = n % 8
            h, d, j = u % 2, (u // 2) % 2, u // 4
            near = 1 + 2 * d
            o = jnp.where(role == 0, 2, near)
            r = jnp.where(role == 1, lane(1 - d, j), lane(d, j))
            real, imag = unit(slot_of(t, h, o, r))

            @pl.when(role == 2)
            def _():
                copy1(n - 16).wait_recv()
                send1[n, 0] = (real + recv1[n - 16, 0].astype(f32)).astype(bf16)
                send1[n, 1] = (imag + recv1[n - 16, 1].astype(f32)).astype(bf16)

            @pl.when(role != 2)
            def _():
                send1[n, 0] = real.astype(bf16)
                send1[n, 1] = imag.astype(bf16)

            copy1(n).start()
            return carry

        lax.fori_loop(low, high, body, 0)

    def arrival1(t, h, d, r):
        role = 2 - (r + d) % 2
        return t * 24 + role * 8 + lane_place(r) * 4 + d * 2 + h

    def line_sum(t, h, r):
        real, imag = unit(slot_of(t, h, 0, r))
        for d in range(2):
            n = arrival1(t, h, d, r)
            copy1(n).wait_recv()
            real = real + recv1[n, 0].astype(f32)
            imag = imag + recv1[n, 1].astype(f32)
        return real, imag

    def place(t, h, d):
        return (t * 2 + h) * 2 + d

    def copy_a(t, h, d):
        i = place(t, h, d)
        return remote(send_a.at[i], recv_a.at[i], a_send.at[i], a_recv.at[i], neighbour(1 - h, d))

    def copy_b(t, h, d, k):
        i = place(t, h, d)
        return remote(
            send_b.at[i, k], recv_b.at[i, k], b_send.at[i * 2 + k], b_recv.at[i * 2 + k],
            neighbour(1 - h, d),
        )

    def second_ring_open(t):
        def body(v, carry):
            h, w = v % 2, v // 2
            r = jnp.where(w == 0, 2, 2 * w - 1)
            real, imag = line_sum(t, h, r)

            @pl.when(w == 0)
            def _():
                send_a[place(t, h, 0)] = real.astype(bf16)
                copy_a(t, h, 0).start()
                send_a[place(t, h, 1)] = imag.astype(bf16)
                copy_a(t, h, 1).start()

            @pl.when(w == 1)
            def _():
                i = place(t, h, 0)
                send_b[i, 1] = imag.astype(bf16)
                keep[i] = real
                copy_b(t, h, 0, 1).start()

            @pl.when(w == 2)
            def _():
                i = place(t, h, 1)
                send_b[i, 0] = real.astype(bf16)
                keep[i] = imag
                copy_b(t, h, 1, 0).start()

            return carry

        lax.fori_loop(0, 6, body, 0)

    def second_ring_close(t):
        def body(v, carry):
            h, d = v % 2, v // 2
            i = place(t, h, d)
            copy_a(t, h, d).wait_recv()
            send_b[i, d] = (keep[i] + recv_a[i].astype(f32)).astype(bf16)
            copy_b(t, h, d, d).start()
            return carry

        lax.fori_loop(0, 4, body, 0)

    def copy_g1(t, h, d):
        s, i = slot_of(t, h, 0, 0), place(t, h, d)
        return remote(abuf.at[s], abuf.at[s], g1_send.at[i], g1_recv.at[i], neighbour(1 - h, d))

    def copy_g1f(t, h, d):
        s, i = slot_of(t, h, 0, 3 - 2 * d), place(t, h, d)
        return remote(abuf.at[s, d], abuf.at[s, d], g1f_send.at[i], g1f_recv.at[i], neighbour(1 - h, d))

    def copy_g2(t, h, d, r):
        s, i = slot_of(t, h, 0, r), place(t, h, d) * 4 + r
        return remote(abuf.at[s], abuf.at[s], g2_send.at[i], g2_recv.at[i], neighbour(h, d))

    def copy_g2f(t, h, d, j):
        s, i = slot_of(t, h, 3 - 2 * d, lane(d, j)), place(t, h, d) * 2 + j
        return remote(abuf.at[s], abuf.at[s], g2f_send.at[i], g2f_recv.at[i], neighbour(h, d))

    ones = jnp.ones((8, block), f32)

    def lane_sum(values):
        return lax.dot_general(
            ones[:, : values.shape[1]], values, (((1,), (1,)), ((), ())),
            precision=lax.Precision.HIGHEST, preferred_element_type=f32,
        )

    def own_adjoint(t):
        def body(h, carry):
            real, imag = line_sum(t, h, 0)
            for d in range(2):
                i = place(t, h, d)
                for k in range(2):
                    copy_b(t, h, d, k).wait_recv()
                real = real + recv_b[i, 0].astype(f32)
                imag = imag + recv_b[i, 1].astype(f32)
            s = slot_of(t, h, 0, 0)
            q = h * 2 + t
            kept = jnp.zeros_like(real)
            for k, value in enumerate((real, imag)):
                cross = value * f32(root_scale)
                seen = ohat[q, k]
                abuf[s, k] = (0.5 * cross - seen * f32(1.0 / lags)).astype(bf16)
                kept = kept + cross * (f32(lags / 2) * cross - 2.0 * seen)
            for d in range(2):
                copy_g1(t, h, d).start()
            for d in range(2):
                copy_g2(t, h, d, 0).start()
            total[q] = kept
            return carry

        lax.fori_loop(0, 2, body, 0)

    def gather_1(t):
        def body(v, carry):
            h, d = v % 2, v // 2
            copy_g1(t, h, d).wait_recv()
            copy_g1f(t, h, d).start()
            for side_d in range(2):
                copy_g2(t, h, side_d, 3 - 2 * d).start()
            return carry

        lax.fori_loop(0, 4, body, 0)

    def gather_2(t):
        def body(h, carry):
            for d in range(2):
                copy_g1f(t, h, d).wait_recv()
            for d in range(2):
                copy_g2(t, h, d, 2).start()
            return carry

        lax.fori_loop(0, 2, body, 0)

    def gather_lane(t, r):
        e = r % 2
        j = lane_place(r)

        def body(h, carry):
            copy_g2(t, h, e, r).wait_recv()
            copy_g2f(t, h, e, j).start()
            copy_g2(t, h, 1 - e, r).wait_recv()
            return carry

        lax.fori_loop(0, 2, body, 0)

    def gather_end(t, r):
        def body(h, carry):
            copy_g2f(t, h, r % 2, lane_place(r)).wait_recv()
            return carry

        lax.fori_loop(0, 2, body, 0)

    def back(t, count, choose):
        def body(v, carry):
            h, w = v % 2, v // 2
            o, r = choose(w)
            s = slot_of(t, h, o, r)
            weights = abuf[s]
            top = jnp.concatenate((weights[0], -weights[1]), axis=1)
            low = jnp.concatenate((weights[1], weights[0]), axis=1)
            right = gbuf[:, ids[slot_count + s]].reshape(2 * block, 2 * points)
            moved = jnp.dot(
                jnp.concatenate((top, low), axis=0), right, preferred_element_type=f32
            )
            left = gbuf[:, ids[s]].reshape(2 * block, 2 * points).astype(f32)
            return carry + jnp.sum((moved * left).reshape(2 * block // 8, 8, 2 * points), axis=0)

        gsum[...] = lax.fori_loop(0, 2 * count, body, gsum[...])

    def project():
        load_obs.wait()

        def body(i, carry):
            first = pl.multiple_of(i * group, group)
            seen = jnp.concatenate(
                [
                    jnp.concatenate([obs[s, first + k] for k in range(group)], axis=1)
                    for s in range(pair_dev)
                ],
                axis=0,
            )
            out = lax.dot_general(
                spread[...], seen, (((1,), (1,)), ((), ())), preferred_element_type=f32
            )
            out = jnp.sum(out.reshape(pieces, 4 * group, pair_dev * block), axis=0)
            for s in range(pair_dev):
                for k in range(2):
                    cols = slice(s * block, (s + 1) * block)
                    ohat[2 * c + s, k, pl.ds(first, group), :] = out[k * group : (k + 1) * group, cols]
                    ohat_send[s, k, pl.ds(first, group), :] = out[(2 + k) * group : (3 + k) * group, cols]
            return carry

        lax.fori_loop(0, block // group, body, 0)

    swap_ohat = remote(
        ohat_send, ohat.at[pl.ds(2 * c, 2)], core_send.at[3], core_recv.at[3], other
    )
    part_rows = block // freq_devices

    def energies():
        def body(i, carry):
            for s in range(pair_dev):
                seen = obs[s, z * part_rows + i].astype(f32)
                energy[pl.ds(s * part_rows + i, 1), :] = jnp.sum(seen * seen, axis=0, keepdims=True)
            return carry

        lax.fori_loop(0, part_rows, body, 0)

    gsum[...] = jnp.zeros_like(gsum)
    first_ring(0, 40)
    second_ring_open(0)
    project()
    swap_ohat.start()
    first_ring(40, 48)
    second_ring_close(0)
    swap_ohat.wait_recv()
    own_adjoint(0)
    second_ring_open(1)
    gather_1(0)
    second_ring_close(1)
    own_adjoint(1)
    gather_2(0)
    back(0, 1, lambda w: (0, 0))
    gather_lane(0, 0)
    gather_1(1)
    back(1, 1, lambda w: (0, 0))
    back(0, 2, lambda w: (1 + 2 * w, 0))
    gather_2(1)
    gather_lane(1, 0)
    back(0, 3, lambda w: (0, 1 + w))
    energies()
    gather_lane(0, 1)
    gather_lane(0, 3)
    back(1, 2, lambda w: (1 + 2 * w, 0))
    back(1, 3, lambda w: (0, 1 + w))

    mis_own[...] = jnp.zeros_like(mis_own)
    for q in range(2 * stages):
        mis_own[pl.ds(q, 1), :] = lane_sum(total[q])[:1]
    swap_mis = remote(mis_own, mis_other, core_send.at[4], core_recv.at[4], other)
    swap_mis.start()

    back(0, 4, lambda w: (1 + 2 * (w % 2), 1 + 2 * (w // 2)))
    gather_lane(0, 2)
    gather_lane(1, 1)
    gather_lane(1, 3)
    swap_mis.wait_recv()
    mis_pair[...] = mis_own[...] + mis_other[...]

    def copy_z(dz):
        return pltpu.make_async_remote_copy(
            src_ref=mis_pair, dst_ref=mis_freq.at[dz - 1],
            send_sem=z_send.at[dz - 1], recv_sem=z_recv.at[dz - 1],
            device_id={"freq": (z + dz) % freq_devices}, device_id_type=MESH,
        )

    for dz in range(1, freq_devices):
        copy_z(dz).start()
    back(0, 2, lambda w: (1 + 2 * w, 2))
    back(1, 4, lambda w: (1 + 2 * (w % 2), 1 + 2 * (w // 2)))
    gather_lane(1, 2)
    back(1, 2, lambda w: (1 + 2 * w, 2))

    mine = mis_pair[...]
    for dz in range(1, freq_devices):
        copy_z(dz).wait_recv()
        mine = mine + mis_freq[dz - 1]
    mis_own_sum = lane_sum(energy[...])[:1]
    picked = jnp.zeros((mine.shape[0], part_rows), f32)
    for part in range(freq_devices):
        picked = jnp.where(z == part, mine[:, part * part_rows : (part + 1) * part_rows], picked)
    for s in range(pair_dev):
        row = jnp.where(c == 0, picked[s : s + 1], picked[2 + s : 3 + s])
        row = row + mis_own_sum[:, s * part_rows : (s + 1) * part_rows]
        misfit_out[pl.ds(s, 1), :] = row * f32(1.0 / (2.0 * block * lags * freq_total))

    for t in range(stages):
        for r in (0, 1, 3, 2):
            gather_end(t, r)
            back(t, 1, lambda w: (2, r))

    lines = jnp.sum(gsum[...], axis=0, keepdims=True) * f32(1.0 / (block * math.sqrt(slot_count)))
    gsend[...] = jnp.broadcast_to(lines[:, points:], gsend.shape)
    swap_sum = remote(gsend, grecv, core_send.at[5], core_recv.at[5], other)
    swap_sum.start()
    swap_sum.wait_recv()
    row_ids = lax.broadcasted_iota(jnp.int32, (2, points), 0)
    gradient_out[...] = jnp.where(
        row_ids == c, jnp.broadcast_to(lines[:, :points], (2, points)), grecv[:2]
    )

    swap_psd.wait_send()
    for copy in swap_green:
        copy.wait_send()
    swap_ohat.wait_send()
    swap_mis.wait_send()
    swap_sum.wait_send()
    for dz in range(1, freq_devices):
        copy_z(dz).wait_send()

    def leave1(n, carry):
        copy1(n).wait_send()
        return carry

    lax.fori_loop(0, 48, leave1, 0)

    def leave2(v, carry):
        t, h, d = v // 4, (v // 2) % 2, v % 2
        copy_a(t, h, d).wait_send()
        for k in range(2):
            copy_b(t, h, d, k).wait_send()
        copy_g1(t, h, d).wait_send()
        copy_g1f(t, h, d).wait_send()
        for r in range(4):
            copy_g2(t, h, d, r).wait_send()
        for j in range(2):
            copy_g2f(t, h, d, j).wait_send()
        return carry

    lax.fori_loop(0, 8, leave2, 0)


def local(green_spectra, source_psd, pair_list, owner_map, observed):
    freq_devices = lax.axis_size("freq")
    planes, freq_dev, stations, points = green_spectra.shape
    pair_dev, block, unused_cols, lags = observed.shape
    slot_count = owner_map.shape[0]
    blocks = stations // block
    freq_total = freq_dev * freq_devices
    places = jnp.arange(slot_count, dtype=jnp.int32)
    earlier = (owner_map[None, :] < owner_map[:, None]) | (
        (owner_map[None, :] == owner_map[:, None]) & (places[None, :] < places[:, None])
    )
    slot_of_entry = jnp.sum(earlier.astype(jnp.int32), axis=1)
    hit = slot_of_entry[None, :] == places[:, None]
    ids = jnp.sum(jnp.where(hit[None], pair_list.T[:, None, :], 0), axis=2).reshape(2 * slot_count)
    table = jnp.asarray(phase_table(freq_total, lags, freq_devices))
    rows = table.shape[1]
    units = stages * 2 * 2
    dma = pltpu.SemaphoreType.DMA
    vmem = pl.BlockSpec(memory_space=pltpu.VMEM)
    anywhere = pl.BlockSpec(memory_space=pl.ANY)
    pair = (2, block, block)
    gradient, misfit = pl.pallas_call(
        functools.partial(kernel, freq_devices),
        out_shape=(
            jax.ShapeDtypeStruct((freq_dev, points), f32),
            jax.ShapeDtypeStruct((pair_dev, block // freq_devices), f32),
        ),
        in_specs=[pl.BlockSpec(memory_space=pltpu.SMEM), vmem, anywhere, anywhere, anywhere],
        out_specs=(vmem, vmem),
        scratch_shapes=[
            pltpu.VMEM((2, blocks, block, 2 * points), bf16),
            pltpu.VMEM((2, blocks, block, 2 * points), bf16),
            pltpu.VMEM((freq_dev, points), f32),
            pltpu.VMEM((pair_dev, block, block, lags), bf16),
            pltpu.VMEM((rows, lags), bf16),
            pltpu.VMEM((rows, group * lags), bf16),
            pltpu.VMEM((2 * pair_dev,) + pair, f32),
            pltpu.VMEM((pair_dev,) + pair, f32),
            pltpu.VMEM((pair_dev * (block // freq_devices), lags), f32),
            pltpu.VMEM((24 * stages,) + pair, bf16),
            pltpu.VMEM((24 * stages,) + pair, bf16),
            pltpu.VMEM((units, block, block), bf16),
            pltpu.VMEM((units, block, block), bf16),
            pltpu.VMEM((units,) + pair, bf16),
            pltpu.VMEM((units,) + pair, bf16),
            pltpu.VMEM((units, block, block), f32),
            pltpu.VMEM((slot_count,) + pair, bf16),
            pltpu.VMEM((2 * stages, block, block), f32),
            pltpu.VMEM((8, block), f32),
            pltpu.VMEM((8, block), f32),
            pltpu.VMEM((8, block), f32),
            pltpu.VMEM((freq_devices - 1, 8, block), f32),
            pltpu.VMEM((8, 2 * points), f32),
            pltpu.VMEM((8, points), f32),
            pltpu.VMEM((8, points), f32),
            dma((4,)),
            dma((6,)),
            dma((6,)),
            dma((24 * stages,)),
            dma((24 * stages,)),
            dma((units,)),
            dma((units,)),
            dma((2 * units,)),
            dma((2 * units,)),
            dma((units,)),
            dma((units,)),
            dma((units,)),
            dma((units,)),
            dma((4 * units,)),
            dma((4 * units,)),
            dma((2 * units,)),
            dma((2 * units,)),
            dma((freq_devices - 1,)),
            dma((freq_devices - 1,)),
        ],
        compiler_params=pltpu.CompilerParams(
            collective_id=0, has_side_effects=True, vmem_limit_bytes=48 * 1024 * 1024
        ),
        cost_estimate=pl.CostEstimate(
            flops=8 * slot_count * freq_dev * 2 * block * block * points,
            bytes_accessed=12 * 1024 * 1024,
            transcendentals=0,
        ),
        name="misfit_gradient",
    )(
        ids,
        source_psd,
        table,
        green_spectra.reshape(planes, freq_dev, blocks, block, points),
        observed,
    )
    return (gradient, misfit)


def solution(mesh):
    in_specs = (
        P(None, "freq", None, "grid"),
        P("freq", "grid"),
        P(),
        P(),
        P("grid", None, None, None),
    )
    out_specs = (P("freq", "grid"), P("grid", "freq"))
    return jax.shard_map(local, mesh=mesh, in_specs=in_specs, out_specs=out_specs, check_vma=False)
```

```python
import functools
import math

import jax
import jax.numpy as jnp
import ml_dtypes
import numpy as np
from jax import lax
from jax.experimental import pallas as pl
from jax.experimental.pallas import tpu as pltpu
from jax.sharding import PartitionSpec as P

harmonic_step = 3
side = 4
stages = 2
pieces = 3
group = 8
MESH = pl.DeviceIdType.MESH
f32 = jnp.float32
bf16 = jnp.bfloat16


def phase_table(freq_total, lag_count, freq_devices):
    freq_ids = np.arange(freq_total)[:, None]
    turns = harmonic_step * (freq_ids + 1) * np.arange(lag_count)[None, :] % lag_count
    angles = turns * (2.0 * math.pi / lag_count)
    exact = np.stack((np.cos(angles), -np.sin(angles)), axis=1)
    parts = []
    for unused in range(pieces):
        part = exact.astype(ml_dtypes.bfloat16)
        parts.append(part)
        exact = exact - part.astype(np.float64)
    table = np.stack(parts).reshape(pieces, freq_devices, 2, 2, lag_count)
    both = np.stack((table, table[:, :, ::-1]), axis=2)
    both = both.transpose(1, 2, 0, 3, 4, 5).reshape(freq_devices * 2, pieces * 4, lag_count)
    return np.repeat(both, group, axis=1)


def kernel(
    freq_devices,
    owner,
    pairs,
    psd_hbm,
    table,
    green,
    observed,
    gradient_out,
    misfit_out,
    gbuf,
    wbuf,
    psd,
    psd_other,
    owner_row,
    pair_rows,
    ids_row,
    ids,
    obs,
    phi,
    spread,
    ohat,
    ohat_send,
    energy,
    send1,
    recv1,
    send_a,
    recv_a,
    send_b,
    recv_b,
    keep,
    own_sum,
    abuf,
    total,
    mis_own,
    mis_other,
    mis_pair,
    mis_freq,
    gsum,
    gsend,
    grecv,
    local_sem,
    core_send,
    core_recv,
    green_send,
    green_recv,
    one_send,
    one_recv,
    a_send,
    a_recv,
    b_send,
    b_recv,
    g1_send,
    g1_recv,
    g1f_send,
    g1f_recv,
    g2_send,
    g2_recv,
    g2f_send,
    g2f_recv,
    z_send,
    z_recv,
):
    z = lax.axis_index("freq")
    g = lax.axis_index("grid")
    c = g % 2
    x = (g // 2) % side
    y = g // (2 * side)
    other = g + 1 - 2 * c
    points = psd_hbm.shape[1]
    pair_dev, block, unused_cols, lags = observed.shape
    freq_total = 2 * freq_devices
    slot_count = 2 * side * side * pair_dev
    root_scale = 1.0 / math.sqrt(points * 2 * side * side)

    def neighbour(axis, d):
        step = 1 + 2 * d
        nx = (x + (1 - axis) * step) % side
        ny = (y + axis * step) % side
        return (ny * side + nx) * 2 + c

    def slot_of(t, h, o, r):
        sx = (x + (1 - h) * o + h * r) % side
        sy = (y + h * o + (1 - h) * r) % side
        return (sy * side + sx) * 4 + h * 2 + t

    def lane(d, j):
        return (1 - d) * (2 - 2 * j) + d * (1 + 2 * j)

    def lane_place(r):
        return ((r + 1) // 2 + 1) % 2

    def remote(src, dst, send, recv, device):
        return pltpu.make_async_remote_copy(
            src_ref=src, dst_ref=dst, send_sem=send, recv_sem=recv,
            device_id={"grid": device}, device_id_type=MESH,
        )

    barrier = pltpu.get_barrier_semaphore()
    friends = [{"grid": other}]
    for axis in range(2):
        for d in range(2):
            friends.append({"grid": neighbour(axis, d)})
    for dz in range(1, freq_devices):
        friends.append({"freq": (z + dz) % freq_devices})
    for friend in friends:
        pl.semaphore_signal(barrier, inc=1, device_id=friend, device_id_type=MESH)

    own_points = pl.ds(0, points)
    other_points = pl.ds(points, points)
    load_owner = pltpu.make_async_copy(owner, owner_row, local_sem.at[4])
    load_pairs = pltpu.make_async_copy(pairs, pair_rows, local_sem.at[5])
    load_psd = pltpu.make_async_copy(psd_hbm, psd, local_sem.at[6])
    load_green = [
        pltpu.make_async_copy(green.at[k, c], gbuf.at[k, :, :, own_points], local_sem.at[k])
        for k in range(2)
    ]
    load_table = pltpu.make_async_copy(table.at[z * 2 + c], phi, local_sem.at[2])
    load_obs = pltpu.make_async_copy(observed, obs, local_sem.at[3])
    load_owner.start()
    load_pairs.start()
    load_psd.start()
    for copy in load_green:
        copy.start()
    load_table.start()
    pl.semaphore_wait(barrier, len(friends))

    swap_psd = remote(psd_hbm, psd_other, core_send.at[2], core_recv.at[2], other)
    half = gbuf.shape[1] // 2

    def swap_green(n):
        k, some = n // 2, pl.ds(n % 2 * half, half)
        return remote(
            green.at[k, 1 - c, some], gbuf.at[k, some, :, other_points],
            green_send.at[n], green_recv.at[n], other,
        )

    swap_psd.start()
    for n in range(4):
        swap_green(n).start()
    load_obs.start()

    def weigh(k, first, count, where, row):
        def body(b, carry):
            for i in range(4):
                place = first + 4 * b + i
                wbuf[k, place, :, where] = (gbuf[k, place, :, where].astype(f32) * row).astype(bf16)
            return carry

        lax.fori_loop(0, count // 4, body, 0)

    load_owner.wait()
    load_pairs.wait()
    square = (slot_count, slot_count)
    across = lax.broadcasted_iota(jnp.int32, square, 1)
    along = lax.broadcasted_iota(jnp.int32, square, 0)

    def down(row):
        return jnp.sum(jnp.where(across == along, jnp.broadcast_to(row, square), 0), axis=1, keepdims=True)

    their_owner = jnp.broadcast_to(owner_row[...], square)
    my_owner = down(owner_row[...])
    earlier = (their_owner < my_owner) | ((their_owner == my_owner) & (across < along))
    ids_row[...] = jnp.zeros_like(ids_row)
    entry_slot = jnp.sum(jnp.where(earlier, 1, 0), axis=1, keepdims=True)
    hit = entry_slot == across
    for k in range(2):
        chosen = jnp.where(hit, down(pair_rows[pl.ds(k, 1), :]), 0)
        ids_row[pl.ds(k, 1), pl.ds(0, slot_count)] = jnp.sum(chosen, axis=0, keepdims=True)
    move_ids = pltpu.make_async_copy(ids_row, ids, local_sem.at[7])
    move_ids.start()

    load_psd.wait()
    own_row = psd[pl.ds(c, 1), :]
    for k in range(2):
        load_green[k].wait()
        weigh(k, 0, 2 * half, own_points, own_row)

    load_table.wait()
    rows = phi.shape[0]
    row_in_group = lax.broadcasted_iota(jnp.int32, (rows, lags), 0) % group
    phi_values = phi[...].astype(f32)
    for i in range(group):
        spread[:, pl.ds(i * lags, lags)] = jnp.where(row_in_group == i, phi_values, 0.0).astype(bf16)

    recv1[48] = jnp.zeros_like(recv1[48])
    gsum[...] = jnp.zeros_like(gsum)
    mis_own[...] = jnp.zeros_like(mis_own)
    move_ids.wait()
    swap_psd.wait_recv()
    other_row = psd_other[pl.ds(c, 1), :]
    for n in range(4):
        swap_green(n).wait_recv()
        weigh(n // 2, n % 2 * half, half, other_points, other_row)

    def units(slots):
        pairs_of = []
        for slot in slots:
            left = wbuf[:, ids[0, slot]].reshape(2 * block, 2 * points)
            right = gbuf[:, ids[1, slot]].reshape(2 * block, 2 * points)
            acc = lax.dot_general(left, right, (((1,), (1,)), ((), ())), preferred_element_type=f32)
            real = acc[:block, :block] + acc[block:, block:]
            imag = acc[block:, :block] - acc[:block, block:]
            pairs_of.append((real, imag))
        return pairs_of

    def copy1(n):
        u = n % 8
        return remote(
            send1.at[n], recv1.at[n], one_send.at[n], one_recv.at[n], neighbour(u % 2, (u // 2) % 2)
        )

    def first_ring(i, carry):
        part, t, j = i // 4, (i % 4) // 2, i % 2
        through = part == 1
        role = jnp.where(through, 2, part // 2)
        first = t * 24 + role * 8 + j * 4

        @pl.when(through)
        def _():
            project(i - 4)
            for u in range(4):
                copy1(first - 16 + u).wait_recv()

        slots = []
        for u in range(4):
            h, d = u % 2, u // 2
            o = jnp.where(part == 0, 2, 1 + 2 * d)
            r = jnp.where(part == 2, lane(1 - d, j), lane(d, j))
            slots.append(slot_of(t, h, o, r))
        for u, values in enumerate(units(slots)):
            n = first + u
            with_n = jnp.where(through, n - 16, 48)
            for k in range(2):
                send1[n, k] = (values[k] + recv1[with_n, k].astype(f32)).astype(bf16)
        for u in range(4):
            copy1(first + u).start()
        return carry

    def arrival1(t, h, d, r):
        role = 2 - (r + d) % 2
        return t * 24 + role * 8 + lane_place(r) * 4 + d * 2 + h

    def line_sums(t, wanted):
        for h, r in wanted:
            for d in range(2):
                copy1(arrival1(t, h, d, r)).wait_recv()
        sums = []
        for (h, r), values in zip(wanted, units([slot_of(t, h, 0, r) for h, r in wanted])):
            arrived = [recv1[arrival1(t, h, d, r)].astype(f32) for d in range(2)]
            sums.append([values[k] + (arrived[0][k] + arrived[1][k]) for k in range(2)])
        return sums

    def place(t, h, d):
        return (t * 2 + h) * 2 + d

    def copy_a(t, h, d):
        i = place(t, h, d)
        return remote(send_a.at[i], recv_a.at[i], a_send.at[i], a_recv.at[i], neighbour(1 - h, d))

    def copy_b(t, h, d, k):
        i = place(t, h, d)
        return remote(
            send_b.at[i, k], recv_b.at[i, k], b_send.at[i * 2 + k], b_recv.at[i * 2 + k],
            neighbour(1 - h, d),
        )

    def second_ring_open(t, carry):
        for h, values in enumerate(line_sums(t, [(0, 2), (1, 2)])):
            for d in range(2):
                send_a[place(t, h, d)] = values[d].astype(bf16)
                copy_a(t, h, d).start()
        wanted = [(h, 1 + 2 * d) for d in range(2) for h in range(2)]
        for (h, r), values in zip(wanted, line_sums(t, wanted)):
            d = r // 2
            i = place(t, h, d)
            send_b[i, 1 - d] = values[1 - d].astype(bf16)
            copy_b(t, h, d, 1 - d).start()
            keep[i] = values[d]
        return carry

    def own_part(t, carry):
        for h, values in enumerate(line_sums(t, [(0, 0), (1, 0)])):
            for k in range(2):
                own_sum[t * 2 + h, k] = values[k]
        return carry

    def second_ring_close(t, carry):
        for d in range(2):
            for h in range(2):
                i = place(t, h, d)
                copy_a(t, h, d).wait_recv()
                send_b[i, d] = (keep[i] + recv_a[i].astype(f32)).astype(bf16)
                copy_b(t, h, d, d).start()
        return carry

    def copy_g1(t, h, d):
        s, i = slot_of(t, h, 0, 0), place(t, h, d)
        return remote(abuf.at[s], abuf.at[s], g1_send.at[i], g1_recv.at[i], neighbour(1 - h, d))

    def copy_g1f(t, h, d):
        s, i = slot_of(t, h, 0, 3 - 2 * d), place(t, h, d)
        return remote(abuf.at[s, d], abuf.at[s, d], g1f_send.at[i], g1f_recv.at[i], neighbour(1 - h, d))

    def copy_g2(t, h, d, r):
        s, i = slot_of(t, h, 0, r), place(t, h, d) * 4 + r
        return remote(abuf.at[s], abuf.at[s], g2_send.at[i], g2_recv.at[i], neighbour(h, d))

    def copy_g2f(t, h, d, j):
        s, i = slot_of(t, h, 3 - 2 * d, lane(d, j)), place(t, h, d) * 2 + j
        return remote(abuf.at[s], abuf.at[s], g2f_send.at[i], g2f_recv.at[i], neighbour(h, d))

    ones = jnp.ones((8, block), f32)

    def lane_sum(values):
        return lax.dot_general(
            ones[:, : values.shape[1]], values, (((1,), (1,)), ((), ())),
            precision=lax.Precision.HIGHEST, preferred_element_type=f32,
        )

    def own_adjoint(t, carry):
        for h in range(2):
            for d in range(2):
                for k in range(2):
                    copy_b(t, h, d, k).wait_recv()
            s, q = slot_of(t, h, 0, 0), h * 2 + t
            kept = jnp.zeros((block, block), f32)
            for k in range(2):
                value = own_sum[t * 2 + h, k]
                for d in range(2):
                    value = value + recv_b[place(t, h, d), k].astype(f32)
                cross = value * f32(root_scale)
                seen = ohat[q, k]
                abuf[s, k] = (0.5 * cross - seen * f32(1.0 / lags)).astype(bf16)
                kept = kept + cross * (f32(lags / 2) * cross - 2.0 * seen)
            for d in range(2):
                copy_g1(t, h, d).start()
            for d in range(2):
                copy_g2(t, h, d, 0).start()
            total[q] = kept
        return carry

    def gather_1(t):
        def body(v, carry):
            h, d = v % 2, v // 2
            copy_g1(t, h, d).wait_recv()
            copy_g1f(t, h, d).start()
            for side_d in range(2):
                copy_g2(t, h, side_d, 3 - 2 * d).start()
            return carry

        lax.fori_loop(0, 4, body, 0)

    def gather_2(t):
        def body(h, carry):
            for d in range(2):
                copy_g1f(t, h, d).wait_recv()
            for d in range(2):
                copy_g2(t, h, d, 2).start()
            return carry

        lax.fori_loop(0, 2, body, 0)

    def gather_lane(t, r):
        e = r % 2
        j = lane_place(r)

        def body(h, carry):
            copy_g2(t, h, e, r).wait_recv()
            copy_g2f(t, h, e, j).start()
            copy_g2(t, h, 1 - e, r).wait_recv()
            return carry

        lax.fori_loop(0, 2, body, 0)

    def gather_end(t, r):
        def body(h, carry):
            copy_g2f(t, h, r % 2, lane_place(r)).wait_recv()
            return carry

        lax.fori_loop(0, 2, body, 0)

    def back(slots, carry):
        for s in slots:
            weights = abuf[s]
            top = jnp.concatenate((weights[0], -weights[1]), axis=1)
            low = jnp.concatenate((weights[1], weights[0]), axis=1)
            right = gbuf[:, ids[1, s]].reshape(2 * block, 2 * points)
            moved = jnp.dot(
                jnp.concatenate((top, low), axis=0), right, preferred_element_type=f32
            )
            left = gbuf[:, ids[0, s]].reshape(2 * block, 2 * points).astype(f32)
            carry = carry + jnp.sum((moved * left).reshape(2 * block // 8, 8, 2 * points), axis=0)
        return carry

    def project(quarter):
        @pl.when(quarter == 0)
        def _():
            load_obs.wait()

        chunks = block // group // 4

        def body(i, carry):
            first = pl.multiple_of((quarter * chunks + i) * group, group)
            seen = jnp.concatenate(
                [
                    jnp.concatenate([obs[s, first + k] for k in range(group)], axis=1)
                    for s in range(pair_dev)
                ],
                axis=0,
            )
            out = lax.dot_general(
                spread[...], seen, (((1,), (1,)), ((), ())), preferred_element_type=f32
            )
            out = jnp.sum(out.reshape(pieces, 4 * group, pair_dev * block), axis=0)
            for s in range(pair_dev):
                for k in range(2):
                    cols = slice(s * block, (s + 1) * block)
                    ohat[2 * c + s, k, pl.ds(first, group), :] = out[k * group : (k + 1) * group, cols]
                    ohat_send[s, k, pl.ds(first, group), :] = out[(2 + k) * group : (3 + k) * group, cols]
            return carry

        lax.fori_loop(0, chunks, body, 0, unroll=2)

    swap_ohat = remote(
        ohat_send, ohat.at[pl.ds(2 * c, 2)], core_send.at[3], core_recv.at[3], other
    )
    part_rows = block // freq_devices

    def energies():
        def body(i, carry):
            for s in range(pair_dev):
                seen = obs[s, z * part_rows + i].astype(f32)
                energy[pl.ds(s * part_rows + i, 1), :] = jnp.sum(seen * seen, axis=0, keepdims=True)
            return carry

        lax.fori_loop(0, part_rows, body, 0)

    swap_mis = remote(mis_own, mis_other, core_send.at[4], core_recv.at[4], other)

    def copy_z(dz):
        return pltpu.make_async_remote_copy(
            src_ref=mis_pair, dst_ref=mis_freq.at[dz - 1],
            send_sem=z_send.at[dz - 1], recv_sem=z_recv.at[dz - 1],
            device_id={"freq": (z + dz) % freq_devices}, device_id_type=MESH,
        )

    def misfit_parts():
        for q in range(2 * stages):
            mis_own[pl.ds(q, 1), :] = lane_sum(total[q])[:1]
        swap_mis.start()

    def misfit_sums():
        swap_mis.wait_recv()
        mis_pair[...] = mis_own[...] + mis_other[...]
        for dz in range(1, freq_devices):
            copy_z(dz).start()

    def misfit_end():
        mine = mis_pair[...]
        for dz in range(1, freq_devices):
            copy_z(dz).wait_recv()
            mine = mine + mis_freq[dz - 1]
        from_observed = lane_sum(energy[...])[:1]
        picked = jnp.zeros((mine.shape[0], part_rows), f32)
        for part in range(freq_devices):
            picked = jnp.where(z == part, mine[:, part * part_rows : (part + 1) * part_rows], picked)
        for s in range(pair_dev):
            row = jnp.where(c == 0, picked[s : s + 1], picked[2 + s : 3 + s])
            row = row + from_observed[:, s * part_rows : (s + 1) * part_rows]
            misfit_out[pl.ds(s, 1), :] = row * f32(1.0 / (2.0 * block * lags * freq_total))

    def leave1(n, carry):
        copy1(n).wait_send()
        return carry

    def leave2(v, carry):
        t, h, d = v // 4, (v // 2) % 2, v % 2
        copy_a(t, h, d).wait_send()
        for k in range(2):
            copy_b(t, h, d, k).wait_send()
        copy_g1(t, h, d).wait_send()
        return carry

    def leave3(v, carry):
        t, h, d = v // 4, (v // 2) % 2, v % 2
        copy_g1f(t, h, d).wait_send()
        for r in range(4):
            copy_g2(t, h, d, r).wait_send()
        for j in range(2):
            copy_g2f(t, h, d, j).wait_send()
        return carry

    lax.fori_loop(0, 12, first_ring, 0)
    swap_ohat.start()
    energies()
    lax.fori_loop(0, 2, second_ring_open, 0)
    lax.fori_loop(0, 2, own_part, 0)
    lax.fori_loop(0, 2, second_ring_close, 0)
    swap_ohat.wait_recv()
    lax.fori_loop(0, 2, own_adjoint, 0)

    steps = [
        ([], (0, 1), (0, 0), (0, 0)),
        ([(gather_1, 0)], (0, 0), (0, 0), (1, 2)),
        ([(gather_lane, 0, 0)], (0, 0), (1, 2), (0, 0)),
        ([(gather_1, 1)], (1, 0), (0, 0), (1, 2)),
        ([(gather_lane, 1, 0)], (1, 0), (1, 2), (0, 0)),
        ([(gather_2, 0), (gather_lane, 0, 1)], (0, 0), (1, 2), (1, 0)),
        ([(gather_lane, 0, 3)], (0, 0), (1, 2), (3, 0)),
        ([(gather_2, 1), (misfit_parts,)], (0, 1), (0, 0), (2, 0)),
        ([(gather_end, 0, 0), (gather_end, 1, 0)], (0, 1), (2, 0), (0, 0)),
        ([(gather_lane, 1, 1), (misfit_sums,)], (1, 0), (1, 2), (1, 0)),
        ([(gather_lane, 1, 3)], (1, 0), (1, 2), (3, 0)),
        ([(gather_lane, 0, 2)], (0, 0), (1, 2), (2, 0)),
        ([(gather_lane, 1, 2), (misfit_end,)], (1, 0), (1, 2), (2, 0)),
        ([(gather_end, 0, 1), (gather_end, 1, 1)], (0, 1), (2, 0), (1, 0)),
        ([(gather_end, 0, 3), (gather_end, 1, 3)], (0, 1), (2, 0), (3, 0)),
        ([(gather_end, 0, 2), (gather_end, 1, 2)], (0, 1), (2, 0), (2, 0)),
    ]

    def choose(i, values):
        chosen = values[0]
        for n in range(1, len(values)):
            chosen = jnp.where(i >= n, values[n], chosen) if values[n] != values[n - 1] else chosen
        return chosen

    def gather_step(i, carry):
        for n, step in enumerate(steps):
            if step[0]:
                @pl.when(i == n)
                def _(actions=tuple(step[0])):
                    for action in actions:
                        action[0](*action[1:])

        slots = []
        for u in range(4):
            t, o, r = (
                choose(i, [step[part][0] + u // 2 * step[part][1] for step in steps]) for part in (1, 2, 3)
            )
            slots.append(slot_of(t, u % 2, o, r))
        return back(slots, carry)

    gsum[...] = lax.fori_loop(0, len(steps), gather_step, gsum[...])

    lines = jnp.sum(gsum[...], axis=0, keepdims=True) * f32(1.0 / (block * math.sqrt(slot_count)))
    gsend[...] = jnp.broadcast_to(lines[:, points:], gsend.shape)
    swap_sum = remote(gsend, grecv, core_send.at[5], core_recv.at[5], other)
    swap_sum.start()
    swap_sum.wait_recv()
    row_ids = lax.broadcasted_iota(jnp.int32, (2, points), 0)
    gradient_out[...] = jnp.where(
        row_ids == c, jnp.broadcast_to(lines[:, :points], (2, points)), grecv[:2]
    )

    swap_psd.wait_send()
    for n in range(4):
        swap_green(n).wait_send()
    swap_ohat.wait_send()
    swap_mis.wait_send()
    swap_sum.wait_send()
    for dz in range(1, freq_devices):
        copy_z(dz).wait_send()
    lax.fori_loop(0, 48, leave1, 0)
    lax.fori_loop(0, 8, leave2, 0)
    lax.fori_loop(0, 8, leave3, 0)


def local(green_spectra, source_psd, pair_list, owner_map, observed):
    freq_devices = lax.axis_size("freq")
    planes, freq_dev, stations, points = green_spectra.shape
    pair_dev, block, unused_cols, lags = observed.shape
    slot_count = owner_map.shape[0]
    blocks = stations // block
    freq_total = freq_dev * freq_devices
    table = jnp.asarray(phase_table(freq_total, lags, freq_devices))
    rows = table.shape[1]
    units = stages * 2 * 2
    dma = pltpu.SemaphoreType.DMA
    vmem = pl.BlockSpec(memory_space=pltpu.VMEM)
    hbm = pl.BlockSpec(memory_space=pltpu.HBM)
    pair = (2, block, block)
    gradient, misfit = pl.pallas_call(
        functools.partial(kernel, freq_devices),
        out_shape=(
            jax.ShapeDtypeStruct((freq_dev, points), f32),
            jax.ShapeDtypeStruct((pair_dev, block // freq_devices), f32),
        ),
        in_specs=[hbm] * 6,
        out_specs=(vmem, vmem),
        scratch_shapes=[
            pltpu.VMEM((2, blocks, block, 2 * points), bf16),
            pltpu.VMEM((2, blocks, block, 2 * points), bf16),
            pltpu.VMEM((freq_dev, points), f32),
            pltpu.VMEM((freq_dev, points), f32),
            pltpu.VMEM((1, slot_count), jnp.int32),
            pltpu.VMEM((2, slot_count), jnp.int32),
            pltpu.VMEM((8, 128), jnp.int32),
            pltpu.SMEM((8, 128), jnp.int32),
            pltpu.VMEM((pair_dev, block, block, lags), bf16),
            pltpu.VMEM((rows, lags), bf16),
            pltpu.VMEM((rows, group * lags), bf16),
            pltpu.VMEM((2 * pair_dev,) + pair, f32),
            pltpu.VMEM((pair_dev,) + pair, f32),
            pltpu.VMEM((pair_dev * (block // freq_devices), lags), f32),
            pltpu.VMEM((24 * stages,) + pair, bf16),
            pltpu.VMEM((24 * stages + 1,) + pair, bf16),
            pltpu.VMEM((units, block, block), bf16),
            pltpu.VMEM((units, block, block), bf16),
            pltpu.VMEM((units,) + pair, bf16),
            pltpu.VMEM((units,) + pair, bf16),
            pltpu.VMEM((units, block, block), f32),
            pltpu.VMEM((2 * stages,) + pair, f32),
            pltpu.VMEM((slot_count,) + pair, bf16),
            pltpu.VMEM((2 * stages, block, block), f32),
            pltpu.VMEM((8, block), f32),
            pltpu.VMEM((8, block), f32),
            pltpu.VMEM((8, block), f32),
            pltpu.VMEM((freq_devices - 1, 8, block), f32),
            pltpu.VMEM((8, 2 * points), f32),
            pltpu.VMEM((8, points), f32),
            pltpu.VMEM((8, points), f32),
            dma((8,)),
            dma((6,)),
            dma((6,)),
            dma((4,)),
            dma((4,)),
            dma((24 * stages,)),
            dma((24 * stages,)),
            dma((units,)),
            dma((units,)),
            dma((2 * units,)),
            dma((2 * units,)),
            dma((units,)),
            dma((units,)),
            dma((units,)),
            dma((units,)),
            dma((4 * units,)),
            dma((4 * units,)),
            dma((2 * units,)),
            dma((2 * units,)),
            dma((freq_devices - 1,)),
            dma((freq_devices - 1,)),
        ],
        compiler_params=pltpu.CompilerParams(
            collective_id=0, has_side_effects=True, vmem_limit_bytes=60 * 1024 * 1024
        ),
        cost_estimate=pl.CostEstimate(
            flops=8 * slot_count * freq_dev * 2 * block * block * points,
            bytes_accessed=12 * 1024 * 1024,
            transcendentals=0,
        ),
        name="misfit_gradient",
    )(
        owner_map.reshape(1, slot_count),
        pair_list.T,
        source_psd,
        table,
        green_spectra.reshape(planes, freq_dev, blocks, block, points),
        observed,
    )
    return (gradient, misfit)


def solution(mesh):
    in_specs = (
        P(None, "freq", None, "grid"),
        P("freq", "grid"),
        P(),
        P(),
        P("grid", None, None, None),
    )
    out_specs = (P("freq", "grid"), P("grid", "freq"))
    return jax.shard_map(local, mesh=mesh, in_specs=in_specs, out_specs=out_specs, check_vma=False)
```

```python
import functools
import math

import jax
import jax.numpy as jnp
import ml_dtypes
import numpy as np
from jax import lax
from jax.experimental import pallas as pl
from jax.experimental.pallas import tpu as pltpu
from jax.sharding import PartitionSpec as P

harmonic_step = 3
side = 4
stages = 2
pieces = 3
group = 8
MESH = pl.DeviceIdType.MESH
f32 = jnp.float32
bf16 = jnp.bfloat16


def phase_table(freq_total, lag_count, freq_devices):
    freq_ids = np.arange(freq_total)[:, None]
    turns = harmonic_step * (freq_ids + 1) * np.arange(lag_count)[None, :] % lag_count
    angles = turns * (2.0 * math.pi / lag_count)
    exact = np.stack((np.cos(angles), -np.sin(angles)), axis=1)
    parts = []
    for unused in range(pieces):
        part = exact.astype(ml_dtypes.bfloat16)
        parts.append(part)
        exact = exact - part.astype(np.float64)
    table = np.stack(parts).reshape(pieces, freq_devices, 2, 2, lag_count)
    both = np.stack((table, table[:, :, ::-1]), axis=2)
    both = both.transpose(1, 2, 0, 3, 4, 5).reshape(freq_devices * 2, pieces * 4, lag_count)
    return np.repeat(both, group, axis=1)


def kernel(
    freq_devices,
    owner,
    pairs,
    psd_hbm,
    table,
    green,
    observed,
    gradient_out,
    misfit_out,
    gbuf,
    wbuf,
    psd,
    psd_other,
    owner_row,
    pair_rows,
    ids_row,
    ids,
    obs,
    phi,
    spread,
    ohat,
    ohat_send,
    energy,
    send1,
    recv1,
    send_a,
    recv_a,
    send_b,
    recv_b,
    keep,
    own_sum,
    abuf,
    total,
    mis_own,
    mis_other,
    mis_pair,
    mis_freq,
    gsum,
    gsend,
    grecv,
    local_sem,
    core_send,
    core_recv,
    green_send,
    green_recv,
    one_send,
    one_recv,
    a_send,
    a_recv,
    b_send,
    b_recv,
    g_send,
    g1_recv,
    g1f_recv,
    g2_recv,
    g2f_recv,
    z_send,
    z_recv,
    z_here,
):
    z = lax.axis_index("freq")
    g = lax.axis_index("grid")
    c = g % 2
    x = (g // 2) % side
    y = g // (2 * side)
    other = g + 1 - 2 * c
    points = psd_hbm.shape[1]
    pair_dev, block, unused_cols, lags = observed.shape
    freq_total = 2 * freq_devices
    slot_count = 2 * side * side * pair_dev
    root_scale = 1.0 / math.sqrt(points * 2 * side * side)

    def neighbour(axis, d):
        step = 1 + 2 * d
        nx = (x + (1 - axis) * step) % side
        ny = (y + axis * step) % side
        return (ny * side + nx) * 2 + c

    def slot_of(t, h, o, r):
        sx = (x + (1 - h) * o + h * r) % side
        sy = (y + h * o + (1 - h) * r) % side
        return (sy * side + sx) * 4 + h * 2 + t

    def lane(d, j):
        return (1 - d) * (2 - 2 * j) + d * (1 + 2 * j)

    def lane_place(r):
        return ((r + 1) // 2 + 1) % 2

    def remote(src, dst, send, recv, device):
        return pltpu.make_async_remote_copy(
            src_ref=src, dst_ref=dst, send_sem=send, recv_sem=recv,
            device_id={"grid": device}, device_id_type=MESH,
        )

    barrier = pltpu.get_barrier_semaphore()
    friends = [{"grid": other}]
    for axis in range(2):
        for d in range(2):
            friends.append({"grid": neighbour(axis, d)})
    for friend in friends:
        pl.semaphore_signal(barrier, inc=1, device_id=friend, device_id_type=MESH)
    for dz in range(1, freq_devices):

        @pl.when(z + dz < freq_devices)
        def _():
            pl.semaphore_signal(barrier, inc=1, device_id={"freq": z + dz}, device_id_type=MESH)


    own_points = pl.ds(0, points)
    other_points = pl.ds(points, points)
    load_owner = pltpu.make_async_copy(owner, owner_row, local_sem.at[4])
    load_pairs = pltpu.make_async_copy(pairs, pair_rows, local_sem.at[5])
    load_psd = pltpu.make_async_copy(psd_hbm, psd, local_sem.at[6])
    load_green = [
        pltpu.make_async_copy(green.at[k, c], gbuf.at[k, :, :, own_points], local_sem.at[k])
        for k in range(2)
    ]
    load_table = pltpu.make_async_copy(table.at[z * 2 + c], phi, local_sem.at[2])
    load_obs = pltpu.make_async_copy(observed, obs, local_sem.at[3])
    load_owner.start()
    load_pairs.start()
    load_psd.start()
    for copy in load_green:
        copy.start()
    load_table.start()
    pl.semaphore_wait(barrier, len(friends) + z)
    for dz in range(1, freq_devices):

        @pl.when(z >= dz)
        def _():
            pl.semaphore_signal(z_here, inc=1, device_id={"freq": z - dz}, device_id_type=MESH)


    swap_psd = remote(psd_hbm, psd_other, core_send.at[2], core_recv.at[2], other)
    half = gbuf.shape[1] // 2

    def swap_green(n):
        k, some = n // 2, pl.ds(n % 2 * half, half)
        return remote(
            green.at[k, 1 - c, some], gbuf.at[k, some, :, other_points],
            green_send.at[0], green_recv.at[n], other,
        )

    swap_psd.start()
    for n in range(4):
        swap_green(n).start()
    load_obs.start()

    def weigh(k, first, count, where, row):
        def body(b, carry):
            for i in range(4):
                place = first + 4 * b + i
                wbuf[k, place, :, where] = (gbuf[k, place, :, where].astype(f32) * row).astype(bf16)
            return carry

        lax.fori_loop(0, count // 4, body, 0)

    load_owner.wait()
    load_pairs.wait()
    square = (slot_count, slot_count)
    across = lax.broadcasted_iota(jnp.int32, square, 1)
    along = lax.broadcasted_iota(jnp.int32, square, 0)

    def down(row):
        return jnp.sum(jnp.where(across == along, jnp.broadcast_to(row, square), 0), axis=1, keepdims=True)

    their_owner = jnp.broadcast_to(owner_row[...], square)
    my_owner = down(owner_row[...])
    earlier = (their_owner < my_owner) | ((their_owner == my_owner) & (across < along))
    ids_row[...] = jnp.zeros_like(ids_row)
    entry_slot = jnp.sum(jnp.where(earlier, 1, 0), axis=1, keepdims=True)
    hit = entry_slot == across
    for k in range(2):
        chosen = jnp.where(hit, down(pair_rows[pl.ds(k, 1), :]), 0)
        ids_row[pl.ds(k, 1), pl.ds(0, slot_count)] = jnp.sum(chosen, axis=0, keepdims=True)
    move_ids = pltpu.make_async_copy(ids_row, ids, local_sem.at[7])
    move_ids.start()

    load_psd.wait()
    own_row = psd[pl.ds(c, 1), :]
    for k in range(2):
        load_green[k].wait()
        weigh(k, 0, 2 * half, own_points, own_row)

    load_table.wait()
    rows = phi.shape[0]
    row_in_group = lax.broadcasted_iota(jnp.int32, (rows, lags), 0) % group
    phi_values = phi[...].astype(f32)
    for i in range(group):
        spread[:, pl.ds(i * lags, lags)] = jnp.where(row_in_group == i, phi_values, 0.0).astype(bf16)

    recv1[48] = jnp.zeros_like(recv1[48])
    gsum[...] = jnp.zeros_like(gsum)
    mis_own[...] = jnp.zeros_like(mis_own)
    move_ids.wait()
    swap_psd.wait_recv()
    other_row = psd_other[pl.ds(c, 1), :]
    for n in range(4):
        swap_green(n).wait_recv()
        weigh(n // 2, n % 2 * half, half, other_points, other_row)

    def units(slots):
        pairs_of = []
        for slot in slots:
            left = wbuf[:, ids[0, slot]].reshape(2 * block, 2 * points)
            right = gbuf[:, ids[1, slot]].reshape(2 * block, 2 * points)
            acc = lax.dot_general(left, right, (((1,), (1,)), ((), ())), preferred_element_type=f32)
            real = acc[:block, :block] + acc[block:, block:]
            imag = acc[block:, :block] - acc[:block, block:]
            pairs_of.append((real, imag))
        return pairs_of

    def copy1(n):
        t, role, u = n // 24, (n % 24) // 8, n % 8
        h, d, j = u % 2, (u // 2) % 2, u // 4
        r = jnp.where(role == 1, lane(1 - d, j), lane(d, j))
        i = jnp.where(role == 0, t * 2 + j, 4 + t * 4 + r)
        return remote(send1.at[n], recv1.at[n], one_send.at[0], one_recv.at[i], neighbour(h, d))

    def wait_all(buffer, count, semaphore):
        some = buffer.at[pl.ds(0, count)]
        pltpu.make_async_copy(some, some, semaphore).wait()

    def wait1(i):
        wait_all(recv1, 4, one_recv.at[i])

    def first_ring(i, carry):
        part, t, j = i // 4, (i % 4) // 2, i % 2
        through = part == 1
        role = jnp.where(through, 2, part // 2)
        first = t * 24 + role * 8 + j * 4

        @pl.when(through)
        def _():
            project(i - 4)
            wait1(t * 2 + j)

        slots = []
        for u in range(4):
            h, d = u % 2, u // 2
            o = jnp.where(part == 0, 2, 1 + 2 * d)
            r = jnp.where(part == 2, lane(1 - d, j), lane(d, j))
            slots.append(slot_of(t, h, o, r))
        for u, values in enumerate(units(slots)):
            n = first + u
            with_n = jnp.where(through, n - 16, 48)
            for k in range(2):
                send1[n, k] = (values[k] + recv1[with_n, k].astype(f32)).astype(bf16)
        for u in range(4):
            copy1(first + u).start()
        return carry

    def arrival1(t, h, d, r):
        role = 2 - (r + d) % 2
        return t * 24 + role * 8 + lane_place(r) * 4 + d * 2 + h

    def line_sums(t, wanted):
        for r in sorted({r for h, r in wanted}):
            wait1(4 + t * 4 + r)
        sums = []
        for (h, r), values in zip(wanted, units([slot_of(t, h, 0, r) for h, r in wanted])):
            arrived = [recv1[arrival1(t, h, d, r)].astype(f32) for d in range(2)]
            sums.append([values[k] + (arrived[0][k] + arrived[1][k]) for k in range(2)])
        return sums

    def place(t, h, d):
        return (t * 2 + h) * 2 + d

    def copy_a(t, h, d):
        i = place(t, h, d)
        return remote(send_a.at[i], recv_a.at[i], a_send.at[0], a_recv.at[t], neighbour(1 - h, d))

    def copy_b(t, h, d, k):
        i = place(t, h, d)
        return remote(
            send_b.at[i, k], recv_b.at[i, k], b_send.at[0], b_recv.at[t], neighbour(1 - h, d)
        )

    def second_ring_open(t, carry):
        for h, values in enumerate(line_sums(t, [(0, 2), (1, 2)])):
            for d in range(2):
                send_a[place(t, h, d)] = values[d].astype(bf16)
                copy_a(t, h, d).start()
        wanted = [(h, 1 + 2 * d) for d in range(2) for h in range(2)]
        for (h, r), values in zip(wanted, line_sums(t, wanted)):
            d = r // 2
            i = place(t, h, d)
            send_b[i, 1 - d] = values[1 - d].astype(bf16)
            copy_b(t, h, d, 1 - d).start()
            keep[i] = values[d]
        return carry

    def own_part(t, carry):
        for h, values in enumerate(line_sums(t, [(0, 0), (1, 0)])):
            for k in range(2):
                own_sum[t * 2 + h, k] = values[k]
        return carry

    def second_ring_close(t, carry):
        wait_all(recv_a, 4, a_recv.at[t])
        for d in range(2):
            for h in range(2):
                i = place(t, h, d)
                send_b[i, d] = (keep[i] + recv_a[i].astype(f32)).astype(bf16)
                copy_b(t, h, d, d).start()
        return carry

    def copy_g1(t, h, d):
        s = slot_of(t, h, 0, 0)
        return remote(abuf.at[s], abuf.at[s], g_send.at[0], g1_recv.at[t], neighbour(1 - h, d))

    def copy_g1f(t, h, d):
        s = slot_of(t, h, 0, 3 - 2 * d)
        return remote(abuf.at[s, d], abuf.at[s, d], g_send.at[0], g1f_recv.at[t], neighbour(1 - h, d))

    def copy_g2(t, h, d, r):
        s = slot_of(t, h, 0, r)
        return remote(abuf.at[s], abuf.at[s], g_send.at[0], g2_recv.at[t * 4 + r], neighbour(h, d))

    def copy_g2f(t, h, d, j):
        r = lane(d, j)
        s = slot_of(t, h, 3 - 2 * d, r)
        return remote(abuf.at[s], abuf.at[s], g_send.at[0], g2f_recv.at[r], neighbour(h, d))

    ones = jnp.ones((8, block), f32)

    def lane_sum(values):
        return lax.dot_general(
            ones[:, : values.shape[1]], values, (((1,), (1,)), ((), ())),
            precision=lax.Precision.HIGHEST, preferred_element_type=f32,
        )

    def own_adjoint(t, carry):
        wait_all(recv_b, 4, b_recv.at[t])
        for h in range(2):
            s, q = slot_of(t, h, 0, 0), h * 2 + t
            kept = jnp.zeros((block, block), f32)
            for k in range(2):
                value = own_sum[t * 2 + h, k]
                for d in range(2):
                    value = value + recv_b[place(t, h, d), k].astype(f32)
                cross = value * f32(root_scale)
                seen = ohat[q, k]
                abuf[s, k] = (0.5 * cross - seen * f32(1.0 / lags)).astype(bf16)
                kept = kept + cross * (f32(lags / 2) * cross - 2.0 * seen)
            for d in range(2):
                copy_g1(t, h, d).start()
            for d in range(2):
                copy_g2(t, h, d, 0).start()
            total[q] = kept
        return carry

    def gather_1(t):
        wait_all(abuf, 4, g1_recv.at[t])

        def body(v, carry):
            h, d = v % 2, v // 2
            copy_g1f(t, h, d).start()
            for side_d in range(2):
                copy_g2(t, h, side_d, 3 - 2 * d).start()
            return carry

        lax.fori_loop(0, 4, body, 0)

    def gather_2(t):
        wait_all(abuf, 2, g1f_recv.at[t])
        for h in range(2):
            for d in range(2):
                copy_g2(t, h, d, 2).start()

    def gather_lane(t, r):
        wait_all(abuf, 4, g2_recv.at[t * 4 + r])
        for h in range(2):
            copy_g2f(t, h, r % 2, lane_place(r)).start()

    def gather_end(r):
        wait_all(abuf, 4, g2f_recv.at[r])

    def back(slots, carry):
        for s in slots:
            weights = abuf[s]
            top = jnp.concatenate((weights[0], -weights[1]), axis=1)
            low = jnp.concatenate((weights[1], weights[0]), axis=1)
            right = gbuf[:, ids[1, s]].reshape(2 * block, 2 * points)
            moved = jnp.dot(
                jnp.concatenate((top, low), axis=0), right, preferred_element_type=f32
            )
            left = gbuf[:, ids[0, s]].reshape(2 * block, 2 * points).astype(f32)
            carry = carry + jnp.sum((moved * left).reshape(2 * block // 8, 8, 2 * points), axis=0)
        return carry

    def project(quarter):
        @pl.when(quarter == 0)
        def _():
            load_obs.wait()

        chunks = block // group // 4

        def body(i, carry):
            first = pl.multiple_of((quarter * chunks + i) * group, group)
            seen = jnp.concatenate(
                [
                    jnp.concatenate([obs[s, first + k] for k in range(group)], axis=1)
                    for s in range(pair_dev)
                ],
                axis=0,
            )
            out = lax.dot_general(
                spread[...], seen, (((1,), (1,)), ((), ())), preferred_element_type=f32
            )
            out = jnp.sum(out.reshape(pieces, 4 * group, pair_dev * block), axis=0)
            for s in range(pair_dev):
                for k in range(2):
                    cols = slice(s * block, (s + 1) * block)
                    ohat[2 * c + s, k, pl.ds(first, group), :] = out[k * group : (k + 1) * group, cols]
                    ohat_send[s, k, pl.ds(first, group), :] = out[(2 + k) * group : (3 + k) * group, cols]
            return carry

        lax.fori_loop(0, chunks, body, 0, unroll=2)

    swap_ohat = remote(
        ohat_send, ohat.at[pl.ds(2 * c, 2)], core_send.at[3], core_recv.at[3], other
    )
    part_rows = block // freq_devices

    def energies():
        def body(i, carry):
            for s in range(pair_dev):
                seen = obs[s, z * part_rows + i].astype(f32)
                energy[pl.ds(s * part_rows + i, 1), :] = jnp.sum(seen * seen, axis=0, keepdims=True)
            return carry

        lax.fori_loop(0, part_rows, body, 0)

    swap_mis = remote(mis_own, mis_other, core_send.at[4], core_recv.at[4], other)

    def copy_z(dz):
        return pltpu.make_async_remote_copy(
            src_ref=mis_pair, dst_ref=mis_freq.at[dz - 1],
            send_sem=z_send.at[0], recv_sem=z_recv.at[0],
            device_id={"freq": (z + dz) % freq_devices}, device_id_type=MESH,
        )

    def misfit_parts():
        for q in range(2 * stages):
            mis_own[pl.ds(q, 1), :] = lane_sum(total[q])[:1]
        swap_mis.start()

    def misfit_sums():
        swap_mis.wait_recv()
        mis_pair[...] = mis_own[...] + mis_other[...]

        @pl.when(z < freq_devices - 1)
        def _():
            pl.semaphore_wait(z_here, freq_devices - 1 - z)

        for dz in range(1, freq_devices):
            copy_z(dz).start()

    def misfit_end():
        wait_all(mis_freq, freq_devices - 1, z_recv.at[0])
        mine = mis_pair[...]
        for dz in range(1, freq_devices):
            mine = mine + mis_freq[dz - 1]
        from_observed = lane_sum(energy[...])[:1]
        picked = jnp.zeros((mine.shape[0], part_rows), f32)
        for part in range(freq_devices):
            picked = jnp.where(z == part, mine[:, part * part_rows : (part + 1) * part_rows], picked)
        for s in range(pair_dev):
            row = jnp.where(c == 0, picked[s : s + 1], picked[2 + s : 3 + s])
            row = row + from_observed[:, s * part_rows : (s + 1) * part_rows]
            misfit_out[pl.ds(s, 1), :] = row * f32(1.0 / (2.0 * block * lags * freq_total))

    lax.fori_loop(0, 12, first_ring, 0)
    swap_ohat.start()
    energies()
    lax.fori_loop(0, 2, second_ring_open, 0)
    lax.fori_loop(0, 2, own_part, 0)
    lax.fori_loop(0, 2, second_ring_close, 0)
    swap_ohat.wait_recv()
    lax.fori_loop(0, 2, own_adjoint, 0)

    steps = [
        ([], (0, 1), (0, 0), (0, 0)),
        ([(gather_1, 0)], (0, 0), (0, 0), (1, 2)),
        ([(gather_lane, 0, 0)], (0, 0), (1, 2), (0, 0)),
        ([(gather_1, 1)], (1, 0), (0, 0), (1, 2)),
        ([(gather_lane, 1, 0)], (1, 0), (1, 2), (0, 0)),
        ([(gather_2, 0), (gather_lane, 0, 1)], (0, 0), (1, 2), (1, 0)),
        ([(gather_lane, 0, 3)], (0, 0), (1, 2), (3, 0)),
        ([(gather_2, 1), (misfit_parts,)], (0, 1), (0, 0), (2, 0)),
        ([(gather_end, 0)], (0, 1), (2, 0), (0, 0)),
        ([(gather_lane, 1, 1), (misfit_sums,)], (1, 0), (1, 2), (1, 0)),
        ([(gather_lane, 1, 3)], (1, 0), (1, 2), (3, 0)),
        ([(gather_lane, 0, 2)], (0, 0), (1, 2), (2, 0)),
        ([(gather_lane, 1, 2), (misfit_end,)], (1, 0), (1, 2), (2, 0)),
        ([(gather_end, 1)], (0, 1), (2, 0), (1, 0)),
        ([(gather_end, 3)], (0, 1), (2, 0), (3, 0)),
        ([(gather_end, 2)], (0, 1), (2, 0), (2, 0)),
    ]

    def choose(i, values):
        chosen = values[0]
        for n in range(1, len(values)):
            chosen = jnp.where(i >= n, values[n], chosen) if values[n] != values[n - 1] else chosen
        return chosen

    def gather_step(i, carry):
        for n, step in enumerate(steps):
            if step[0]:
                @pl.when(i == n)
                def _(actions=tuple(step[0])):
                    for action in actions:
                        action[0](*action[1:])

        slots = []
        for u in range(4):
            t, o, r = (
                choose(i, [step[part][0] + u // 2 * step[part][1] for step in steps]) for part in (1, 2, 3)
            )
            slots.append(slot_of(t, u % 2, o, r))
        return back(slots, carry)

    gsum[...] = lax.fori_loop(0, len(steps), gather_step, gsum[...])

    lines = jnp.sum(gsum[...], axis=0, keepdims=True) * f32(1.0 / (block * math.sqrt(slot_count)))
    gsend[...] = jnp.broadcast_to(lines[:, points:], gsend.shape)
    swap_sum = remote(gsend, grecv, core_send.at[5], core_recv.at[5], other)
    swap_sum.start()
    swap_sum.wait_recv()
    row_ids = lax.broadcasted_iota(jnp.int32, (2, points), 0)
    gradient_out[...] = jnp.where(
        row_ids == c, jnp.broadcast_to(lines[:, :points], (2, points)), grecv[:2]
    )

    swap_psd.wait_send()
    wait_all(gbuf.at[:, :, :, other_points], 2, green_send.at[0])
    swap_ohat.wait_send()
    swap_mis.wait_send()
    swap_sum.wait_send()
    wait_all(mis_freq, freq_devices - 1, z_send.at[0])
    wait_all(send1, 24 * stages, one_send.at[0])
    wait_all(send_a, 4 * stages, a_send.at[0])
    wait_all(send_b, 4 * stages, b_send.at[0])
    wait_all(abuf, 30 * stages, g_send.at[0])


def hand_on(gradient, misfit, gradient_out, misfit_out):
    gradient_out[...] = gradient[...]
    misfit_out[...] = misfit[...]


def local(green_spectra, source_psd, pair_list, owner_map, observed):
    freq_devices = lax.axis_size("freq")
    planes, freq_dev, stations, points = green_spectra.shape
    pair_dev, block, unused_cols, lags = observed.shape
    slot_count = owner_map.shape[0]
    blocks = stations // block
    freq_total = freq_dev * freq_devices
    table = jnp.asarray(phase_table(freq_total, lags, freq_devices))
    rows = table.shape[1]
    units = stages * 2 * 2
    dma = pltpu.SemaphoreType.DMA
    vmem = pl.BlockSpec(memory_space=pltpu.VMEM)
    hbm = pl.BlockSpec(memory_space=pltpu.HBM)
    pair = (2, block, block)
    gradient, misfit = pl.pallas_call(
        functools.partial(kernel, freq_devices),
        out_shape=(
            jax.ShapeDtypeStruct((freq_dev, points), f32),
            jax.ShapeDtypeStruct((pair_dev, block // freq_devices), f32),
        ),
        in_specs=[hbm] * 6,
        out_specs=(vmem, vmem),
        scratch_shapes=[
            pltpu.VMEM((2, blocks, block, 2 * points), bf16),
            pltpu.VMEM((2, blocks, block, 2 * points), bf16),
            pltpu.VMEM((freq_dev, points), f32),
            pltpu.VMEM((freq_dev, points), f32),
            pltpu.VMEM((1, slot_count), jnp.int32),
            pltpu.VMEM((2, slot_count), jnp.int32),
            pltpu.VMEM((8, 128), jnp.int32),
            pltpu.SMEM((8, 128), jnp.int32),
            pltpu.VMEM((pair_dev, block, block, lags), bf16),
            pltpu.VMEM((rows, lags), bf16),
            pltpu.VMEM((rows, group * lags), bf16),
            pltpu.VMEM((2 * pair_dev,) + pair, f32),
            pltpu.VMEM((pair_dev,) + pair, f32),
            pltpu.VMEM((pair_dev * (block // freq_devices), lags), f32),
            pltpu.VMEM((24 * stages,) + pair, bf16),
            pltpu.VMEM((24 * stages + 1,) + pair, bf16),
            pltpu.VMEM((units, block, block), bf16),
            pltpu.VMEM((units, block, block), bf16),
            pltpu.VMEM((units,) + pair, bf16),
            pltpu.VMEM((units,) + pair, bf16),
            pltpu.VMEM((units, block, block), f32),
            pltpu.VMEM((2 * stages,) + pair, f32),
            pltpu.VMEM((slot_count,) + pair, bf16),
            pltpu.VMEM((2 * stages, block, block), f32),
            pltpu.VMEM((8, block), f32),
            pltpu.VMEM((8, block), f32),
            pltpu.VMEM((8, block), f32),
            pltpu.VMEM((freq_devices - 1, 8, block), f32),
            pltpu.VMEM((8, 2 * points), f32),
            pltpu.VMEM((8, points), f32),
            pltpu.VMEM((8, points), f32),
            dma((8,)),
            dma((6,)),
            dma((6,)),
            dma((1,)),
            dma((4,)),
            dma((1,)),
            dma((6 * stages,)),
            dma((1,)),
            dma((stages,)),
            dma((1,)),
            dma((stages,)),
            dma((1,)),
            dma((stages,)),
            dma((stages,)),
            dma((4 * stages,)),
            dma((4,)),
            dma((1,)),
            dma((1,)),
            pltpu.SemaphoreType.REGULAR,
        ],
        compiler_params=pltpu.CompilerParams(
            collective_id=0, has_side_effects=True, vmem_limit_bytes=60 * 1024 * 1024
        ),
        cost_estimate=pl.CostEstimate(
            flops=8 * slot_count * freq_dev * 2 * block * block * points,
            bytes_accessed=12 * 1024 * 1024,
            transcendentals=0,
        ),
        name="misfit_gradient",
    )(
        owner_map.reshape(1, slot_count),
        pair_list.T,
        source_psd,
        table,
        green_spectra.reshape(planes, freq_dev, blocks, block, points),
        observed,
    )
    return pl.pallas_call(
        hand_on,
        out_shape=(
            jax.ShapeDtypeStruct(gradient.shape, f32),
            jax.ShapeDtypeStruct(misfit.shape, f32),
        ),
        in_specs=[vmem, vmem],
        out_specs=(vmem, vmem),
        name="hand_on",
    )(gradient, misfit)


def solution(mesh):
    in_specs = (
        P(None, "freq", None, "grid"),
        P("freq", "grid"),
        P(),
        P(),
        P("grid", None, None, None),
    )
    out_specs = (P("freq", "grid"), P("grid", "freq"))
    return jax.shard_map(local, mesh=mesh, in_specs=in_specs, out_specs=out_specs, check_vma=False)
```

```python
import functools
import math

import jax
import jax.numpy as jnp
import ml_dtypes
import numpy as np
from jax import lax
from jax.experimental import pallas as pl
from jax.experimental.pallas import tpu as pltpu
from jax.sharding import PartitionSpec as P

harmonic_step = 3
side = 4
stages = 2
pieces = 3
group = 8
MESH = pl.DeviceIdType.MESH
f32 = jnp.float32
bf16 = jnp.bfloat16


def phase_table(freq_total, lag_count, freq_devices):
    freq_ids = np.arange(freq_total)[:, None]
    turns = harmonic_step * (freq_ids + 1) * np.arange(lag_count)[None, :] % lag_count
    angles = turns * (2.0 * math.pi / lag_count)
    exact = np.stack((np.cos(angles), -np.sin(angles)), axis=1)
    parts = []
    for unused in range(pieces):
        part = exact.astype(ml_dtypes.bfloat16)
        parts.append(part)
        exact = exact - part.astype(np.float64)
    table = np.stack(parts).reshape(pieces, freq_devices, 2, 2, lag_count)
    both = np.stack((table, table[:, :, ::-1]), axis=2)
    both = both.transpose(1, 2, 0, 3, 4, 5).reshape(freq_devices * 2, pieces * 4, lag_count)
    return np.repeat(both, group, axis=1)


def kernel(
    freq_devices,
    owner,
    pairs,
    psd_hbm,
    table,
    green,
    observed,
    gradient_out,
    misfit_out,
    gbuf,
    wbuf,
    psd,
    psd_other,
    owner_row,
    pair_rows,
    ids_row,
    ids,
    obs,
    phi,
    spread,
    ohat,
    ohat_send,
    energy,
    send1,
    recv1,
    send_a,
    recv_a,
    send_b,
    recv_b,
    keep,
    own_sum,
    abuf,
    total,
    mis_own,
    mis_other,
    mis_pair,
    mis_freq,
    gsum,
    gsend,
    grecv,
    local_sem,
    core_send,
    core_recv,
    green_send,
    green_recv,
    one_send,
    one_recv,
    a_send,
    a_recv,
    b_send,
    b_recv,
    g_send,
    g1_recv,
    g1f_recv,
    g2_recv,
    g2f_recv,
    z_send,
    z_recv,
    z_here,
):
    z = lax.axis_index("freq")
    g = lax.axis_index("grid")
    c = g % 2
    x = (g // 2) % side
    y = g // (2 * side)
    other = g + 1 - 2 * c
    points = psd_hbm.shape[1]
    pair_dev, block, unused_cols, lags = observed.shape
    freq_total = 2 * freq_devices
    slot_count = 2 * side * side * pair_dev
    root_scale = 1.0 / math.sqrt(points * 2 * side * side)

    def neighbour(axis, d):
        step = 1 + 2 * d
        nx = (x + (1 - axis) * step) % side
        ny = (y + axis * step) % side
        return (ny * side + nx) * 2 + c

    def slot_of(t, h, o, r):
        sx = (x + (1 - h) * o + h * r) % side
        sy = (y + h * o + (1 - h) * r) % side
        return (sy * side + sx) * 4 + h * 2 + t

    def lane(d, j):
        return (1 - d) * (2 - 2 * j) + d * (1 + 2 * j)

    def lane_place(r):
        return ((r + 1) // 2 + 1) % 2

    def remote(src, dst, send, recv, device):
        return pltpu.make_async_remote_copy(
            src_ref=src, dst_ref=dst, send_sem=send, recv_sem=recv,
            device_id={"grid": device}, device_id_type=MESH,
        )

    barrier = pltpu.get_barrier_semaphore()
    friends = [{"grid": other}]
    for axis in range(2):
        for d in range(2):
            friends.append({"grid": neighbour(axis, d)})
    for friend in friends:
        pl.semaphore_signal(barrier, inc=1, device_id=friend, device_id_type=MESH)
    for dz in range(1, freq_devices):

        @pl.when(z + dz < freq_devices)
        def _():
            pl.semaphore_signal(barrier, inc=1, device_id={"freq": z + dz}, device_id_type=MESH)


    own_points = pl.ds(0, points)
    other_points = pl.ds(points, points)
    load_owner = pltpu.make_async_copy(owner, owner_row, local_sem.at[4])
    load_pairs = pltpu.make_async_copy(pairs, pair_rows, local_sem.at[5])
    load_psd = pltpu.make_async_copy(psd_hbm, psd, local_sem.at[6])
    load_green = [
        pltpu.make_async_copy(green.at[k, c], gbuf.at[k, :, :, own_points], local_sem.at[k])
        for k in range(2)
    ]
    load_table = pltpu.make_async_copy(table.at[z * 2 + c], phi, local_sem.at[2])
    load_obs = pltpu.make_async_copy(observed, obs, local_sem.at[3])
    load_owner.start()
    load_pairs.start()
    load_psd.start()
    for copy in load_green:
        copy.start()
    load_table.start()
    pl.semaphore_wait(barrier, len(friends) + z)
    for dz in range(1, freq_devices):

        @pl.when(z >= dz)
        def _():
            pl.semaphore_signal(z_here, inc=1, device_id={"freq": z - dz}, device_id_type=MESH)


    swap_psd = remote(psd_hbm, psd_other, core_send.at[2], core_recv.at[2], other)
    half = gbuf.shape[1] // 2

    def swap_green(n):
        k, some = n // 2, pl.ds(n % 2 * half, half)
        return remote(
            green.at[k, 1 - c, some], gbuf.at[k, some, :, other_points],
            green_send.at[0], green_recv.at[n], other,
        )

    swap_psd.start()
    for n in range(4):
        swap_green(n).start()
    load_obs.start()

    def weigh(k, first, count, where, row):
        def body(b, carry):
            for i in range(4):
                place = first + 4 * b + i
                wbuf[k, place, :, where] = (gbuf[k, place, :, where].astype(f32) * row).astype(bf16)
            return carry

        lax.fori_loop(0, count // 4, body, 0)

    load_owner.wait()
    load_pairs.wait()
    square = (slot_count, slot_count)
    across = lax.broadcasted_iota(jnp.int32, square, 1)
    along = lax.broadcasted_iota(jnp.int32, square, 0)

    def down(row):
        return jnp.sum(jnp.where(across == along, jnp.broadcast_to(row, square), 0), axis=1, keepdims=True)

    their_owner = jnp.broadcast_to(owner_row[...], square)
    my_owner = down(owner_row[...])
    earlier = (their_owner < my_owner) | ((their_owner == my_owner) & (across < along))
    ids_row[...] = jnp.zeros_like(ids_row)
    entry_slot = jnp.sum(jnp.where(earlier, 1, 0), axis=1, keepdims=True)
    hit = entry_slot == across
    for k in range(2):
        chosen = jnp.where(hit, down(pair_rows[pl.ds(k, 1), :]), 0)
        ids_row[pl.ds(k, 1), pl.ds(0, slot_count)] = jnp.sum(chosen, axis=0, keepdims=True)
    move_ids = pltpu.make_async_copy(ids_row, ids, local_sem.at[7])
    move_ids.start()

    load_psd.wait()
    own_row = psd[pl.ds(c, 1), :]
    for k in range(2):
        load_green[k].wait()
        weigh(k, 0, 2 * half, own_points, own_row)

    load_table.wait()
    rows = phi.shape[0]
    row_in_group = lax.broadcasted_iota(jnp.int32, (rows, lags), 0) % group
    phi_values = phi[...].astype(f32)
    for i in range(group):
        spread[:, pl.ds(i * lags, lags)] = jnp.where(row_in_group == i, phi_values, 0.0).astype(bf16)

    recv1[48] = jnp.zeros_like(recv1[48])
    gsum[...] = jnp.zeros_like(gsum)
    mis_own[...] = jnp.zeros_like(mis_own)
    move_ids.wait()
    swap_psd.wait_recv()
    other_row = psd_other[pl.ds(c, 1), :]
    for n in range(4):
        swap_green(n).wait_recv()
        weigh(n // 2, n % 2 * half, half, other_points, other_row)

    def units(slots):
        pairs_of = []
        for slot in slots:
            left = wbuf[:, ids[0, slot]].reshape(2 * block, 2 * points)
            right = gbuf[:, ids[1, slot]].reshape(2 * block, 2 * points)
            acc = lax.dot_general(left, right, (((1,), (1,)), ((), ())), preferred_element_type=f32)
            real = acc[:block, :block] + acc[block:, block:]
            imag = acc[block:, :block] - acc[:block, block:]
            pairs_of.append((real, imag))
        return pairs_of

    def copy1(n):
        t, role, u = n // 24, (n % 24) // 8, n % 8
        h, d, j = u % 2, (u // 2) % 2, u // 4
        r = jnp.where(role == 1, lane(1 - d, j), lane(d, j))
        i = jnp.where(role == 0, t * 2 + j, 4 + t * 4 + r)
        return remote(send1.at[n], recv1.at[n], one_send.at[0], one_recv.at[i], neighbour(h, d))

    def wait_all(buffer, count, semaphore):
        some = buffer.at[pl.ds(0, count)]
        pltpu.make_async_copy(some, some, semaphore).wait()

    def wait1(i):
        wait_all(recv1, 4, one_recv.at[i])

    def choose(i, values):
        chosen = values[0]
        for n in range(1, len(values)):
            chosen = jnp.where(i >= n, values[n], chosen) if values[n] != values[n - 1] else chosen
        return chosen

    groups = [
        (0, 1, 1), (0, 0, 0), (0, 0, 1), (2, 1, 0), (0, 1, 0), (2, 1, 1),
        (1, 0, 1), (1, 0, 0), (2, 0, 1), (2, 0, 0), (1, 1, 0), (1, 1, 1),
    ]

    def first_ring(i, carry):
        part, t, j = (choose(i, [values[k] for values in groups]) for k in range(3))
        through = part == 1
        role = jnp.where(through, 2, part // 2)
        first = t * 24 + role * 8 + j * 4

        @pl.when(i == 6)
        def _():
            load_obs.wait()
            energies()

        @pl.when((i == 6) | (i > 9))
        def _():
            project(jnp.where(i == 6, 0, i - 9))

        @pl.when(through)
        def _():
            wait1(t * 2 + j)

        slots = []
        for u in range(4):
            h, d = u % 2, u // 2
            o = jnp.where(part == 0, 2, 1 + 2 * d)
            r = jnp.where(part == 2, lane(1 - d, j), lane(d, j))
            slots.append(slot_of(t, h, o, r))
        for u, values in enumerate(units(slots)):
            n = first + u
            with_n = jnp.where(through, n - 16, 48)
            for k in range(2):
                send1[n, k] = (values[k] + recv1[with_n, k].astype(f32)).astype(bf16)
        for u in range(4):
            copy1(first + u).start()
        return carry

    def arrival1(t, h, d, r):
        role = 2 - (r + d) % 2
        return t * 24 + role * 8 + lane_place(r) * 4 + d * 2 + h

    def line_sums(t, wanted):
        for r in sorted({r for h, r in wanted}):
            wait1(4 + t * 4 + r)
        sums = []
        for (h, r), values in zip(wanted, units([slot_of(t, h, 0, r) for h, r in wanted])):
            arrived = [recv1[arrival1(t, h, d, r)].astype(f32) for d in range(2)]
            sums.append([values[k] + (arrived[0][k] + arrived[1][k]) for k in range(2)])
        return sums

    def place(t, h, d):
        return (t * 2 + h) * 2 + d

    def copy_a(t, h, d):
        i = place(t, h, d)
        return remote(send_a.at[i], recv_a.at[i], a_send.at[0], a_recv.at[t], neighbour(1 - h, d))

    def copy_b(t, h, d, k):
        i = place(t, h, d)
        return remote(
            send_b.at[i, k], recv_b.at[i, k], b_send.at[0], b_recv.at[t], neighbour(1 - h, d)
        )

    def second_ring_far(t):
        for h, values in enumerate(line_sums(t, [(0, 2), (1, 2)])):
            for d in range(2):
                send_a[place(t, h, d)] = values[d].astype(bf16)
                copy_a(t, h, d).start()

    def second_ring_near(t):
        wanted = [(h, 1 + 2 * d) for d in range(2) for h in range(2)]
        for (h, r), values in zip(wanted, line_sums(t, wanted)):
            d = r // 2
            i = place(t, h, d)
            send_b[i, 1 - d] = values[1 - d].astype(bf16)
            copy_b(t, h, d, 1 - d).start()
            keep[i] = values[d]

    def own_part(t):
        for h, values in enumerate(line_sums(t, [(0, 0), (1, 0)])):
            for k in range(2):
                own_sum[t * 2 + h, k] = values[k]

    def second_ring_close(t):
        wait_all(recv_a, 4, a_recv.at[t])
        for d in range(2):
            for h in range(2):
                i = place(t, h, d)
                send_b[i, d] = (keep[i] + recv_a[i].astype(f32)).astype(bf16)
                copy_b(t, h, d, d).start()

    def copy_g1(t, h, d):
        s = slot_of(t, h, 0, 0)
        return remote(abuf.at[s], abuf.at[s], g_send.at[0], g1_recv.at[t], neighbour(1 - h, d))

    def copy_g1f(t, h, d):
        s = slot_of(t, h, 0, 3 - 2 * d)
        return remote(abuf.at[s, d], abuf.at[s, d], g_send.at[0], g1f_recv.at[t], neighbour(1 - h, d))

    def copy_g2(t, h, d, r):
        s = slot_of(t, h, 0, r)
        return remote(abuf.at[s], abuf.at[s], g_send.at[0], g2_recv.at[t * 4 + r], neighbour(h, d))

    def copy_g2f(t, h, d, j):
        r = lane(d, j)
        s = slot_of(t, h, 3 - 2 * d, r)
        return remote(abuf.at[s], abuf.at[s], g_send.at[0], g2f_recv.at[r], neighbour(h, d))

    ones = jnp.ones((8, block), f32)

    def lane_sum(values):
        return lax.dot_general(
            ones[:, : values.shape[1]], values, (((1,), (1,)), ((), ())),
            precision=lax.Precision.HIGHEST, preferred_element_type=f32,
        )

    def own_adjoint(t, carry):
        wait_all(recv_b, 4, b_recv.at[t])
        for h in range(2):
            s, q = slot_of(t, h, 0, 0), h * 2 + t
            kept = jnp.zeros((block, block), f32)
            for k in range(2):
                value = own_sum[t * 2 + h, k]
                for d in range(2):
                    value = value + recv_b[place(t, h, d), k].astype(f32)
                cross = value * f32(root_scale)
                seen = ohat[q, k]
                abuf[s, k] = (0.5 * cross - seen * f32(1.0 / lags)).astype(bf16)
                kept = kept + cross * (f32(lags / 2) * cross - 2.0 * seen)
            for d in range(2):
                copy_g1(t, h, d).start()
            for d in range(2):
                copy_g2(t, h, d, 0).start()
            total[q] = kept
        return carry

    def gather_1(t):
        wait_all(abuf, 4, g1_recv.at[t])

        def body(v, carry):
            h, d = v % 2, v // 2
            copy_g1f(t, h, d).start()
            for side_d in range(2):
                copy_g2(t, h, side_d, 3 - 2 * d).start()
            return carry

        lax.fori_loop(0, 4, body, 0)

    def gather_2(t):
        wait_all(abuf, 2, g1f_recv.at[t])
        for h in range(2):
            for d in range(2):
                copy_g2(t, h, d, 2).start()

    def gather_lane(t, r):
        wait_all(abuf, 4, g2_recv.at[t * 4 + r])
        for h in range(2):
            copy_g2f(t, h, r % 2, lane_place(r)).start()

    def gather_end(r):
        wait_all(abuf, 4, g2f_recv.at[r])

    def back(slots, carry):
        for s in slots:
            weights = abuf[s]
            top = jnp.concatenate((weights[0], -weights[1]), axis=1)
            low = jnp.concatenate((weights[1], weights[0]), axis=1)
            right = gbuf[:, ids[1, s]].reshape(2 * block, 2 * points)
            moved = jnp.dot(
                jnp.concatenate((top, low), axis=0), right, preferred_element_type=f32
            )
            left = gbuf[:, ids[0, s]].reshape(2 * block, 2 * points).astype(f32)
            carry = carry + jnp.sum((moved * left).reshape(2 * block // 8, 8, 2 * points), axis=0)
        return carry

    def project(quarter):
        chunks = block // group // 4

        def body(i, carry):
            first = pl.multiple_of((quarter * chunks + i) * group, group)
            seen = jnp.concatenate(
                [
                    jnp.concatenate([obs[s, first + k] for k in range(group)], axis=1)
                    for s in range(pair_dev)
                ],
                axis=0,
            )
            out = lax.dot_general(
                spread[...], seen, (((1,), (1,)), ((), ())), preferred_element_type=f32
            )
            out = jnp.sum(out.reshape(pieces, 4 * group, pair_dev * block), axis=0)
            for s in range(pair_dev):
                for k in range(2):
                    cols = slice(s * block, (s + 1) * block)
                    ohat[2 * c + s, k, pl.ds(first, group), :] = out[k * group : (k + 1) * group, cols]
                    ohat_send[s, k, pl.ds(first, group), :] = out[(2 + k) * group : (3 + k) * group, cols]
            return carry

        lax.fori_loop(0, chunks, body, 0, unroll=2)

    swap_ohat = remote(
        ohat_send, ohat.at[pl.ds(2 * c, 2)], core_send.at[3], core_recv.at[3], other
    )
    part_rows = block // freq_devices

    def energies():
        def body(i, carry):
            for s in range(pair_dev):
                seen = obs[s, z * part_rows + i].astype(f32)
                energy[pl.ds(s * part_rows + i, 1), :] = jnp.sum(seen * seen, axis=0, keepdims=True)
            return carry

        lax.fori_loop(0, part_rows, body, 0)

    swap_mis = remote(mis_own, mis_other, core_send.at[4], core_recv.at[4], other)

    def copy_z(dz):
        return pltpu.make_async_remote_copy(
            src_ref=mis_pair, dst_ref=mis_freq.at[dz - 1],
            send_sem=z_send.at[0], recv_sem=z_recv.at[0],
            device_id={"freq": (z + dz) % freq_devices}, device_id_type=MESH,
        )

    def misfit_parts():
        for q in range(2 * stages):
            mis_own[pl.ds(q, 1), :] = lane_sum(total[q])[:1]
        swap_mis.start()

    def misfit_sums():
        swap_mis.wait_recv()
        mis_pair[...] = mis_own[...] + mis_other[...]

        @pl.when(z < freq_devices - 1)
        def _():
            pl.semaphore_wait(z_here, freq_devices - 1 - z)

        for dz in range(1, freq_devices):
            copy_z(dz).start()

    def misfit_end():
        wait_all(mis_freq, freq_devices - 1, z_recv.at[0])
        mine = mis_pair[...]
        for dz in range(1, freq_devices):
            mine = mine + mis_freq[dz - 1]
        from_observed = lane_sum(energy[...])[:1]
        picked = jnp.zeros((mine.shape[0], part_rows), f32)
        for part in range(freq_devices):
            picked = jnp.where(z == part, mine[:, part * part_rows : (part + 1) * part_rows], picked)
        for s in range(pair_dev):
            row = jnp.where(c == 0, picked[s : s + 1], picked[2 + s : 3 + s])
            row = row + from_observed[:, s * part_rows : (s + 1) * part_rows]
            misfit_out[pl.ds(s, 1), :] = row * f32(1.0 / (2.0 * block * lags * freq_total))

    lax.fori_loop(0, 12, first_ring, 0)
    project(3)
    swap_ohat.start()
    own_part(0)
    second_ring_far(0)
    second_ring_near(0)
    second_ring_far(1)
    second_ring_close(0)
    second_ring_near(1)
    own_part(1)
    second_ring_close(1)
    swap_ohat.wait_recv()
    lax.fori_loop(0, 2, own_adjoint, 0)

    steps = [
        ([], (0, 1), (0, 0), (0, 0)),
        ([(misfit_parts,), (gather_1, 0)], (0, 0), (0, 0), (1, 2)),
        ([(gather_1, 1)], (1, 0), (0, 0), (1, 2)),
        ([(gather_lane, 0, 0), (misfit_sums,)], (0, 0), (1, 2), (0, 0)),
        ([(gather_lane, 1, 0)], (1, 0), (1, 2), (0, 0)),
        ([(gather_lane, 0, 1)], (0, 0), (1, 2), (1, 0)),
        ([(gather_2, 0), (gather_lane, 0, 3)], (0, 0), (1, 2), (3, 0)),
        ([(gather_2, 1)], (0, 1), (0, 0), (2, 0)),
        ([(gather_lane, 1, 1)], (1, 0), (1, 2), (1, 0)),
        ([(gather_lane, 1, 3)], (1, 0), (1, 2), (3, 0)),
        ([(gather_end, 0)], (0, 1), (2, 0), (0, 0)),
        ([(gather_lane, 0, 2)], (0, 0), (1, 2), (2, 0)),
        ([(gather_lane, 1, 2)], (1, 0), (1, 2), (2, 0)),
        ([(gather_end, 1)], (0, 1), (2, 0), (1, 0)),
        ([(gather_end, 3)], (0, 1), (2, 0), (3, 0)),
        ([(gather_end, 2)], (0, 1), (2, 0), (2, 0)),
    ]

    def gather_step(i, carry):
        for n, step in enumerate(steps):
            if step[0]:
                @pl.when(i == n)
                def _(actions=tuple(step[0])):
                    for action in actions:
                        action[0](*action[1:])

        slots = []
        for u in range(4):
            t, o, r = (
                choose(i, [step[part][0] + u // 2 * step[part][1] for step in steps]) for part in (1, 2, 3)
            )
            slots.append(slot_of(t, u % 2, o, r))
        return back(slots, carry)

    gsum[...] = lax.fori_loop(0, len(steps), gather_step, gsum[...])

    lines = jnp.sum(gsum[...], axis=0, keepdims=True) * f32(1.0 / (block * math.sqrt(slot_count)))
    gsend[...] = jnp.broadcast_to(lines[:, points:], gsend.shape)
    swap_sum = remote(gsend, grecv, core_send.at[5], core_recv.at[5], other)
    swap_sum.start()
    misfit_end()
    swap_sum.wait_recv()
    row_ids = lax.broadcasted_iota(jnp.int32, (2, points), 0)
    gradient_out[...] = jnp.where(
        row_ids == c, jnp.broadcast_to(lines[:, :points], (2, points)), grecv[:2]
    )

    swap_psd.wait_send()
    wait_all(gbuf.at[:, :, :, other_points], 2, green_send.at[0])
    swap_ohat.wait_send()
    swap_mis.wait_send()
    swap_sum.wait_send()
    wait_all(mis_freq, freq_devices - 1, z_send.at[0])
    wait_all(send1, 24 * stages, one_send.at[0])
    wait_all(send_a, 4 * stages, a_send.at[0])
    wait_all(send_b, 4 * stages, b_send.at[0])
    wait_all(abuf, 30 * stages, g_send.at[0])


def hand_on(gradient, misfit, gradient_out, misfit_out):
    gradient_out[...] = gradient[...]
    misfit_out[...] = misfit[...]


def local(green_spectra, source_psd, pair_list, owner_map, observed):
    freq_devices = lax.axis_size("freq")
    planes, freq_dev, stations, points = green_spectra.shape
    pair_dev, block, unused_cols, lags = observed.shape
    slot_count = owner_map.shape[0]
    blocks = stations // block
    freq_total = freq_dev * freq_devices
    table = jnp.asarray(phase_table(freq_total, lags, freq_devices))
    rows = table.shape[1]
    units = stages * 2 * 2
    dma = pltpu.SemaphoreType.DMA
    vmem = pl.BlockSpec(memory_space=pltpu.VMEM)
    hbm = pl.BlockSpec(memory_space=pltpu.HBM)
    pair = (2, block, block)
    gradient, misfit = pl.pallas_call(
        functools.partial(kernel, freq_devices),
        out_shape=(
            jax.ShapeDtypeStruct((freq_dev, points), f32),
            jax.ShapeDtypeStruct((pair_dev, block // freq_devices), f32),
        ),
        in_specs=[hbm] * 6,
        out_specs=(vmem, vmem),
        scratch_shapes=[
            pltpu.VMEM((2, blocks, block, 2 * points), bf16),
            pltpu.VMEM((2, blocks, block, 2 * points), bf16),
            pltpu.VMEM((freq_dev, points), f32),
            pltpu.VMEM((freq_dev, points), f32),
            pltpu.VMEM((1, slot_count), jnp.int32),
            pltpu.VMEM((2, slot_count), jnp.int32),
            pltpu.VMEM((8, 128), jnp.int32),
            pltpu.SMEM((8, 128), jnp.int32),
            pltpu.VMEM((pair_dev, block, block, lags), bf16),
            pltpu.VMEM((rows, lags), bf16),
            pltpu.VMEM((rows, group * lags), bf16),
            pltpu.VMEM((2 * pair_dev,) + pair, f32),
            pltpu.VMEM((pair_dev,) + pair, f32),
            pltpu.VMEM((pair_dev * (block // freq_devices), lags), f32),
            pltpu.VMEM((24 * stages,) + pair, bf16),
            pltpu.VMEM((24 * stages + 1,) + pair, bf16),
            pltpu.VMEM((units, block, block), bf16),
            pltpu.VMEM((units, block, block), bf16),
            pltpu.VMEM((units,) + pair, bf16),
            pltpu.VMEM((units,) + pair, bf16),
            pltpu.VMEM((units, block, block), f32),
            pltpu.VMEM((2 * stages,) + pair, f32),
            pltpu.VMEM((slot_count,) + pair, bf16),
            pltpu.VMEM((2 * stages, block, block), f32),
            pltpu.VMEM((8, block), f32),
            pltpu.VMEM((8, block), f32),
            pltpu.VMEM((8, block), f32),
            pltpu.VMEM((freq_devices - 1, 8, block), f32),
            pltpu.VMEM((8, 2 * points), f32),
            pltpu.VMEM((8, points), f32),
            pltpu.VMEM((8, points), f32),
            dma((8,)),
            dma((6,)),
            dma((6,)),
            dma((1,)),
            dma((4,)),
            dma((1,)),
            dma((6 * stages,)),
            dma((1,)),
            dma((stages,)),
            dma((1,)),
            dma((stages,)),
            dma((1,)),
            dma((stages,)),
            dma((stages,)),
            dma((4 * stages,)),
            dma((4,)),
            dma((1,)),
            dma((1,)),
            pltpu.SemaphoreType.REGULAR,
        ],
        compiler_params=pltpu.CompilerParams(
            collective_id=0, has_side_effects=True, vmem_limit_bytes=60 * 1024 * 1024
        ),
        cost_estimate=pl.CostEstimate(
            flops=8 * slot_count * freq_dev * 2 * block * block * points,
            bytes_accessed=12 * 1024 * 1024,
            transcendentals=0,
        ),
        name="misfit_gradient",
    )(
        owner_map.reshape(1, slot_count),
        pair_list.T,
        source_psd,
        table,
        green_spectra.reshape(planes, freq_dev, blocks, block, points),
        observed,
    )
    return pl.pallas_call(
        hand_on,
        out_shape=(
            jax.ShapeDtypeStruct(gradient.shape, f32),
            jax.ShapeDtypeStruct(misfit.shape, f32),
        ),
        in_specs=[vmem, vmem],
        out_specs=(vmem, vmem),
        name="hand_on",
    )(gradient, misfit)


def solution(mesh):
    in_specs = (
        P(None, "freq", None, "grid"),
        P("freq", "grid"),
        P(),
        P(),
        P("grid", None, None, None),
    )
    out_specs = (P("freq", "grid"), P("grid", "freq"))
    return jax.shard_map(local, mesh=mesh, in_specs=in_specs, out_specs=out_specs, check_vma=False)
```

```python
import functools
import math

import jax
import jax.numpy as jnp
import ml_dtypes
import numpy as np
from jax import lax
from jax.experimental import pallas as pl
from jax.experimental.pallas import tpu as pltpu
from jax.sharding import PartitionSpec as P

harmonic_step = 3
side = 4
stages = 2
pieces = 3
group = 8
MESH = pl.DeviceIdType.MESH
f32 = jnp.float32
bf16 = jnp.bfloat16


def phase_table(freq_total, lag_count, freq_devices):
    freq_ids = np.arange(freq_total)[:, None]
    turns = harmonic_step * (freq_ids + 1) * np.arange(lag_count)[None, :] % lag_count
    angles = turns * (2.0 * math.pi / lag_count)
    exact = np.stack((np.cos(angles), -np.sin(angles)), axis=1)
    parts = []
    for unused in range(pieces):
        part = exact.astype(ml_dtypes.bfloat16)
        parts.append(part)
        exact = exact - part.astype(np.float64)
    table = np.stack(parts).reshape(pieces, freq_devices, 2, 2, lag_count)
    both = np.stack((table, table[:, :, ::-1]), axis=2)
    both = both.transpose(1, 2, 0, 3, 4, 5).reshape(freq_devices * 2, pieces * 4, lag_count)
    return np.repeat(both, group, axis=1)


def kernel(
    freq_devices,
    owner,
    pairs,
    psd_hbm,
    table,
    green,
    observed,
    gradient_out,
    misfit_out,
    gbuf,
    wbuf,
    psd,
    psd_other,
    owner_row,
    pair_rows,
    ids_row,
    ids,
    obs,
    phi,
    spread,
    ohat,
    ohat_send,
    energy,
    send1,
    recv1,
    send_a,
    recv_a,
    send_b,
    recv_b,
    keep,
    own_sum,
    abuf,
    total,
    mis_own,
    mis_other,
    mis_pair,
    mis_freq,
    gsum,
    gsend,
    grecv,
    local_sem,
    core_send,
    core_recv,
    green_send,
    green_recv,
    one_send,
    one_recv,
    a_send,
    a_recv,
    b_send,
    b_recv,
    g_send,
    g1_recv,
    g1f_recv,
    g2_recv,
    g2f_recv,
    z_send,
    z_recv,
    z_here,
    near_here,
):
    z = lax.axis_index("freq")
    g = lax.axis_index("grid")
    c = g % 2
    x = (g // 2) % side
    y = g // (2 * side)
    other = g + 1 - 2 * c
    points = psd_hbm.shape[1]
    pair_dev, block, unused_cols, lags = observed.shape
    freq_total = 2 * freq_devices
    slot_count = 2 * side * side * pair_dev
    root_scale = 1.0 / math.sqrt(points * 2 * side * side)

    def neighbour(axis, d):
        step = 1 + 2 * d
        nx = (x + (1 - axis) * step) % side
        ny = (y + axis * step) % side
        return (ny * side + nx) * 2 + c

    def slot_of(t, h, o, r):
        sx = (x + (1 - h) * o + h * r) % side
        sy = (y + h * o + (1 - h) * r) % side
        return (sy * side + sx) * 4 + h * 2 + t

    def lane(d, j):
        return (1 - d) * (2 - 2 * j) + d * (1 + 2 * j)

    def lane_place(r):
        return ((r + 1) // 2 + 1) % 2

    def remote(src, dst, send, recv, device):
        return pltpu.make_async_remote_copy(
            src_ref=src, dst_ref=dst, send_sem=send, recv_sem=recv,
            device_id={"grid": device}, device_id_type=MESH,
        )

    barrier = pltpu.get_barrier_semaphore()
    def distance(p):
        return jnp.minimum(p, side - p)

    lower = distance(x) + distance(y)
    pl.semaphore_signal(barrier, inc=1, device_id={"grid": other}, device_id_type=MESH)

    def greet(semaphore, upward):
        for axis, p in enumerate((x, y)):
            for d in range(2):
                q = (p + 1 + 2 * d) % side
                near, far = (distance(p), distance(q)) if upward else (distance(q), distance(p))

                @pl.when(near < far)
                def _():
                    pl.semaphore_signal(
                        semaphore, inc=1, device_id={"grid": neighbour(axis, d)}, device_id_type=MESH
                    )

    greet(barrier, True)
    for dz in range(1, freq_devices):

        @pl.when(z + dz < freq_devices)
        def _():
            pl.semaphore_signal(barrier, inc=1, device_id={"freq": z + dz}, device_id_type=MESH)

    own_points = pl.ds(0, points)
    other_points = pl.ds(points, points)
    load_owner = pltpu.make_async_copy(owner, owner_row, local_sem.at[4])
    load_pairs = pltpu.make_async_copy(pairs, pair_rows, local_sem.at[5])
    load_psd = pltpu.make_async_copy(psd_hbm, psd, local_sem.at[6])
    load_green = [
        pltpu.make_async_copy(green.at[k, c], gbuf.at[k, :, :, own_points], local_sem.at[k])
        for k in range(2)
    ]
    load_table = pltpu.make_async_copy(table.at[z * 2 + c], phi, local_sem.at[2])
    load_obs = pltpu.make_async_copy(observed, obs, local_sem.at[3])
    load_owner.start()
    load_pairs.start()
    load_psd.start()
    for copy in load_green:
        copy.start()
    load_table.start()
    pl.semaphore_wait(barrier, 1 + lower + z)

    swap_psd = remote(psd_hbm, psd_other, core_send.at[2], core_recv.at[2], other)
    half = gbuf.shape[1] // 2

    def swap_green(n):
        k, some = n // 2, pl.ds(n % 2 * half, half)
        return remote(
            green.at[k, 1 - c, some], gbuf.at[k, some, :, other_points],
            green_send.at[0], green_recv.at[n], other,
        )

    swap_psd.start()
    for n in range(4):
        swap_green(n).start()
    load_obs.start()

    greet(near_here, False)
    for dz in range(1, freq_devices):

        @pl.when(z >= dz)
        def _():
            pl.semaphore_signal(z_here, inc=1, device_id={"freq": z - dz}, device_id_type=MESH)

    def weigh(k, first, count, where, row):
        def body(b, carry):
            for i in range(4):
                place = first + 4 * b + i
                wbuf[k, place, :, where] = (gbuf[k, place, :, where].astype(f32) * row).astype(bf16)
            return carry

        lax.fori_loop(0, count // 4, body, 0)

    load_owner.wait()
    load_pairs.wait()
    square = (slot_count, slot_count)
    across = lax.broadcasted_iota(jnp.int32, square, 1)
    along = lax.broadcasted_iota(jnp.int32, square, 0)

    def down(row):
        return jnp.sum(jnp.where(across == along, jnp.broadcast_to(row, square), 0), axis=1, keepdims=True)

    their_owner = jnp.broadcast_to(owner_row[...], square)
    my_owner = down(owner_row[...])
    earlier = (their_owner < my_owner) | ((their_owner == my_owner) & (across < along))
    ids_row[...] = jnp.zeros_like(ids_row)
    entry_slot = jnp.sum(jnp.where(earlier, 1, 0), axis=1, keepdims=True)
    hit = entry_slot == across
    for k in range(2):
        chosen = jnp.where(hit, down(pair_rows[pl.ds(k, 1), :]), 0)
        ids_row[pl.ds(k, 1), pl.ds(0, slot_count)] = jnp.sum(chosen, axis=0, keepdims=True)
    move_ids = pltpu.make_async_copy(ids_row, ids, local_sem.at[7])
    move_ids.start()

    load_psd.wait()
    own_row = psd[pl.ds(c, 1), :]
    for k in range(2):
        load_green[k].wait()
        weigh(k, 0, 2 * half, own_points, own_row)

    load_table.wait()
    rows = phi.shape[0]
    row_in_group = lax.broadcasted_iota(jnp.int32, (rows, lags), 0) % group
    phi_values = phi[...].astype(f32)
    for i in range(group):
        spread[:, pl.ds(i * lags, lags)] = jnp.where(row_in_group == i, phi_values, 0.0).astype(bf16)

    recv1[48] = jnp.zeros_like(recv1[48])
    gsum[...] = jnp.zeros_like(gsum)
    mis_own[...] = jnp.zeros_like(mis_own)
    move_ids.wait()
    swap_psd.wait_recv()
    other_row = psd_other[pl.ds(c, 1), :]
    for n in range(4):
        swap_green(n).wait_recv()
        weigh(n // 2, n % 2 * half, half, other_points, other_row)

    def units(slots):
        pairs_of = []
        for slot in slots:
            left = wbuf[:, ids[0, slot]].reshape(2 * block, 2 * points)
            right = gbuf[:, ids[1, slot]].reshape(2 * block, 2 * points)
            acc = lax.dot_general(left, right, (((1,), (1,)), ((), ())), preferred_element_type=f32)
            real = acc[:block, :block] + acc[block:, block:]
            imag = acc[block:, :block] - acc[:block, block:]
            pairs_of.append((real, imag))
        return pairs_of

    def copy1(n):
        t, role, u = n // 24, (n % 24) // 8, n % 8
        h, d, j = u % 2, (u // 2) % 2, u // 4
        r = jnp.where(role == 1, lane(1 - d, j), lane(d, j))
        i = jnp.where(role == 0, t * 2 + j, 4 + t * 4 + r)
        return remote(send1.at[n], recv1.at[n], one_send.at[0], one_recv.at[i], neighbour(h, d))

    def wait_all(buffer, count, semaphore):
        some = buffer.at[pl.ds(0, count)]
        pltpu.make_async_copy(some, some, semaphore).wait()

    def wait1(i):
        wait_all(recv1, 4, one_recv.at[i])

    def choose(i, values):
        chosen = values[0]
        for n in range(1, len(values)):
            chosen = jnp.where(i >= n, values[n], chosen) if values[n] != values[n - 1] else chosen
        return chosen

    groups = [
        (0, 1, 1), (0, 0, 0), (0, 0, 1), (2, 1, 0), (0, 1, 0), (2, 1, 1),
        (1, 0, 1), (1, 0, 0), (2, 0, 1), (2, 0, 0), (1, 1, 0), (1, 1, 1),
    ]

    def first_ring(i, carry):
        part, t, j = (choose(i, [values[k] for values in groups]) for k in range(3))
        through = part == 1
        role = jnp.where(through, 2, part // 2)
        first = t * 24 + role * 8 + j * 4

        @pl.when(i == 6)
        def _():
            load_obs.wait()
            energies()

        @pl.when((i == 6) | (i > 9))
        def _():
            project(jnp.where(i == 6, 0, i - 9))

        @pl.when(through)
        def _():
            wait1(t * 2 + j)

        slots = []
        for u in range(4):
            h, d = u % 2, u // 2
            o = jnp.where(part == 0, 2, 1 + 2 * d)
            r = jnp.where(part == 2, lane(1 - d, j), lane(d, j))
            slots.append(slot_of(t, h, o, r))
        for u, values in enumerate(units(slots)):
            n = first + u
            with_n = jnp.where(through, n - 16, 48)
            for k in range(2):
                send1[n, k] = (values[k] + recv1[with_n, k].astype(f32)).astype(bf16)
        @pl.when((i == 0) & (lower < side))
        def _():
            pl.semaphore_wait(near_here, side - lower)

        for u in range(4):
            copy1(first + u).start()
        return carry

    def arrival1(t, h, d, r):
        role = 2 - (r + d) % 2
        return t * 24 + role * 8 + lane_place(r) * 4 + d * 2 + h

    def line_sums(t, wanted):
        for r in sorted({r for h, r in wanted}):
            wait1(4 + t * 4 + r)
        sums = []
        for (h, r), values in zip(wanted, units([slot_of(t, h, 0, r) for h, r in wanted])):
            arrived = [recv1[arrival1(t, h, d, r)].astype(f32) for d in range(2)]
            sums.append([values[k] + (arrived[0][k] + arrived[1][k]) for k in range(2)])
        return sums

    def place(t, h, d):
        return (t * 2 + h) * 2 + d

    def copy_a(t, h, d):
        i = place(t, h, d)
        return remote(send_a.at[i], recv_a.at[i], a_send.at[0], a_recv.at[t], neighbour(1 - h, d))

    def copy_b(t, h, d, k):
        i = place(t, h, d)
        return remote(
            send_b.at[i, k], recv_b.at[i, k], b_send.at[0], b_recv.at[t], neighbour(1 - h, d)
        )

    def second_ring_far(t):
        for h, values in enumerate(line_sums(t, [(0, 2), (1, 2)])):
            for d in range(2):
                send_a[place(t, h, d)] = values[d].astype(bf16)
                copy_a(t, h, d).start()

    def second_ring_near(t):
        wanted = [(h, 1 + 2 * d) for d in range(2) for h in range(2)]
        for (h, r), values in zip(wanted, line_sums(t, wanted)):
            d = r // 2
            i = place(t, h, d)
            send_b[i, 1 - d] = values[1 - d].astype(bf16)
            copy_b(t, h, d, 1 - d).start()
            keep[i] = values[d]

    def own_part(t):
        for h, values in enumerate(line_sums(t, [(0, 0), (1, 0)])):
            for k in range(2):
                own_sum[t * 2 + h, k] = values[k]

    def second_ring_close(t):
        wait_all(recv_a, 4, a_recv.at[t])
        for d in range(2):
            for h in range(2):
                i = place(t, h, d)
                send_b[i, d] = (keep[i] + recv_a[i].astype(f32)).astype(bf16)
                copy_b(t, h, d, d).start()

    def copy_g1(t, h, d):
        s = slot_of(t, h, 0, 0)
        return remote(abuf.at[s], abuf.at[s], g_send.at[0], g1_recv.at[t], neighbour(1 - h, d))

    def copy_g1f(t, h, d):
        s = slot_of(t, h, 0, 3 - 2 * d)
        return remote(abuf.at[s, d], abuf.at[s, d], g_send.at[0], g1f_recv.at[t], neighbour(1 - h, d))

    def copy_g2(t, h, d, r):
        s = slot_of(t, h, 0, r)
        return remote(abuf.at[s], abuf.at[s], g_send.at[0], g2_recv.at[t * 4 + r], neighbour(h, d))

    def copy_g2f(t, h, d, j):
        r = lane(d, j)
        s = slot_of(t, h, 3 - 2 * d, r)
        return remote(abuf.at[s], abuf.at[s], g_send.at[0], g2f_recv.at[r], neighbour(h, d))

    ones = jnp.ones((8, block), f32)

    def lane_sum(values):
        return lax.dot_general(
            ones[:, : values.shape[1]], values, (((1,), (1,)), ((), ())),
            precision=lax.Precision.HIGHEST, preferred_element_type=f32,
        )

    def own_adjoint(t, carry):
        wait_all(recv_b, 4, b_recv.at[t])
        for h in range(2):
            s, q = slot_of(t, h, 0, 0), h * 2 + t
            kept = jnp.zeros((block, block), f32)
            for k in range(2):
                value = own_sum[t * 2 + h, k]
                for d in range(2):
                    value = value + recv_b[place(t, h, d), k].astype(f32)
                cross = value * f32(root_scale)
                seen = ohat[q, k]
                abuf[s, k] = (0.5 * cross - seen * f32(1.0 / lags)).astype(bf16)
                kept = kept + cross * (f32(lags / 2) * cross - 2.0 * seen)
            for d in range(2):
                copy_g1(t, h, d).start()
            for d in range(2):
                copy_g2(t, h, d, 0).start()
            total[q] = kept
        return carry

    def gather_1(t):
        wait_all(abuf, 4, g1_recv.at[t])

        def body(v, carry):
            h, d = v % 2, v // 2
            copy_g1f(t, h, d).start()
            for side_d in range(2):
                copy_g2(t, h, side_d, 3 - 2 * d).start()
            return carry

        lax.fori_loop(0, 4, body, 0)

    def gather_2(t):
        wait_all(abuf, 2, g1f_recv.at[t])
        for h in range(2):
            for d in range(2):
                copy_g2(t, h, d, 2).start()

    def gather_lane(t, r):
        wait_all(abuf, 4, g2_recv.at[t * 4 + r])
        for h in range(2):
            copy_g2f(t, h, r % 2, lane_place(r)).start()

    def gather_end(r):
        wait_all(abuf, 4, g2f_recv.at[r])

    def back(slots, carry, where, count):
        for s in slots:
            weights = abuf[s]
            top = jnp.concatenate((weights[0], -weights[1]), axis=1)
            low = jnp.concatenate((weights[1], weights[0]), axis=1)
            right = gbuf[:, ids[1, s], :, where].reshape(2 * block, count)
            moved = jnp.dot(
                jnp.concatenate((top, low), axis=0), right, preferred_element_type=f32
            )
            left = gbuf[:, ids[0, s], :, where].reshape(2 * block, count).astype(f32)
            carry = carry + jnp.sum((moved * left).reshape(2 * block // 8, 8, count), axis=0)
        return carry

    def project(quarter):
        chunks = block // group // 4

        def body(i, carry):
            first = pl.multiple_of((quarter * chunks + i) * group, group)
            seen = jnp.concatenate(
                [
                    jnp.concatenate([obs[s, first + k] for k in range(group)], axis=1)
                    for s in range(pair_dev)
                ],
                axis=0,
            )
            out = lax.dot_general(
                spread[...], seen, (((1,), (1,)), ((), ())), preferred_element_type=f32
            )
            out = jnp.sum(out.reshape(pieces, 4 * group, pair_dev * block), axis=0)
            for s in range(pair_dev):
                for k in range(2):
                    cols = slice(s * block, (s + 1) * block)
                    ohat[2 * c + s, k, pl.ds(first, group), :] = out[k * group : (k + 1) * group, cols]
                    ohat_send[s, k, pl.ds(first, group), :] = out[(2 + k) * group : (3 + k) * group, cols]
            return carry

        lax.fori_loop(0, chunks, body, 0, unroll=2)

    swap_ohat = remote(
        ohat_send, ohat.at[pl.ds(2 * c, 2)], core_send.at[3], core_recv.at[3], other
    )
    part_rows = block // freq_devices

    def energies():
        def body(i, carry):
            for s in range(pair_dev):
                seen = obs[s, z * part_rows + i].astype(f32)
                energy[pl.ds(s * part_rows + i, 1), :] = jnp.sum(seen * seen, axis=0, keepdims=True)
            return carry

        lax.fori_loop(0, part_rows, body, 0)

    swap_mis = remote(mis_own, mis_other, core_send.at[4], core_recv.at[4], other)

    def copy_z(dz):
        return pltpu.make_async_remote_copy(
            src_ref=mis_pair, dst_ref=mis_freq.at[dz - 1],
            send_sem=z_send.at[0], recv_sem=z_recv.at[0],
            device_id={"freq": (z + dz) % freq_devices}, device_id_type=MESH,
        )

    def misfit_parts():
        for q in range(2 * stages):
            mis_own[pl.ds(q, 1), :] = lane_sum(total[q])[:1]
        swap_mis.start()

    def misfit_sums():
        swap_mis.wait_recv()
        mis_pair[...] = mis_own[...] + mis_other[...]

        @pl.when(z < freq_devices - 1)
        def _():
            pl.semaphore_wait(z_here, freq_devices - 1 - z)

        for dz in range(1, freq_devices):
            copy_z(dz).start()

    def misfit_end():
        wait_all(mis_freq, freq_devices - 1, z_recv.at[0])
        mine = mis_pair[...]
        for dz in range(1, freq_devices):
            mine = mine + mis_freq[dz - 1]
        from_observed = lane_sum(energy[...])[:1]
        picked = jnp.zeros((mine.shape[0], part_rows), f32)
        for part in range(freq_devices):
            picked = jnp.where(z == part, mine[:, part * part_rows : (part + 1) * part_rows], picked)
        for s in range(pair_dev):
            row = jnp.where(c == 0, picked[s : s + 1], picked[2 + s : 3 + s])
            row = row + from_observed[:, s * part_rows : (s + 1) * part_rows]
            misfit_out[pl.ds(s, 1), :] = row * f32(1.0 / (2.0 * block * lags * freq_total))

    lax.fori_loop(0, 12, first_ring, 0)
    project(3)
    swap_ohat.start()
    own_part(0)
    second_ring_far(0)
    second_ring_near(0)
    second_ring_far(1)
    second_ring_close(0)
    second_ring_near(1)
    own_part(1)
    second_ring_close(1)
    swap_ohat.wait_recv()
    lax.fori_loop(0, 2, own_adjoint, 0)

    steps = [
        ([], (0, 1), (0, 0), (0, 0)),
        ([(misfit_parts,), (gather_1, 0)], (0, 0), (0, 0), (1, 2)),
        ([(gather_1, 1)], (1, 0), (0, 0), (1, 2)),
        ([(gather_lane, 0, 0), (misfit_sums,)], (0, 0), (1, 2), (0, 0)),
        ([(gather_lane, 1, 0)], (1, 0), (1, 2), (0, 0)),
        ([(gather_lane, 0, 1)], (0, 0), (1, 2), (1, 0)),
        ([(gather_2, 0), (gather_lane, 0, 3)], (0, 0), (1, 2), (3, 0)),
        ([(gather_2, 1)], (0, 1), (0, 0), (2, 0)),
        ([(gather_lane, 1, 1)], (1, 0), (1, 2), (1, 0)),
        ([(gather_lane, 1, 3)], (1, 0), (1, 2), (3, 0)),
        ([(gather_end, 0)], (0, 1), (2, 0), (0, 0)),
        ([(gather_lane, 0, 2)], (0, 0), (1, 2), (2, 0)),
        ([(gather_lane, 1, 2)], (1, 0), (1, 2), (2, 0)),
        ([(gather_end, 1)], (0, 1), (2, 0), (1, 0)),
        ([(gather_end, 3)], (0, 1), (2, 0), (3, 0)),
    ]

    def gather_step(i, carry):
        for n, step in enumerate(steps):
            if step[0]:
                @pl.when(i == n)
                def _(actions=tuple(step[0])):
                    for action in actions:
                        action[0](*action[1:])

        slots = []
        for u in range(4):
            t, o, r = (
                choose(i, [step[part][0] + u // 2 * step[part][1] for step in steps]) for part in (1, 2, 3)
            )
            slots.append(slot_of(t, u % 2, o, r))
        return back(slots, carry, pl.ds(0, 2 * points), 2 * points)

    gsum[...] = lax.fori_loop(0, len(steps), gather_step, gsum[...])

    gather_end(2)
    last = [slot_of(t, h, 2, 2) for t in range(stages) for h in range(2)]
    scale = f32(1.0 / (block * math.sqrt(slot_count)))

    def finish(where):
        parts = back(last, gsum[:, where], where, points)
        return jnp.sum(parts, axis=0, keepdims=True) * scale

    gsend[...] = jnp.broadcast_to(finish(other_points), gsend.shape)
    swap_sum = remote(gsend, grecv, core_send.at[5], core_recv.at[5], other)
    swap_sum.start()
    own_lines = finish(own_points)
    misfit_end()
    row_ids = lax.broadcasted_iota(jnp.int32, (2, points), 0)
    swap_sum.wait_recv()
    gradient_out[...] = jnp.where(
        row_ids == c, jnp.broadcast_to(own_lines, (2, points)), grecv[:2]
    )

    swap_psd.wait_send()
    wait_all(gbuf.at[:, :, :, other_points], 2, green_send.at[0])
    swap_ohat.wait_send()
    swap_mis.wait_send()
    swap_sum.wait_send()
    wait_all(mis_freq, freq_devices - 1, z_send.at[0])
    wait_all(send1, 24 * stages, one_send.at[0])
    wait_all(send_a, 4 * stages, a_send.at[0])
    wait_all(send_b, 4 * stages, b_send.at[0])
    wait_all(abuf, 30 * stages, g_send.at[0])


def hand_on(gradient, misfit, gradient_out, misfit_out):
    gradient_out[...] = gradient[...]
    misfit_out[...] = misfit[...]


def local(green_spectra, source_psd, pair_list, owner_map, observed):
    freq_devices = lax.axis_size("freq")
    planes, freq_dev, stations, points = green_spectra.shape
    pair_dev, block, unused_cols, lags = observed.shape
    slot_count = owner_map.shape[0]
    blocks = stations // block
    freq_total = freq_dev * freq_devices
    table = jnp.asarray(phase_table(freq_total, lags, freq_devices))
    rows = table.shape[1]
    units = stages * 2 * 2
    dma = pltpu.SemaphoreType.DMA
    vmem = pl.BlockSpec(memory_space=pltpu.VMEM)
    hbm = pl.BlockSpec(memory_space=pltpu.HBM)
    pair = (2, block, block)
    gradient, misfit = pl.pallas_call(
        functools.partial(kernel, freq_devices),
        out_shape=(
            jax.ShapeDtypeStruct((freq_dev, points), f32),
            jax.ShapeDtypeStruct((pair_dev, block // freq_devices), f32),
        ),
        in_specs=[hbm] * 6,
        out_specs=(vmem, vmem),
        scratch_shapes=[
            pltpu.VMEM((2, blocks, block, 2 * points), bf16),
            pltpu.VMEM((2, blocks, block, 2 * points), bf16),
            pltpu.VMEM((freq_dev, points), f32),
            pltpu.VMEM((freq_dev, points), f32),
            pltpu.VMEM((1, slot_count), jnp.int32),
            pltpu.VMEM((2, slot_count), jnp.int32),
            pltpu.VMEM((8, 128), jnp.int32),
            pltpu.SMEM((8, 128), jnp.int32),
            pltpu.VMEM((pair_dev, block, block, lags), bf16),
            pltpu.VMEM((rows, lags), bf16),
            pltpu.VMEM((rows, group * lags), bf16),
            pltpu.VMEM((2 * pair_dev,) + pair, f32),
            pltpu.VMEM((pair_dev,) + pair, f32),
            pltpu.VMEM((pair_dev * (block // freq_devices), lags), f32),
            pltpu.VMEM((24 * stages,) + pair, bf16),
            pltpu.VMEM((24 * stages + 1,) + pair, bf16),
            pltpu.VMEM((units, block, block), bf16),
            pltpu.VMEM((units, block, block), bf16),
            pltpu.VMEM((units,) + pair, bf16),
            pltpu.VMEM((units,) + pair, bf16),
            pltpu.VMEM((units, block, block), f32),
            pltpu.VMEM((2 * stages,) + pair, f32),
            pltpu.VMEM((slot_count,) + pair, bf16),
            pltpu.VMEM((2 * stages, block, block), f32),
            pltpu.VMEM((8, block), f32),
            pltpu.VMEM((8, block), f32),
            pltpu.VMEM((8, block), f32),
            pltpu.VMEM((freq_devices - 1, 8, block), f32),
            pltpu.VMEM((8, 2 * points), f32),
            pltpu.VMEM((8, points), f32),
            pltpu.VMEM((8, points), f32),
            dma((8,)),
            dma((6,)),
            dma((6,)),
            dma((1,)),
            dma((4,)),
            dma((1,)),
            dma((6 * stages,)),
            dma((1,)),
            dma((stages,)),
            dma((1,)),
            dma((stages,)),
            dma((1,)),
            dma((stages,)),
            dma((stages,)),
            dma((4 * stages,)),
            dma((4,)),
            dma((1,)),
            dma((1,)),
            pltpu.SemaphoreType.REGULAR,
            pltpu.SemaphoreType.REGULAR,
        ],
        compiler_params=pltpu.CompilerParams(
            collective_id=0, has_side_effects=True, vmem_limit_bytes=60 * 1024 * 1024
        ),
        cost_estimate=pl.CostEstimate(
            flops=8 * slot_count * freq_dev * 2 * block * block * points,
            bytes_accessed=12 * 1024 * 1024,
            transcendentals=0,
        ),
        name="misfit_gradient",
    )(
        owner_map.reshape(1, slot_count),
        pair_list.T,
        source_psd,
        table,
        green_spectra.reshape(planes, freq_dev, blocks, block, points),
        observed,
    )
    return pl.pallas_call(
        hand_on,
        out_shape=(
            jax.ShapeDtypeStruct(gradient.shape, f32),
            jax.ShapeDtypeStruct(misfit.shape, f32),
        ),
        in_specs=[vmem, vmem],
        out_specs=(vmem, vmem),
        name="hand_on",
    )(gradient, misfit)


def solution(mesh):
    in_specs = (
        P(None, "freq", None, "grid"),
        P("freq", "grid"),
        P(),
        P(),
        P("grid", None, None, None),
    )
    out_specs = (P("freq", "grid"), P("grid", "freq"))
    return jax.shard_map(local, mesh=mesh, in_specs=in_specs, out_specs=out_specs, check_vma=False)
```

```python
import functools
import math

import jax
import jax.numpy as jnp
import ml_dtypes
import numpy as np
from jax import lax
from jax.experimental import pallas as pl
from jax.experimental.pallas import tpu as pltpu
from jax.sharding import PartitionSpec as P

harmonic_step = 3
side = 4
stages = 2
pieces = 3
group = 8
MESH = pl.DeviceIdType.MESH
f32 = jnp.float32
bf16 = jnp.bfloat16


def phase_table(freq_total, lag_count, freq_devices):
    freq_ids = np.arange(freq_total)[:, None]
    turns = harmonic_step * (freq_ids + 1) * np.arange(lag_count)[None, :] % lag_count
    angles = turns * (2.0 * math.pi / lag_count)
    exact = np.stack((np.cos(angles), -np.sin(angles)), axis=1)
    parts = []
    for unused in range(pieces):
        part = exact.astype(ml_dtypes.bfloat16)
        parts.append(part)
        exact = exact - part.astype(np.float64)
    table = np.stack(parts).reshape(pieces, freq_devices, 2, 2, lag_count)
    both = np.stack((table, table[:, :, ::-1]), axis=2)
    both = both.transpose(1, 2, 0, 3, 4, 5).reshape(freq_devices * 2, pieces * 4, lag_count)
    return np.repeat(both, group, axis=1)


def kernel(
    freq_devices,
    owner,
    pairs,
    psd_hbm,
    table,
    green,
    observed,
    gradient_out,
    misfit_out,
    green_own,
    green_other,
    green_cross,
    weighted_own,
    weighted_other,
    cross_send,
    cross_recv,
    psd,
    psd_other,
    owner_row,
    pair_rows,
    ids_row,
    ids,
    obs,
    phi,
    spread,
    ohat,
    ohat_send,
    energy,
    send1,
    recv1,
    send_a,
    recv_a,
    send_b,
    recv_b,
    keep,
    own_sum,
    abuf,
    total,
    mis_own,
    mis_other,
    mis_pair,
    mis_freq,
    gsum,
    gsend,
    grecv,
    local_sem,
    core_send,
    core_recv,
    green_send,
    green_recv,
    one_send,
    one_recv,
    a_send,
    a_recv,
    b_send,
    b_recv,
    g_send,
    g1_recv,
    g1f_recv,
    g2_recv,
    g2f_recv,
    z_send,
    z_recv,
    z_here,
    near_here,
):
    z = lax.axis_index("freq")
    g = lax.axis_index("grid")
    c = g % 2
    x = (g // 2) % side
    y = g // (2 * side)
    other = g + 1 - 2 * c
    points = psd_hbm.shape[1]
    pair_dev, block, unused_cols, lags = observed.shape
    freq_total = 2 * freq_devices
    slot_count = 2 * side * side * pair_dev
    root_scale = 1.0 / math.sqrt(points * 2 * side * side)

    def neighbour(axis, d):
        step = 1 + 2 * d
        nx = (x + (1 - axis) * step) % side
        ny = (y + axis * step) % side
        return (ny * side + nx) * 2 + c

    def slot_of(t, h, o, r):
        sx = (x + (1 - h) * o + h * r) % side
        sy = (y + h * o + (1 - h) * r) % side
        return (sy * side + sx) * 4 + h * 2 + t

    def lane(d, j):
        return (1 - d) * (2 - 2 * j) + d * (1 + 2 * j)

    def lane_place(r):
        return ((r + 1) // 2 + 1) % 2

    def remote(src, dst, send, recv, device):
        return pltpu.make_async_remote_copy(
            src_ref=src, dst_ref=dst, send_sem=send, recv_sem=recv,
            device_id={"grid": device}, device_id_type=MESH,
        )

    def copy1(n):
        t, role, u = n // 24, (n % 24) // 8, n % 8
        h, d, j = u % 2, (u // 2) % 2, u // 4
        r = jnp.where(role == 1, lane(1 - d, j), lane(d, j))
        i = jnp.where(role == 0, t * 2 + j, 4 + t * 4 + r)
        return remote(send1.at[n], recv1.at[n], one_send.at[0], one_recv.at[i], neighbour(h, d))

    early_first = 24 + 4

    barrier = pltpu.get_barrier_semaphore()
    def distance(p):
        return jnp.minimum(p, side - p)

    lower = distance(x) + distance(y)
    pl.semaphore_signal(barrier, inc=1, device_id={"grid": other}, device_id_type=MESH)

    def greet(semaphore, upward):
        for axis, p in enumerate((x, y)):
            for d in range(2):
                q = (p + 1 + 2 * d) % side
                near, far = (distance(p), distance(q)) if upward else (distance(q), distance(p))

                @pl.when(near < far)
                def _():
                    pl.semaphore_signal(
                        semaphore, inc=1, device_id={"grid": neighbour(axis, d)}, device_id_type=MESH
                    )

    greet(barrier, True)
    for dz in range(1, freq_devices):

        @pl.when(z + dz < freq_devices)
        def _():
            pl.semaphore_signal(barrier, inc=1, device_id={"freq": z + dz}, device_id_type=MESH)

    load_owner = pltpu.make_async_copy(owner, owner_row, local_sem.at[4])
    load_pairs = pltpu.make_async_copy(pairs, pair_rows, local_sem.at[5])
    load_psd = pltpu.make_async_copy(psd_hbm, psd, local_sem.at[6])
    load_green = pltpu.make_async_copy(green.at[:, c], green_own, local_sem.at[0])
    load_cross = pltpu.make_async_copy(green.at[:, 1 - c], green_cross, local_sem.at[1])
    load_table = pltpu.make_async_copy(table.at[z * 2 + c], phi, local_sem.at[2])
    load_obs = pltpu.make_async_copy(observed, obs, local_sem.at[3])
    load_owner.start()
    load_pairs.start()
    load_psd.start()
    load_cross.start()
    load_green.start()
    load_table.start()
    pl.semaphore_wait(barrier, 1 + lower + z)

    swap_psd = remote(psd_hbm, psd_other, core_send.at[2], core_recv.at[2], other)
    parts = 4
    blocks = green.shape[2]

    def swap_green(n):
        k, some = n // parts, pl.ds(n % parts * (blocks // parts), blocks // parts)
        return remote(
            green.at[k, 1 - c, some], green_other.at[k, some], green_send.at[0], green_recv.at[n], other
        )

    swap_psd.start()
    for n in range(3):
        swap_green(n).start()

    greet(near_here, False)
    for dz in range(1, freq_devices):

        @pl.when(z >= dz)
        def _():
            pl.semaphore_signal(z_here, inc=1, device_id={"freq": z - dz}, device_id_type=MESH)

    def weigh(k, first, count, source, result, row):
        def body(b, carry):
            for i in range(4):
                place = first + 4 * b + i
                result[k, place] = (source[k, place].astype(f32) * row).astype(bf16)
            return carry

        lax.fori_loop(0, count // 4, body, 0)

    def cross_parts(left, right):
        acc = lax.dot_general(left, right, (((1,), (1,)), ((), ())), preferred_element_type=f32)
        return acc[:block, :block] + acc[block:, block:], acc[block:, :block] - acc[:block, block:]

    load_owner.wait()
    load_pairs.wait()
    square = (slot_count, slot_count)
    across = lax.broadcasted_iota(jnp.int32, square, 1)
    along = lax.broadcasted_iota(jnp.int32, square, 0)

    def down(row):
        return jnp.sum(jnp.where(across == along, jnp.broadcast_to(row, square), 0), axis=1, keepdims=True)

    their_owner = jnp.broadcast_to(owner_row[...], square)
    my_owner = down(owner_row[...])
    earlier = (their_owner < my_owner) | ((their_owner == my_owner) & (across < along))
    ids_row[...] = jnp.zeros_like(ids_row)
    entry_slot = jnp.sum(jnp.where(earlier, 1, 0), axis=1, keepdims=True)
    hit = entry_slot == across
    for k in range(2):
        chosen = jnp.where(hit, down(pair_rows[pl.ds(k, 1), :]), 0)
        ids_row[pl.ds(k, 1), pl.ds(0, slot_count)] = jnp.sum(chosen, axis=0, keepdims=True)
    move_ids = pltpu.make_async_copy(ids_row, ids, local_sem.at[7])
    move_ids.start()

    early = [slot_of(1, u % 2, 2, lane(u // 2, 1)) for u in range(4)]
    load_psd.wait()
    cross_row = psd[pl.ds(1 - c, 1), :]
    load_cross.wait()
    move_ids.wait()
    for u, slot in enumerate(early):
        left = (green_cross[:, ids[0, slot]].astype(f32) * cross_row).astype(bf16)
        right = green_cross[:, ids[1, slot]]
        values = cross_parts(left.reshape(2 * block, points), right.reshape(2 * block, points))
        for k in range(2):
            cross_send[u, k] = values[k].astype(bf16)
    swap_cross = remote(cross_send, cross_recv, core_send.at[0], core_recv.at[0], other)
    swap_cross.start()
    for n in range(3, 2 * parts):
        swap_green(n).start()
    load_obs.start()

    own_row = psd[pl.ds(c, 1), :]
    load_green.wait()
    for k in range(2):
        weigh(k, 0, blocks, green_own, weighted_own, own_row)
    early_shares = [
        cross_parts(
            weighted_own[:, ids[0, slot]].reshape(2 * block, points),
            green_own[:, ids[1, slot]].reshape(2 * block, points),
        )
        for slot in early
    ]
    swap_cross.wait_recv()
    for u, values in enumerate(early_shares):
        for k in range(2):
            send1[early_first + u, k] = (values[k] + cross_recv[u, k].astype(f32)).astype(bf16)

    @pl.when(lower < side)
    def _():
        pl.semaphore_wait(near_here, side - lower)

    for u in range(4):
        copy1(early_first + u).start()

    load_table.wait()
    rows = phi.shape[0]
    row_in_group = lax.broadcasted_iota(jnp.int32, (rows, lags), 0) % group
    phi_values = phi[...].astype(f32)
    for i in range(group):
        spread[:, pl.ds(i * lags, lags)] = jnp.where(row_in_group == i, phi_values, 0.0).astype(bf16)

    recv1[48] = jnp.zeros_like(recv1[48])
    gsum[...] = jnp.zeros_like(gsum)
    mis_own[...] = jnp.zeros_like(mis_own)
    swap_psd.wait_recv()
    other_row = psd_other[pl.ds(c, 1), :]
    for n in range(2 * parts):
        swap_green(n).wait_recv()
        weigh(n // parts, n % parts * (blocks // parts), blocks // parts, green_other, weighted_other, other_row)

    def both(own, others, place):
        return jnp.concatenate((own[:, place], others[:, place]), axis=2).reshape(2 * block, 2 * points)

    def units(slots):
        return [
            cross_parts(
                both(weighted_own, weighted_other, ids[0, slot]),
                both(green_own, green_other, ids[1, slot]),
            )
            for slot in slots
        ]

    def wait_all(buffer, count, semaphore):
        some = buffer.at[pl.ds(0, count)]
        pltpu.make_async_copy(some, some, semaphore).wait()

    def wait1(i):
        wait_all(recv1, 4, one_recv.at[i])

    def choose(i, values):
        chosen = values[0]
        for n in range(1, len(values)):
            chosen = jnp.where(i >= n, values[n], chosen) if values[n] != values[n - 1] else chosen
        return chosen

    groups = [
        (0, 1, 1), (0, 0, 0), (0, 0, 1), (2, 1, 0), (0, 1, 0), (2, 1, 1),
        (1, 0, 1), (1, 0, 0), (2, 0, 1), (2, 0, 0), (1, 1, 0), (1, 1, 1),
    ]

    def first_ring(i, carry):
        part, t, j = (choose(i, [values[k] for values in groups]) for k in range(3))
        through = part == 1
        role = jnp.where(through, 2, part // 2)
        first = t * 24 + role * 8 + j * 4

        @pl.when(i == 6)
        def _():
            load_obs.wait()
            energies()

        @pl.when((i == 6) | (i > 9))
        def _():
            project(jnp.where(i == 6, 0, i - 9))

        @pl.when(through)
        def _():
            wait1(t * 2 + j)

        slots = []
        for u in range(4):
            h, d = u % 2, u // 2
            o = jnp.where(part == 0, 2, 1 + 2 * d)
            r = jnp.where(part == 2, lane(1 - d, j), lane(d, j))
            slots.append(slot_of(t, h, o, r))
        for u, values in enumerate(units(slots)):
            n = first + u
            with_n = jnp.where(through, n - 16, 48)
            for k in range(2):
                send1[n, k] = (values[k] + recv1[with_n, k].astype(f32)).astype(bf16)
        for u in range(4):
            copy1(first + u).start()
        return carry

    def arrival1(t, h, d, r):
        role = 2 - (r + d) % 2
        return t * 24 + role * 8 + lane_place(r) * 4 + d * 2 + h

    def line_sums(t, wanted):
        for r in sorted({r for h, r in wanted}):
            wait1(4 + t * 4 + r)
        sums = []
        for (h, r), values in zip(wanted, units([slot_of(t, h, 0, r) for h, r in wanted])):
            arrived = [recv1[arrival1(t, h, d, r)].astype(f32) for d in range(2)]
            sums.append([values[k] + (arrived[0][k] + arrived[1][k]) for k in range(2)])
        return sums

    def place(t, h, d):
        return (t * 2 + h) * 2 + d

    def copy_a(t, h, d):
        i = place(t, h, d)
        return remote(send_a.at[i], recv_a.at[i], a_send.at[0], a_recv.at[t], neighbour(1 - h, d))

    def copy_b(t, h, d, k):
        i = place(t, h, d)
        return remote(
            send_b.at[i, k], recv_b.at[i, k], b_send.at[0], b_recv.at[t], neighbour(1 - h, d)
        )

    def second_ring_far(t):
        for h, values in enumerate(line_sums(t, [(0, 2), (1, 2)])):
            for d in range(2):
                send_a[place(t, h, d)] = values[d].astype(bf16)
                copy_a(t, h, d).start()

    def second_ring_near(t):
        wanted = [(h, 1 + 2 * d) for d in range(2) for h in range(2)]
        for (h, r), values in zip(wanted, line_sums(t, wanted)):
            d = r // 2
            i = place(t, h, d)
            send_b[i, 1 - d] = values[1 - d].astype(bf16)
            copy_b(t, h, d, 1 - d).start()
            keep[i] = values[d]

    def own_part(t):
        for h, values in enumerate(line_sums(t, [(0, 0), (1, 0)])):
            for k in range(2):
                own_sum[t * 2 + h, k] = values[k]

    def second_ring_close(t):
        wait_all(recv_a, 4, a_recv.at[t])
        for d in range(2):
            for h in range(2):
                i = place(t, h, d)
                send_b[i, d] = (keep[i] + recv_a[i].astype(f32)).astype(bf16)
                copy_b(t, h, d, d).start()

    def copy_g1(t, h, d):
        s = slot_of(t, h, 0, 0)
        return remote(abuf.at[s], abuf.at[s], g_send.at[0], g1_recv.at[t], neighbour(1 - h, d))

    def copy_g1f(t, h, d):
        s = slot_of(t, h, 0, 3 - 2 * d)
        return remote(abuf.at[s, d], abuf.at[s, d], g_send.at[0], g1f_recv.at[t], neighbour(1 - h, d))

    def copy_g2(t, h, d, r):
        s = slot_of(t, h, 0, r)
        return remote(abuf.at[s], abuf.at[s], g_send.at[0], g2_recv.at[t * 4 + r], neighbour(h, d))

    def copy_g2f(t, h, d, j):
        r = lane(d, j)
        s = slot_of(t, h, 3 - 2 * d, r)
        return remote(abuf.at[s], abuf.at[s], g_send.at[0], g2f_recv.at[r], neighbour(h, d))

    ones = jnp.ones((8, block), f32)

    def lane_sum(values):
        return lax.dot_general(
            ones[:, : values.shape[1]], values, (((1,), (1,)), ((), ())),
            precision=lax.Precision.HIGHEST, preferred_element_type=f32,
        )

    def own_adjoint(t, carry):
        wait_all(recv_b, 4, b_recv.at[t])
        for h in range(2):
            s, q = slot_of(t, h, 0, 0), h * 2 + t
            kept = jnp.zeros((block, block), f32)
            for k in range(2):
                value = own_sum[t * 2 + h, k]
                for d in range(2):
                    value = value + recv_b[place(t, h, d), k].astype(f32)
                cross = value * f32(root_scale)
                seen = ohat[q, k]
                abuf[s, k] = (0.5 * cross - seen * f32(1.0 / lags)).astype(bf16)
                kept = kept + cross * (f32(lags / 2) * cross - 2.0 * seen)
            for d in range(2):
                copy_g1(t, h, d).start()
            for d in range(2):
                copy_g2(t, h, d, 0).start()
            total[q] = kept
        return carry

    def gather_1(t):
        wait_all(abuf, 4, g1_recv.at[t])

        def body(v, carry):
            h, d = v % 2, v // 2
            copy_g1f(t, h, d).start()
            for side_d in range(2):
                copy_g2(t, h, side_d, 3 - 2 * d).start()
            return carry

        lax.fori_loop(0, 4, body, 0)

    def gather_2(t):
        wait_all(abuf, 2, g1f_recv.at[t])
        for h in range(2):
            for d in range(2):
                copy_g2(t, h, d, 2).start()

    def gather_lane(t, r):
        wait_all(abuf, 4, g2_recv.at[t * 4 + r])
        for h in range(2):
            copy_g2f(t, h, r % 2, lane_place(r)).start()

    def gather_end(r):
        wait_all(abuf, 4, g2f_recv.at[r])

    def back(slots, carry, of_block, count):
        for s in slots:
            weights = abuf[s]
            top = jnp.concatenate((weights[0], -weights[1]), axis=1)
            low = jnp.concatenate((weights[1], weights[0]), axis=1)
            right = of_block(ids[1, s])
            moved = jnp.dot(
                jnp.concatenate((top, low), axis=0), right, preferred_element_type=f32
            )
            left = of_block(ids[0, s]).astype(f32)
            carry = carry + jnp.sum((moved * left).reshape(2 * block // 8, 8, count), axis=0)
        return carry

    def project(quarter):
        chunks = block // group // 4

        def body(i, carry):
            first = pl.multiple_of((quarter * chunks + i) * group, group)
            seen = jnp.concatenate(
                [
                    jnp.concatenate([obs[s, first + k] for k in range(group)], axis=1)
                    for s in range(pair_dev)
                ],
                axis=0,
            )
            out = lax.dot_general(
                spread[...], seen, (((1,), (1,)), ((), ())), preferred_element_type=f32
            )
            out = jnp.sum(out.reshape(pieces, 4 * group, pair_dev * block), axis=0)
            for s in range(pair_dev):
                for k in range(2):
                    cols = slice(s * block, (s + 1) * block)
                    ohat[2 * c + s, k, pl.ds(first, group), :] = out[k * group : (k + 1) * group, cols]
                    ohat_send[s, k, pl.ds(first, group), :] = out[(2 + k) * group : (3 + k) * group, cols]
            return carry

        lax.fori_loop(0, chunks, body, 0, unroll=2)

    swap_ohat = remote(
        ohat_send, ohat.at[pl.ds(2 * c, 2)], core_send.at[3], core_recv.at[3], other
    )
    part_rows = block // freq_devices

    def energies():
        def body(i, carry):
            for s in range(pair_dev):
                seen = obs[s, z * part_rows + i].astype(f32)
                energy[pl.ds(s * part_rows + i, 1), :] = jnp.sum(seen * seen, axis=0, keepdims=True)
            return carry

        lax.fori_loop(0, part_rows, body, 0)

    swap_mis = remote(mis_own, mis_other, core_send.at[4], core_recv.at[4], other)

    def copy_z(dz):
        return pltpu.make_async_remote_copy(
            src_ref=mis_pair, dst_ref=mis_freq.at[dz - 1],
            send_sem=z_send.at[0], recv_sem=z_recv.at[0],
            device_id={"freq": (z + dz) % freq_devices}, device_id_type=MESH,
        )

    def misfit_parts():
        for q in range(2 * stages):
            mis_own[pl.ds(q, 1), :] = lane_sum(total[q])[:1]
        swap_mis.start()

    def misfit_sums():
        swap_mis.wait_recv()
        mis_pair[...] = mis_own[...] + mis_other[...]

        @pl.when(z < freq_devices - 1)
        def _():
            pl.semaphore_wait(z_here, freq_devices - 1 - z)

        for dz in range(1, freq_devices):
            copy_z(dz).start()

    def misfit_end():
        wait_all(mis_freq, freq_devices - 1, z_recv.at[0])
        mine = mis_pair[...]
        for dz in range(1, freq_devices):
            mine = mine + mis_freq[dz - 1]
        from_observed = lane_sum(energy[...])[:1]
        picked = jnp.zeros((mine.shape[0], part_rows), f32)
        for part in range(freq_devices):
            picked = jnp.where(z == part, mine[:, part * part_rows : (part + 1) * part_rows], picked)
        for s in range(pair_dev):
            row = jnp.where(c == 0, picked[s : s + 1], picked[2 + s : 3 + s])
            row = row + from_observed[:, s * part_rows : (s + 1) * part_rows]
            misfit_out[pl.ds(s, 1), :] = row * f32(1.0 / (2.0 * block * lags * freq_total))

    lax.fori_loop(1, 12, first_ring, 0)
    project(3)
    swap_ohat.start()
    own_part(0)
    second_ring_far(0)
    second_ring_near(0)
    second_ring_far(1)
    second_ring_close(0)
    second_ring_near(1)
    own_part(1)
    second_ring_close(1)
    swap_ohat.wait_recv()
    lax.fori_loop(0, 2, own_adjoint, 0)

    steps = [
        ([], (0, 1), (0, 0), (0, 0)),
        ([(misfit_parts,), (gather_1, 0)], (0, 0), (0, 0), (1, 2)),
        ([(gather_1, 1)], (1, 0), (0, 0), (1, 2)),
        ([(gather_lane, 0, 0), (misfit_sums,)], (0, 0), (1, 2), (0, 0)),
        ([(gather_lane, 1, 0)], (1, 0), (1, 2), (0, 0)),
        ([(gather_lane, 0, 1)], (0, 0), (1, 2), (1, 0)),
        ([(gather_2, 0), (gather_lane, 0, 3)], (0, 0), (1, 2), (3, 0)),
        ([(gather_2, 1)], (0, 1), (0, 0), (2, 0)),
        ([(gather_lane, 1, 1)], (1, 0), (1, 2), (1, 0)),
        ([(gather_lane, 1, 3)], (1, 0), (1, 2), (3, 0)),
        ([(gather_end, 0)], (0, 1), (2, 0), (0, 0)),
        ([(gather_lane, 0, 2)], (0, 0), (1, 2), (2, 0)),
        ([(gather_lane, 1, 2)], (1, 0), (1, 2), (2, 0)),
        ([(gather_end, 1)], (0, 1), (2, 0), (1, 0)),
        ([(gather_end, 3)], (0, 1), (2, 0), (3, 0)),
    ]

    def gather_step(i, carry):
        for n, step in enumerate(steps):
            if step[0]:
                @pl.when(i == n)
                def _(actions=tuple(step[0])):
                    for action in actions:
                        action[0](*action[1:])

        slots = []
        for u in range(4):
            t, o, r = (
                choose(i, [step[part][0] + u // 2 * step[part][1] for step in steps]) for part in (1, 2, 3)
            )
            slots.append(slot_of(t, u % 2, o, r))
        return back(slots, carry, lambda place: both(green_own, green_other, place), 2 * points)

    gsum[...] = lax.fori_loop(0, len(steps), gather_step, gsum[...])

    gather_end(2)
    last = [slot_of(t, h, 2, 2) for t in range(stages) for h in range(2)]
    scale = f32(1.0 / (block * math.sqrt(slot_count)))

    def finish(buffer, first):
        sums = gsum[:, first : first + points]
        sums = back(last, sums, lambda place: buffer[:, place].reshape(2 * block, points), points)
        return jnp.sum(sums, axis=0, keepdims=True) * scale

    gsend[...] = jnp.broadcast_to(finish(green_other, points), gsend.shape)
    swap_sum = remote(gsend, grecv, core_send.at[5], core_recv.at[5], other)
    swap_sum.start()
    own_lines = finish(green_own, 0)
    misfit_end()
    row_ids = lax.broadcasted_iota(jnp.int32, (2, points), 0)
    swap_sum.wait_recv()
    gradient_out[...] = jnp.where(
        row_ids == c, jnp.broadcast_to(own_lines, (2, points)), grecv[:2]
    )

    swap_psd.wait_send()
    wait_all(green_other, 2, green_send.at[0])
    swap_cross.wait_send()
    swap_ohat.wait_send()
    swap_mis.wait_send()
    swap_sum.wait_send()
    wait_all(mis_freq, freq_devices - 1, z_send.at[0])
    wait_all(send1, 24 * stages, one_send.at[0])
    wait_all(send_a, 4 * stages, a_send.at[0])
    wait_all(send_b, 4 * stages, b_send.at[0])
    wait_all(abuf, 30 * stages, g_send.at[0])


def hand_on(gradient, misfit, gradient_out, misfit_out):
    gradient_out[...] = gradient[...]
    misfit_out[...] = misfit[...]


def local(green_spectra, source_psd, pair_list, owner_map, observed):
    freq_devices = lax.axis_size("freq")
    planes, freq_dev, stations, points = green_spectra.shape
    pair_dev, block, unused_cols, lags = observed.shape
    slot_count = owner_map.shape[0]
    blocks = stations // block
    freq_total = freq_dev * freq_devices
    table = jnp.asarray(phase_table(freq_total, lags, freq_devices))
    rows = table.shape[1]
    units = stages * 2 * 2
    dma = pltpu.SemaphoreType.DMA
    vmem = pl.BlockSpec(memory_space=pltpu.VMEM)
    hbm = pl.BlockSpec(memory_space=pltpu.HBM)
    pair = (2, block, block)
    gradient, misfit = pl.pallas_call(
        functools.partial(kernel, freq_devices),
        out_shape=(
            jax.ShapeDtypeStruct((freq_dev, points), f32),
            jax.ShapeDtypeStruct((pair_dev, block // freq_devices), f32),
        ),
        in_specs=[hbm] * 6,
        out_specs=(vmem, vmem),
        scratch_shapes=[
            pltpu.VMEM((2, blocks, block, points), bf16),
            pltpu.VMEM((2, blocks, block, points), bf16),
            pltpu.VMEM((2, blocks, block, points), bf16),
            pltpu.VMEM((2, blocks, block, points), bf16),
            pltpu.VMEM((2, blocks, block, points), bf16),
            pltpu.VMEM((4,) + pair, bf16),
            pltpu.VMEM((4,) + pair, bf16),
            pltpu.VMEM((freq_dev, points), f32),
            pltpu.VMEM((freq_dev, points), f32),
            pltpu.VMEM((1, slot_count), jnp.int32),
            pltpu.VMEM((2, slot_count), jnp.int32),
            pltpu.VMEM((8, 128), jnp.int32),
            pltpu.SMEM((8, 128), jnp.int32),
            pltpu.VMEM((pair_dev, block, block, lags), bf16),
            pltpu.VMEM((rows, lags), bf16),
            pltpu.VMEM((rows, group * lags), bf16),
            pltpu.VMEM((2 * pair_dev,) + pair, f32),
            pltpu.VMEM((pair_dev,) + pair, f32),
            pltpu.VMEM((pair_dev * (block // freq_devices), lags), f32),
            pltpu.VMEM((24 * stages,) + pair, bf16),
            pltpu.VMEM((24 * stages + 1,) + pair, bf16),
            pltpu.VMEM((units, block, block), bf16),
            pltpu.VMEM((units, block, block), bf16),
            pltpu.VMEM((units,) + pair, bf16),
            pltpu.VMEM((units,) + pair, bf16),
            pltpu.VMEM((units, block, block), f32),
            pltpu.VMEM((2 * stages,) + pair, f32),
            pltpu.VMEM((slot_count,) + pair, bf16),
            pltpu.VMEM((2 * stages, block, block), f32),
            pltpu.VMEM((8, block), f32),
            pltpu.VMEM((8, block), f32),
            pltpu.VMEM((8, block), f32),
            pltpu.VMEM((freq_devices - 1, 8, block), f32),
            pltpu.VMEM((8, 2 * points), f32),
            pltpu.VMEM((8, points), f32),
            pltpu.VMEM((8, points), f32),
            dma((8,)),
            dma((6,)),
            dma((6,)),
            dma((1,)),
            dma((8,)),
            dma((1,)),
            dma((6 * stages,)),
            dma((1,)),
            dma((stages,)),
            dma((1,)),
            dma((stages,)),
            dma((1,)),
            dma((stages,)),
            dma((stages,)),
            dma((4 * stages,)),
            dma((4,)),
            dma((1,)),
            dma((1,)),
            pltpu.SemaphoreType.REGULAR,
            pltpu.SemaphoreType.REGULAR,
        ],
        compiler_params=pltpu.CompilerParams(
            collective_id=0, has_side_effects=True, vmem_limit_bytes=60 * 1024 * 1024
        ),
        cost_estimate=pl.CostEstimate(
            flops=8 * slot_count * freq_dev * 2 * block * block * points,
            bytes_accessed=12 * 1024 * 1024,
            transcendentals=0,
        ),
        name="misfit_gradient",
    )(
        owner_map.reshape(1, slot_count),
        pair_list.T,
        source_psd,
        table,
        green_spectra.reshape(planes, freq_dev, blocks, block, points),
        observed,
    )
    return pl.pallas_call(
        hand_on,
        out_shape=(
            jax.ShapeDtypeStruct(gradient.shape, f32),
            jax.ShapeDtypeStruct(misfit.shape, f32),
        ),
        in_specs=[vmem, vmem],
        out_specs=(vmem, vmem),
        name="hand_on",
    )(gradient, misfit)


def solution(mesh):
    in_specs = (
        P(None, "freq", None, "grid"),
        P("freq", "grid"),
        P(),
        P(),
        P("grid", None, None, None),
    )
    out_specs = (P("freq", "grid"), P("grid", "freq"))
    return jax.shard_map(local, mesh=mesh, in_specs=in_specs, out_specs=out_specs, check_vma=False)
```

```python
import functools
import math

import jax
import jax.numpy as jnp
import ml_dtypes
import numpy as np
from jax import lax
from jax.experimental import pallas as pl
from jax.experimental.pallas import tpu as pltpu
from jax.sharding import PartitionSpec as P

harmonic_step = 3
side = 4
stages = 2
pieces = 3
group = 8
MESH = pl.DeviceIdType.MESH
f32 = jnp.float32
bf16 = jnp.bfloat16


def phase_table(freq_total, lag_count, freq_devices):
    freq_ids = np.arange(freq_total)[:, None]
    turns = harmonic_step * (freq_ids + 1) * np.arange(lag_count)[None, :] % lag_count
    angles = turns * (2.0 * math.pi / lag_count)
    exact = np.stack((np.cos(angles), -np.sin(angles)), axis=1)
    parts = []
    for unused in range(pieces):
        part = exact.astype(ml_dtypes.bfloat16)
        parts.append(part)
        exact = exact - part.astype(np.float64)
    table = np.stack(parts).reshape(pieces, freq_devices, 2, 2, lag_count)
    both = np.stack((table, table[:, :, ::-1]), axis=2)
    both = both.transpose(1, 2, 0, 3, 4, 5).reshape(freq_devices * 2, pieces * 4, lag_count)
    return np.repeat(both, group, axis=1)


def kernel(
    freq_devices,
    owner,
    pairs,
    psd_hbm,
    table,
    green,
    observed,
    gradient_out,
    misfit_out,
    green_own,
    green_other,
    green_cross,
    weighted_own,
    weighted_other,
    cross_send,
    cross_recv,
    psd,
    psd_other,
    owner_row,
    pair_rows,
    ids_row,
    ids,
    obs,
    phi,
    spread,
    ohat,
    ohat_send,
    energy,
    send1,
    recv1,
    send_a,
    recv_a,
    send_b,
    recv_b,
    keep,
    own_sum,
    abuf,
    total,
    mis_own,
    mis_other,
    mis_pair,
    mis_freq,
    gsum,
    gsend,
    grecv,
    local_sem,
    core_send,
    core_recv,
    green_send,
    green_recv,
    one_send,
    one_recv,
    a_send,
    a_recv,
    b_send,
    b_recv,
    g_send,
    g1_recv,
    g1f_recv,
    g2_recv,
    g2f_recv,
    z_send,
    z_recv,
    z_here,
    near_here,
):
    z = lax.axis_index("freq")
    g = lax.axis_index("grid")
    c = g % 2
    x = (g // 2) % side
    y = g // (2 * side)
    other = g + 1 - 2 * c
    points = psd_hbm.shape[1]
    pair_dev, block, unused_cols, lags = observed.shape
    freq_total = 2 * freq_devices
    slot_count = 2 * side * side * pair_dev
    root_scale = 1.0 / math.sqrt(points * 2 * side * side)

    def neighbour(axis, d):
        step = 1 + 2 * d
        nx = (x + (1 - axis) * step) % side
        ny = (y + axis * step) % side
        return (ny * side + nx) * 2 + c

    def slot_of(t, h, o, r):
        sx = (x + (1 - h) * o + h * r) % side
        sy = (y + h * o + (1 - h) * r) % side
        return (sy * side + sx) * 4 + h * 2 + t

    def lane(d, j):
        return (1 - d) * (2 - 2 * j) + d * (1 + 2 * j)

    def lane_place(r):
        return ((r + 1) // 2 + 1) % 2

    def remote(src, dst, send, recv, device):
        return pltpu.make_async_remote_copy(
            src_ref=src, dst_ref=dst, send_sem=send, recv_sem=recv,
            device_id={"grid": device}, device_id_type=MESH,
        )

    def copy1(n):
        t, role, u = n // 24, (n % 24) // 8, n % 8
        h, d, j = u % 2, (u // 2) % 2, u // 4
        r = jnp.where(role == 1, lane(1 - d, j), lane(d, j))
        i = jnp.where(role == 0, t * 2 + j, 4 + t * 4 + r)
        return remote(send1.at[n], recv1.at[n], one_send.at[0], one_recv.at[i], neighbour(h, d))

    early = [(1, 1), (0, 0)]

    barrier = pltpu.get_barrier_semaphore()
    def distance(p):
        return jnp.minimum(p, side - p)

    lower = distance(x) + distance(y)
    pl.semaphore_signal(barrier, inc=1, device_id={"grid": other}, device_id_type=MESH)

    def greet(semaphore, upward):
        for axis, p in enumerate((x, y)):
            for d in range(2):
                q = (p + 1 + 2 * d) % side
                near, far = (distance(p), distance(q)) if upward else (distance(q), distance(p))

                @pl.when(near < far)
                def _():
                    pl.semaphore_signal(
                        semaphore, inc=1, device_id={"grid": neighbour(axis, d)}, device_id_type=MESH
                    )

    greet(barrier, True)
    for dz in range(1, freq_devices):

        @pl.when(z + dz < freq_devices)
        def _():
            pl.semaphore_signal(barrier, inc=1, device_id={"freq": z + dz}, device_id_type=MESH)

    load_owner = pltpu.make_async_copy(owner, owner_row, local_sem.at[4])
    load_pairs = pltpu.make_async_copy(pairs, pair_rows, local_sem.at[5])
    load_psd = pltpu.make_async_copy(psd_hbm, psd, local_sem.at[6])
    load_green = pltpu.make_async_copy(green.at[:, c], green_own, local_sem.at[0])
    load_cross = pltpu.make_async_copy(green.at[:, 1 - c], green_cross, local_sem.at[1])
    load_table = pltpu.make_async_copy(table.at[z * 2 + c], phi, local_sem.at[2])
    load_obs = pltpu.make_async_copy(observed, obs, local_sem.at[3])
    load_owner.start()
    load_pairs.start()
    load_psd.start()
    load_cross.start()
    load_green.start()
    load_table.start()
    pl.semaphore_wait(barrier, 1 + lower + z)

    swap_psd = remote(psd_hbm, psd_other, core_send.at[2], core_recv.at[2], other)
    parts = 4
    blocks = green.shape[2]

    def swap_green(n):
        k, some = n // parts, pl.ds(n % parts * (blocks // parts), blocks // parts)
        return remote(
            green.at[k, 1 - c, some], green_other.at[k, some], green_send.at[0], green_recv.at[n], other
        )

    swap_psd.start()
    for n in range(3):
        swap_green(n).start()

    greet(near_here, False)
    for dz in range(1, freq_devices):

        @pl.when(z >= dz)
        def _():
            pl.semaphore_signal(z_here, inc=1, device_id={"freq": z - dz}, device_id_type=MESH)

    def weigh(k, first, count, source, result, row):
        def body(b, carry):
            for i in range(4):
                place = first + 4 * b + i
                result[k, place] = (source[k, place].astype(f32) * row).astype(bf16)
            return carry

        lax.fori_loop(0, count // 4, body, 0)

    def cross_parts(left, right):
        acc = lax.dot_general(left, right, (((1,), (1,)), ((), ())), preferred_element_type=f32)
        return acc[:block, :block] + acc[block:, block:], acc[block:, :block] - acc[:block, block:]

    load_owner.wait()
    load_pairs.wait()
    square = (slot_count, slot_count)
    across = lax.broadcasted_iota(jnp.int32, square, 1)
    along = lax.broadcasted_iota(jnp.int32, square, 0)

    def down(row):
        return jnp.sum(jnp.where(across == along, jnp.broadcast_to(row, square), 0), axis=1, keepdims=True)

    their_owner = jnp.broadcast_to(owner_row[...], square)
    my_owner = down(owner_row[...])
    earlier = (their_owner < my_owner) | ((their_owner == my_owner) & (across < along))
    ids_row[...] = jnp.zeros_like(ids_row)
    entry_slot = jnp.sum(jnp.where(earlier, 1, 0), axis=1, keepdims=True)
    hit = entry_slot == across
    for k in range(2):
        chosen = jnp.where(hit, down(pair_rows[pl.ds(k, 1), :]), 0)
        ids_row[pl.ds(k, 1), pl.ds(0, slot_count)] = jnp.sum(chosen, axis=0, keepdims=True)
    move_ids = pltpu.make_async_copy(ids_row, ids, local_sem.at[7])
    move_ids.start()

    def early_slots(t, j):
        return [slot_of(t, u % 2, 2, lane(u // 2, j)) for u in range(4)]

    def swap_cross(e):
        some = pl.ds(4 * e, 4)
        return remote(
            cross_send.at[some], cross_recv.at[some], core_send.at[e], core_recv.at[e], other
        )

    load_psd.wait()
    cross_row = psd[pl.ds(1 - c, 1), :]
    load_cross.wait()
    move_ids.wait()
    for e, (t, j) in enumerate(early):
        for u, slot in enumerate(early_slots(t, j)):
            left = (green_cross[:, ids[0, slot]].astype(f32) * cross_row).astype(bf16)
            right = green_cross[:, ids[1, slot]]
            values = cross_parts(left.reshape(2 * block, points), right.reshape(2 * block, points))
            for k in range(2):
                cross_send[4 * e + u, k] = values[k].astype(bf16)
        swap_cross(e).start()
        if e == 0:
            swap_green(3).start()
    for n in range(4, 2 * parts):
        swap_green(n).start()
    load_obs.start()

    own_row = psd[pl.ds(c, 1), :]
    load_green.wait()
    for k in range(2):
        weigh(k, 0, blocks, green_own, weighted_own, own_row)
    for e, (t, j) in enumerate(early):
        shares = [
            cross_parts(
                weighted_own[:, ids[0, slot]].reshape(2 * block, points),
                green_own[:, ids[1, slot]].reshape(2 * block, points),
            )
            for slot in early_slots(t, j)
        ]
        swap_cross(e).wait_recv()
        first = t * 24 + j * 4
        for u, values in enumerate(shares):
            for k in range(2):
                send1[first + u, k] = (values[k] + cross_recv[4 * e + u, k].astype(f32)).astype(bf16)
        if e == 0:

            @pl.when(lower < side)
            def _():
                pl.semaphore_wait(near_here, side - lower)

        for u in range(4):
            copy1(first + u).start()

    load_table.wait()
    rows = phi.shape[0]
    row_in_group = lax.broadcasted_iota(jnp.int32, (rows, lags), 0) % group
    phi_values = phi[...].astype(f32)
    for i in range(group):
        spread[:, pl.ds(i * lags, lags)] = jnp.where(row_in_group == i, phi_values, 0.0).astype(bf16)

    recv1[48] = jnp.zeros_like(recv1[48])
    gsum[...] = jnp.zeros_like(gsum)
    mis_own[...] = jnp.zeros_like(mis_own)
    swap_psd.wait_recv()
    other_row = psd_other[pl.ds(c, 1), :]
    for n in range(2 * parts):
        swap_green(n).wait_recv()
        weigh(n // parts, n % parts * (blocks // parts), blocks // parts, green_other, weighted_other, other_row)

    def both(own, others, place):
        return jnp.concatenate((own[:, place], others[:, place]), axis=2).reshape(2 * block, 2 * points)

    def units(slots):
        return [
            cross_parts(
                both(weighted_own, weighted_other, ids[0, slot]),
                both(green_own, green_other, ids[1, slot]),
            )
            for slot in slots
        ]

    def wait_all(buffer, count, semaphore):
        some = buffer.at[pl.ds(0, count)]
        pltpu.make_async_copy(some, some, semaphore).wait()

    def wait1(i):
        wait_all(recv1, 4, one_recv.at[i])

    def choose(i, values):
        chosen = values[0]
        for n in range(1, len(values)):
            chosen = jnp.where(i >= n, values[n], chosen) if values[n] != values[n - 1] else chosen
        return chosen

    groups = [
        (0, 1, 1), (0, 0, 0), (0, 0, 1), (0, 1, 0), (2, 0, 0), (2, 0, 1),
        (1, 0, 0), (1, 0, 1), (2, 1, 0), (2, 1, 1), (1, 1, 0), (1, 1, 1),
    ]

    def first_ring(i, carry):
        part, t, j = (choose(i, [values[k] for values in groups]) for k in range(3))
        through = part == 1
        role = jnp.where(through, 2, part // 2)
        first = t * 24 + role * 8 + j * 4

        @pl.when(i == 6)
        def _():
            load_obs.wait()
            energies()

        @pl.when((i == 6) | (i == 8) | (i == 10))
        def _():
            project(jnp.where(i == 6, 0, jnp.where(i == 8, 1, 2)))

        @pl.when(through)
        def _():
            wait1(t * 2 + j)

        slots = []
        for u in range(4):
            h, d = u % 2, u // 2
            o = jnp.where(part == 0, 2, 1 + 2 * d)
            r = jnp.where(part == 2, lane(1 - d, j), lane(d, j))
            slots.append(slot_of(t, h, o, r))
        for u, values in enumerate(units(slots)):
            n = first + u
            with_n = jnp.where(through, n - 16, 48)
            for k in range(2):
                send1[n, k] = (values[k] + recv1[with_n, k].astype(f32)).astype(bf16)
        for u in range(4):
            copy1(first + u).start()
        return carry

    def arrival1(t, h, d, r):
        role = 2 - (r + d) % 2
        return t * 24 + role * 8 + lane_place(r) * 4 + d * 2 + h

    def line_sums(t, wanted):
        for r in sorted({r for h, r in wanted}):
            wait1(4 + t * 4 + r)
        sums = []
        for (h, r), values in zip(wanted, units([slot_of(t, h, 0, r) for h, r in wanted])):
            arrived = [recv1[arrival1(t, h, d, r)].astype(f32) for d in range(2)]
            sums.append([values[k] + (arrived[0][k] + arrived[1][k]) for k in range(2)])
        return sums

    def place(t, h, d):
        return (t * 2 + h) * 2 + d

    def copy_a(t, h, d):
        i = place(t, h, d)
        return remote(send_a.at[i], recv_a.at[i], a_send.at[0], a_recv.at[t], neighbour(1 - h, d))

    def copy_b(t, h, d, k):
        i = place(t, h, d)
        return remote(
            send_b.at[i, k], recv_b.at[i, k], b_send.at[0], b_recv.at[t], neighbour(1 - h, d)
        )

    def second_ring_far(t):
        for h, values in enumerate(line_sums(t, [(0, 2), (1, 2)])):
            for d in range(2):
                send_a[place(t, h, d)] = values[d].astype(bf16)
                copy_a(t, h, d).start()

    def second_ring_near(t):
        wanted = [(h, 1 + 2 * d) for d in range(2) for h in range(2)]
        for (h, r), values in zip(wanted, line_sums(t, wanted)):
            d = r // 2
            i = place(t, h, d)
            send_b[i, 1 - d] = values[1 - d].astype(bf16)
            copy_b(t, h, d, 1 - d).start()
            keep[i] = values[d]

    def own_part(t):
        for h, values in enumerate(line_sums(t, [(0, 0), (1, 0)])):
            for k in range(2):
                own_sum[t * 2 + h, k] = values[k]

    def second_ring_close(t):
        wait_all(recv_a, 4, a_recv.at[t])
        for d in range(2):
            for h in range(2):
                i = place(t, h, d)
                send_b[i, d] = (keep[i] + recv_a[i].astype(f32)).astype(bf16)
                copy_b(t, h, d, d).start()

    def copy_g1(t, h, d):
        s = slot_of(t, h, 0, 0)
        return remote(abuf.at[s], abuf.at[s], g_send.at[0], g1_recv.at[t], neighbour(1 - h, d))

    def copy_g1f(t, h, d):
        s = slot_of(t, h, 0, 3 - 2 * d)
        return remote(abuf.at[s, d], abuf.at[s, d], g_send.at[0], g1f_recv.at[t], neighbour(1 - h, d))

    def copy_g2(t, h, d, r):
        s = slot_of(t, h, 0, r)
        return remote(abuf.at[s], abuf.at[s], g_send.at[0], g2_recv.at[t * 4 + r], neighbour(h, d))

    def copy_g2f(t, h, d, j):
        r = lane(d, j)
        s = slot_of(t, h, 3 - 2 * d, r)
        return remote(abuf.at[s], abuf.at[s], g_send.at[0], g2f_recv.at[r], neighbour(h, d))

    ones = jnp.ones((8, block), f32)

    def lane_sum(values):
        return lax.dot_general(
            ones[:, : values.shape[1]], values, (((1,), (1,)), ((), ())),
            precision=lax.Precision.HIGHEST, preferred_element_type=f32,
        )

    def own_adjoint(t, carry):
        wait_all(recv_b, 4, b_recv.at[t])
        for h in range(2):
            s, q = slot_of(t, h, 0, 0), h * 2 + t
            kept = jnp.zeros((block, block), f32)
            for k in range(2):
                value = own_sum[t * 2 + h, k]
                for d in range(2):
                    value = value + recv_b[place(t, h, d), k].astype(f32)
                cross = value * f32(root_scale)
                seen = ohat[q, k]
                abuf[s, k] = (0.5 * cross - seen * f32(1.0 / lags)).astype(bf16)
                kept = kept + cross * (f32(lags / 2) * cross - 2.0 * seen)
            for d in range(2):
                copy_g1(t, h, d).start()
            for d in range(2):
                copy_g2(t, h, d, 0).start()
            total[q] = kept
        return carry

    def gather_1(t):
        wait_all(abuf, 4, g1_recv.at[t])

        def body(v, carry):
            h, d = v % 2, v // 2
            copy_g1f(t, h, d).start()
            for side_d in range(2):
                copy_g2(t, h, side_d, 3 - 2 * d).start()
            return carry

        lax.fori_loop(0, 4, body, 0)

    def gather_2(t):
        wait_all(abuf, 2, g1f_recv.at[t])
        for h in range(2):
            for d in range(2):
                copy_g2(t, h, d, 2).start()

    def gather_lane(t, r):
        wait_all(abuf, 4, g2_recv.at[t * 4 + r])
        for h in range(2):
            copy_g2f(t, h, r % 2, lane_place(r)).start()

    def gather_end(r):
        wait_all(abuf, 4, g2f_recv.at[r])

    def back(slots, carry, of_block, count):
        for s in slots:
            weights = abuf[s]
            top = jnp.concatenate((weights[0], -weights[1]), axis=1)
            low = jnp.concatenate((weights[1], weights[0]), axis=1)
            right = of_block(ids[1, s])
            moved = jnp.dot(
                jnp.concatenate((top, low), axis=0), right, preferred_element_type=f32
            )
            left = of_block(ids[0, s]).astype(f32)
            carry = carry + jnp.sum((moved * left).reshape(2 * block // 8, 8, count), axis=0)
        return carry

    def project(quarter):
        chunks = block // group // 4

        def body(i, carry):
            first = pl.multiple_of((quarter * chunks + i) * group, group)
            seen = jnp.concatenate(
                [
                    jnp.concatenate([obs[s, first + k] for k in range(group)], axis=1)
                    for s in range(pair_dev)
                ],
                axis=0,
            )
            out = lax.dot_general(
                spread[...], seen, (((1,), (1,)), ((), ())), preferred_element_type=f32
            )
            out = jnp.sum(out.reshape(pieces, 4 * group, pair_dev * block), axis=0)
            for s in range(pair_dev):
                for k in range(2):
                    cols = slice(s * block, (s + 1) * block)
                    ohat[2 * c + s, k, pl.ds(first, group), :] = out[k * group : (k + 1) * group, cols]
                    ohat_send[s, k, pl.ds(first, group), :] = out[(2 + k) * group : (3 + k) * group, cols]
            return carry

        lax.fori_loop(0, chunks, body, 0, unroll=2)

    swap_ohat = remote(
        ohat_send, ohat.at[pl.ds(2 * c, 2)], core_send.at[3], core_recv.at[3], other
    )
    part_rows = block // freq_devices

    def energies():
        def body(i, carry):
            for s in range(pair_dev):
                seen = obs[s, z * part_rows + i].astype(f32)
                energy[pl.ds(s * part_rows + i, 1), :] = jnp.sum(seen * seen, axis=0, keepdims=True)
            return carry

        lax.fori_loop(0, part_rows, body, 0)

    swap_mis = remote(mis_own, mis_other, core_send.at[4], core_recv.at[4], other)

    def copy_z(dz):
        return pltpu.make_async_remote_copy(
            src_ref=mis_pair, dst_ref=mis_freq.at[dz - 1],
            send_sem=z_send.at[0], recv_sem=z_recv.at[0],
            device_id={"freq": (z + dz) % freq_devices}, device_id_type=MESH,
        )

    def misfit_parts():
        for q in range(2 * stages):
            mis_own[pl.ds(q, 1), :] = lane_sum(total[q])[:1]
        swap_mis.start()

    def misfit_sums():
        swap_mis.wait_recv()
        mis_pair[...] = mis_own[...] + mis_other[...]

        @pl.when(z < freq_devices - 1)
        def _():
            pl.semaphore_wait(z_here, freq_devices - 1 - z)

        for dz in range(1, freq_devices):
            copy_z(dz).start()

    def misfit_end():
        wait_all(mis_freq, freq_devices - 1, z_recv.at[0])
        mine = mis_pair[...]
        for dz in range(1, freq_devices):
            mine = mine + mis_freq[dz - 1]
        from_observed = lane_sum(energy[...])[:1]
        picked = jnp.zeros((mine.shape[0], part_rows), f32)
        for part in range(freq_devices):
            picked = jnp.where(z == part, mine[:, part * part_rows : (part + 1) * part_rows], picked)
        for s in range(pair_dev):
            row = jnp.where(c == 0, picked[s : s + 1], picked[2 + s : 3 + s])
            row = row + from_observed[:, s * part_rows : (s + 1) * part_rows]
            misfit_out[pl.ds(s, 1), :] = row * f32(1.0 / (2.0 * block * lags * freq_total))

    lax.fori_loop(len(early), 12, first_ring, 0)
    project(3)
    swap_ohat.start()
    own_part(0)
    second_ring_far(0)
    second_ring_near(0)
    second_ring_far(1)
    second_ring_close(0)
    second_ring_near(1)
    own_part(1)
    second_ring_close(1)
    swap_ohat.wait_recv()
    lax.fori_loop(0, 2, own_adjoint, 0)

    steps = [
        ([], (0, 1), (0, 0), (0, 0)),
        ([(misfit_parts,), (gather_1, 0)], (0, 0), (0, 0), (1, 2)),
        ([(gather_1, 1)], (1, 0), (0, 0), (1, 2)),
        ([(gather_lane, 0, 0), (misfit_sums,)], (0, 0), (1, 2), (0, 0)),
        ([(gather_lane, 1, 0)], (1, 0), (1, 2), (0, 0)),
        ([(gather_lane, 0, 1)], (0, 0), (1, 2), (1, 0)),
        ([(gather_2, 0), (gather_lane, 0, 3)], (0, 0), (1, 2), (3, 0)),
        ([(gather_2, 1)], (0, 1), (0, 0), (2, 0)),
        ([(gather_lane, 1, 1)], (1, 0), (1, 2), (1, 0)),
        ([(gather_lane, 1, 3)], (1, 0), (1, 2), (3, 0)),
        ([(gather_end, 0)], (0, 1), (2, 0), (0, 0)),
        ([(gather_lane, 0, 2)], (0, 0), (1, 2), (2, 0)),
        ([(gather_lane, 1, 2)], (1, 0), (1, 2), (2, 0)),
        ([(gather_end, 1)], (0, 1), (2, 0), (1, 0)),
        ([(gather_end, 3)], (0, 1), (2, 0), (3, 0)),
    ]

    def gather_step(i, carry):
        for n, step in enumerate(steps):
            if step[0]:
                @pl.when(i == n)
                def _(actions=tuple(step[0])):
                    for action in actions:
                        action[0](*action[1:])

        slots = []
        for u in range(4):
            t, o, r = (
                choose(i, [step[part][0] + u // 2 * step[part][1] for step in steps]) for part in (1, 2, 3)
            )
            slots.append(slot_of(t, u % 2, o, r))
        return back(slots, carry, lambda place: both(green_own, green_other, place), 2 * points)

    gsum[...] = lax.fori_loop(0, len(steps), gather_step, gsum[...])

    gather_end(2)
    last = [slot_of(t, h, 2, 2) for t in range(stages) for h in range(2)]
    scale = f32(1.0 / (block * math.sqrt(slot_count)))

    def finish(buffer, first):
        sums = gsum[:, first : first + points]
        sums = back(last, sums, lambda place: buffer[:, place].reshape(2 * block, points), points)
        return jnp.sum(sums, axis=0, keepdims=True) * scale

    gsend[...] = jnp.broadcast_to(finish(green_other, points), gsend.shape)
    swap_sum = remote(gsend, grecv, core_send.at[5], core_recv.at[5], other)
    swap_sum.start()
    own_lines = finish(green_own, 0)
    misfit_end()
    row_ids = lax.broadcasted_iota(jnp.int32, (2, points), 0)
    swap_sum.wait_recv()
    gradient_out[...] = jnp.where(
        row_ids == c, jnp.broadcast_to(own_lines, (2, points)), grecv[:2]
    )

    swap_psd.wait_send()
    wait_all(green_other, 2, green_send.at[0])
    for e in range(len(early)):
        swap_cross(e).wait_send()
    swap_ohat.wait_send()
    swap_mis.wait_send()
    swap_sum.wait_send()
    wait_all(mis_freq, freq_devices - 1, z_send.at[0])
    wait_all(send1, 24 * stages, one_send.at[0])
    wait_all(send_a, 4 * stages, a_send.at[0])
    wait_all(send_b, 4 * stages, b_send.at[0])
    wait_all(abuf, 30 * stages, g_send.at[0])


def hand_on(gradient, misfit, gradient_out, misfit_out):
    gradient_out[...] = gradient[...]
    misfit_out[...] = misfit[...]


def local(green_spectra, source_psd, pair_list, owner_map, observed):
    freq_devices = lax.axis_size("freq")
    planes, freq_dev, stations, points = green_spectra.shape
    pair_dev, block, unused_cols, lags = observed.shape
    slot_count = owner_map.shape[0]
    blocks = stations // block
    freq_total = freq_dev * freq_devices
    table = jnp.asarray(phase_table(freq_total, lags, freq_devices))
    rows = table.shape[1]
    units = stages * 2 * 2
    dma = pltpu.SemaphoreType.DMA
    vmem = pl.BlockSpec(memory_space=pltpu.VMEM)
    hbm = pl.BlockSpec(memory_space=pltpu.HBM)
    pair = (2, block, block)
    gradient, misfit = pl.pallas_call(
        functools.partial(kernel, freq_devices),
        out_shape=(
            jax.ShapeDtypeStruct((freq_dev, points), f32),
            jax.ShapeDtypeStruct((pair_dev, block // freq_devices), f32),
        ),
        in_specs=[hbm] * 6,
        out_specs=(vmem, vmem),
        scratch_shapes=[
            pltpu.VMEM((2, blocks, block, points), bf16),
            pltpu.VMEM((2, blocks, block, points), bf16),
            pltpu.VMEM((2, blocks, block, points), bf16),
            pltpu.VMEM((2, blocks, block, points), bf16),
            pltpu.VMEM((2, blocks, block, points), bf16),
            pltpu.VMEM((8,) + pair, bf16),
            pltpu.VMEM((8,) + pair, bf16),
            pltpu.VMEM((freq_dev, points), f32),
            pltpu.VMEM((freq_dev, points), f32),
            pltpu.VMEM((1, slot_count), jnp.int32),
            pltpu.VMEM((2, slot_count), jnp.int32),
            pltpu.VMEM((8, 128), jnp.int32),
            pltpu.SMEM((8, 128), jnp.int32),
            pltpu.VMEM((pair_dev, block, block, lags), bf16),
            pltpu.VMEM((rows, lags), bf16),
            pltpu.VMEM((rows, group * lags), bf16),
            pltpu.VMEM((2 * pair_dev,) + pair, f32),
            pltpu.VMEM((pair_dev,) + pair, f32),
            pltpu.VMEM((pair_dev * (block // freq_devices), lags), f32),
            pltpu.VMEM((24 * stages,) + pair, bf16),
            pltpu.VMEM((24 * stages + 1,) + pair, bf16),
            pltpu.VMEM((units, block, block), bf16),
            pltpu.VMEM((units, block, block), bf16),
            pltpu.VMEM((units,) + pair, bf16),
            pltpu.VMEM((units,) + pair, bf16),
            pltpu.VMEM((units, block, block), f32),
            pltpu.VMEM((2 * stages,) + pair, f32),
            pltpu.VMEM((slot_count,) + pair, bf16),
            pltpu.VMEM((2 * stages, block, block), f32),
            pltpu.VMEM((8, block), f32),
            pltpu.VMEM((8, block), f32),
            pltpu.VMEM((8, block), f32),
            pltpu.VMEM((freq_devices - 1, 8, block), f32),
            pltpu.VMEM((8, 2 * points), f32),
            pltpu.VMEM((8, points), f32),
            pltpu.VMEM((8, points), f32),
            dma((8,)),
            dma((6,)),
            dma((6,)),
            dma((1,)),
            dma((8,)),
            dma((1,)),
            dma((6 * stages,)),
            dma((1,)),
            dma((stages,)),
            dma((1,)),
            dma((stages,)),
            dma((1,)),
            dma((stages,)),
            dma((stages,)),
            dma((4 * stages,)),
            dma((4,)),
            dma((1,)),
            dma((1,)),
            pltpu.SemaphoreType.REGULAR,
            pltpu.SemaphoreType.REGULAR,
        ],
        compiler_params=pltpu.CompilerParams(
            collective_id=0, has_side_effects=True, vmem_limit_bytes=60 * 1024 * 1024
        ),
        cost_estimate=pl.CostEstimate(
            flops=8 * slot_count * freq_dev * 2 * block * block * points,
            bytes_accessed=12 * 1024 * 1024,
            transcendentals=0,
        ),
        name="misfit_gradient",
    )(
        owner_map.reshape(1, slot_count),
        pair_list.T,
        source_psd,
        table,
        green_spectra.reshape(planes, freq_dev, blocks, block, points),
        observed,
    )
    return pl.pallas_call(
        hand_on,
        out_shape=(
            jax.ShapeDtypeStruct(gradient.shape, f32),
            jax.ShapeDtypeStruct(misfit.shape, f32),
        ),
        in_specs=[vmem, vmem],
        out_specs=(vmem, vmem),
        name="hand_on",
    )(gradient, misfit)


def solution(mesh):
    in_specs = (
        P(None, "freq", None, "grid"),
        P("freq", "grid"),
        P(),
        P(),
        P("grid", None, None, None),
    )
    out_specs = (P("freq", "grid"), P("grid", "freq"))
    return jax.shard_map(local, mesh=mesh, in_specs=in_specs, out_specs=out_specs, check_vma=False)
```

```python
import functools
import math

import jax
import jax.numpy as jnp
import ml_dtypes
import numpy as np
from jax import lax
from jax.experimental import pallas as pl
from jax.experimental.pallas import tpu as pltpu
from jax.sharding import PartitionSpec as P

harmonic_step = 3
side = 4
stages = 2
pieces = 3
group = 8
MESH = pl.DeviceIdType.MESH
f32 = jnp.float32
bf16 = jnp.bfloat16


def phase_table(freq_total, lag_count, freq_devices):
    freq_ids = np.arange(freq_total)[:, None]
    turns = harmonic_step * (freq_ids + 1) * np.arange(lag_count)[None, :] % lag_count
    angles = turns * (2.0 * math.pi / lag_count)
    exact = np.stack((np.cos(angles), -np.sin(angles)), axis=1)
    parts = []
    for unused in range(pieces):
        part = exact.astype(ml_dtypes.bfloat16)
        parts.append(part)
        exact = exact - part.astype(np.float64)
    table = np.stack(parts).reshape(pieces, freq_devices, 2, 2, lag_count)
    both = np.stack((table, table[:, :, ::-1]), axis=2)
    both = both.transpose(1, 2, 0, 3, 4, 5).reshape(freq_devices * 2, pieces * 4, lag_count)
    return np.repeat(both, group, axis=1)


def kernel(
    freq_devices,
    owner,
    pairs,
    psd_hbm,
    table,
    green,
    observed,
    gradient_out,
    misfit_out,
    green_own,
    green_other,
    green_cross,
    weighted_own,
    weighted_other,
    cross_send,
    cross_recv,
    psd,
    psd_other,
    owner_row,
    pair_rows,
    ids_row,
    ids,
    obs,
    phi,
    spread,
    ohat,
    ohat_send,
    energy,
    send1,
    recv1,
    send_a,
    recv_a,
    send_b,
    recv_b,
    keep,
    own_sum,
    abuf,
    total,
    mis_own,
    mis_other,
    mis_pair,
    mis_freq,
    gsum,
    gsend,
    grecv,
    local_sem,
    core_send,
    core_recv,
    green_send,
    green_recv,
    one_send,
    one_recv,
    a_send,
    a_recv,
    b_send,
    b_recv,
    g_send,
    g1_recv,
    g1f_recv,
    g2_recv,
    g2f_recv,
    z_send,
    z_recv,
    z_here,
    near_here,
):
    z = lax.axis_index("freq")
    g = lax.axis_index("grid")
    c = g % 2
    x = (g // 2) % side
    y = g // (2 * side)
    other = g + 1 - 2 * c
    points = psd_hbm.shape[1]
    pair_dev, block, unused_cols, lags = observed.shape
    freq_total = 2 * freq_devices
    slot_count = 2 * side * side * pair_dev
    root_scale = 1.0 / math.sqrt(points * 2 * side * side)

    def neighbour(axis, d):
        step = 1 + 2 * d
        nx = (x + (1 - axis) * step) % side
        ny = (y + axis * step) % side
        return (ny * side + nx) * 2 + c

    def slot_of(t, h, o, r):
        sx = (x + (1 - h) * o + h * r) % side
        sy = (y + h * o + (1 - h) * r) % side
        return (sy * side + sx) * 4 + h * 2 + t

    def lane(d, j):
        return (1 - d) * (2 - 2 * j) + d * (1 + 2 * j)

    def lane_place(r):
        return ((r + 1) // 2 + 1) % 2

    def remote(src, dst, send, recv, device):
        return pltpu.make_async_remote_copy(
            src_ref=src, dst_ref=dst, send_sem=send, recv_sem=recv,
            device_id={"grid": device}, device_id_type=MESH,
        )

    def copy1(n):
        t, role, u = n // 24, (n % 24) // 8, n % 8
        h, d, j = u % 2, (u // 2) % 2, u // 4
        r = jnp.where(role == 1, lane(1 - d, j), lane(d, j))
        i = jnp.where(role == 0, t * 2 + j, 4 + t * 4 + r)
        return remote(send1.at[n], recv1.at[n], one_send.at[0], one_recv.at[i], neighbour(h, d))

    early = [(1, 1), (0, 0)]

    barrier = pltpu.get_barrier_semaphore()
    def distance(p):
        return jnp.minimum(p, side - p)

    lower = distance(x) + distance(y)
    pl.semaphore_signal(barrier, inc=1, device_id={"grid": other}, device_id_type=MESH)

    def greet(semaphore, upward):
        for axis, p in enumerate((x, y)):
            for d in range(2):
                q = (p + 1 + 2 * d) % side
                near, far = (distance(p), distance(q)) if upward else (distance(q), distance(p))

                @pl.when(near < far)
                def _():
                    pl.semaphore_signal(
                        semaphore, inc=1, device_id={"grid": neighbour(axis, d)}, device_id_type=MESH
                    )

    greet(barrier, True)
    for dz in range(1, freq_devices):

        @pl.when(z + dz < freq_devices)
        def _():
            pl.semaphore_signal(barrier, inc=1, device_id={"freq": z + dz}, device_id_type=MESH)

    load_owner = pltpu.make_async_copy(owner, owner_row, local_sem.at[4])
    load_pairs = pltpu.make_async_copy(pairs, pair_rows, local_sem.at[5])
    load_psd = pltpu.make_async_copy(psd_hbm, psd, local_sem.at[6])
    load_green = pltpu.make_async_copy(green.at[:, c], green_own, local_sem.at[0])
    load_cross = pltpu.make_async_copy(green.at[:, 1 - c], green_cross, local_sem.at[1])
    load_table = pltpu.make_async_copy(table.at[z * 2 + c], phi, local_sem.at[2])
    load_obs = pltpu.make_async_copy(observed, obs, local_sem.at[3])
    load_owner.start()
    load_pairs.start()
    load_psd.start()
    load_cross.start()
    load_green.start()
    load_table.start()
    pl.semaphore_wait(barrier, 1 + lower + z)

    swap_psd = remote(psd_hbm, psd_other, core_send.at[2], core_recv.at[2], other)
    parts = 4
    blocks = green.shape[2]

    def swap_green(n):
        k, some = n // parts, pl.ds(n % parts * (blocks // parts), blocks // parts)
        return remote(
            green.at[k, 1 - c, some], green_other.at[k, some], green_send.at[0], green_recv.at[n], other
        )

    swap_psd.start()
    for n in range(3):
        swap_green(n).start()

    greet(near_here, False)
    for dz in range(1, freq_devices):

        @pl.when(z >= dz)
        def _():
            pl.semaphore_signal(z_here, inc=1, device_id={"freq": z - dz}, device_id_type=MESH)

    def weigh(k, first, count, source, result, row):
        def body(b, carry):
            for i in range(4):
                place = first + 4 * b + i
                result[k, place] = (source[k, place].astype(f32) * row).astype(bf16)
            return carry

        lax.fori_loop(0, count // 4, body, 0)

    def cross_parts(left, right):
        acc = lax.dot_general(left, right, (((1,), (1,)), ((), ())), preferred_element_type=f32)
        return acc[:block, :block] + acc[block:, block:], acc[block:, :block] - acc[:block, block:]

    load_owner.wait()
    load_pairs.wait()
    square = (slot_count, slot_count)
    across = lax.broadcasted_iota(jnp.int32, square, 1)
    along = lax.broadcasted_iota(jnp.int32, square, 0)

    def down(row):
        return jnp.sum(jnp.where(across == along, jnp.broadcast_to(row, square), 0), axis=1, keepdims=True)

    their_owner = jnp.broadcast_to(owner_row[...], square)
    my_owner = down(owner_row[...])
    earlier = (their_owner < my_owner) | ((their_owner == my_owner) & (across < along))
    ids_row[...] = jnp.zeros_like(ids_row)
    entry_slot = jnp.sum(jnp.where(earlier, 1, 0), axis=1, keepdims=True)
    hit = entry_slot == across
    for k in range(2):
        chosen = jnp.where(hit, down(pair_rows[pl.ds(k, 1), :]), 0)
        ids_row[pl.ds(k, 1), pl.ds(0, slot_count)] = jnp.sum(chosen, axis=0, keepdims=True)
    move_ids = pltpu.make_async_copy(ids_row, ids, local_sem.at[7])
    move_ids.start()

    def early_slots(t, j):
        return [slot_of(t, u % 2, 2, lane(u // 2, j)) for u in range(4)]

    def swap_cross(e):
        some = pl.ds(4 * e, 4)
        return remote(
            cross_send.at[some], cross_recv.at[some], core_send.at[e], core_recv.at[e], other
        )

    load_psd.wait()
    cross_row = psd[pl.ds(1 - c, 1), :]
    load_cross.wait()
    move_ids.wait()
    for e, (t, j) in enumerate(early):
        for u, slot in enumerate(early_slots(t, j)):
            left = (green_cross[:, ids[0, slot]].astype(f32) * cross_row).astype(bf16)
            right = green_cross[:, ids[1, slot]]
            values = cross_parts(left.reshape(2 * block, points), right.reshape(2 * block, points))
            for k in range(2):
                cross_send[4 * e + u, k] = values[k].astype(bf16)
        swap_cross(e).start()
        if e == 0:
            swap_green(3).start()
    for n in range(4, 2 * parts):
        swap_green(n).start()
    load_obs.start()

    own_row = psd[pl.ds(c, 1), :]
    load_green.wait()
    for k in range(2):
        weigh(k, 0, blocks, green_own, weighted_own, own_row)
    for e, (t, j) in enumerate(early):
        shares = [
            cross_parts(
                weighted_own[:, ids[0, slot]].reshape(2 * block, points),
                green_own[:, ids[1, slot]].reshape(2 * block, points),
            )
            for slot in early_slots(t, j)
        ]
        swap_cross(e).wait_recv()
        first = t * 24 + j * 4
        for u, values in enumerate(shares):
            for k in range(2):
                send1[first + u, k] = (values[k] + cross_recv[4 * e + u, k].astype(f32)).astype(bf16)
        if e == 0:

            @pl.when(lower < side)
            def _():
                pl.semaphore_wait(near_here, side - lower)

        for u in range(4):
            copy1(first + u).start()

    load_table.wait()
    rows = phi.shape[0]
    row_in_group = lax.broadcasted_iota(jnp.int32, (rows, lags), 0) % group
    phi_values = phi[...].astype(f32)
    for i in range(group):
        spread[:, pl.ds(i * lags, lags)] = jnp.where(row_in_group == i, phi_values, 0.0).astype(bf16)

    recv1[48] = jnp.zeros_like(recv1[48])
    gsum[...] = jnp.zeros_like(gsum)
    mis_own[...] = jnp.zeros_like(mis_own)
    swap_psd.wait_recv()
    other_row = psd_other[pl.ds(c, 1), :]
    for n in range(2 * parts):
        swap_green(n).wait_recv()
        weigh(n // parts, n % parts * (blocks // parts), blocks // parts, green_other, weighted_other, other_row)

    def both(own, others, place):
        return jnp.concatenate((own[:, place], others[:, place]), axis=2).reshape(2 * block, 2 * points)

    def units(slots):
        return [
            cross_parts(
                both(weighted_own, weighted_other, ids[0, slot]),
                both(green_own, green_other, ids[1, slot]),
            )
            for slot in slots
        ]

    def wait_all(buffer, count, semaphore):
        some = buffer.at[pl.ds(0, count)]
        pltpu.make_async_copy(some, some, semaphore).wait()

    def wait1(i):
        wait_all(recv1, 4, one_recv.at[i])

    def choose(i, values):
        chosen = values[0]
        for n in range(1, len(values)):
            chosen = jnp.where(i >= n, values[n], chosen) if values[n] != values[n - 1] else chosen
        return chosen

    groups = [
        (0, 1, 1), (0, 0, 0), (0, 0, 1), (0, 1, 0), (2, 0, 0), (2, 0, 1),
        (1, 0, 0), (1, 0, 1), (2, 1, 0), (2, 1, 1), (1, 1, 0), (1, 1, 1),
    ]

    def first_ring(i, carry):
        part, t, j = (choose(i, [values[k] for values in groups]) for k in range(3))
        through = part == 1
        role = jnp.where(through, 2, part // 2)
        first = t * 24 + role * 8 + j * 4

        @pl.when(i == 6)
        def _():
            load_obs.wait()
            energies()

        @pl.when((i == 6) | (i == 8) | (i == 10))
        def _():
            project(jnp.where(i == 6, 0, jnp.where(i == 8, 1, 2)))

        @pl.when(through)
        def _():
            wait1(t * 2 + j)

        slots = []
        for u in range(4):
            h, d = u % 2, u // 2
            o = jnp.where(part == 0, 2, 1 + 2 * d)
            r = jnp.where(part == 2, lane(1 - d, j), lane(d, j))
            slots.append(slot_of(t, h, o, r))
        for u, values in enumerate(units(slots)):
            n = first + u
            with_n = jnp.where(through, n - 16, 48)
            for k in range(2):
                send1[n, k] = (values[k] + recv1[with_n, k].astype(f32)).astype(bf16)
        for u in range(4):
            copy1(first + u).start()
        return carry

    def arrival1(t, h, d, r):
        role = 2 - (r + d) % 2
        return t * 24 + role * 8 + lane_place(r) * 4 + d * 2 + h

    def line_sums(t, wanted):
        for r in sorted({r for h, r in wanted}):
            wait1(4 + t * 4 + r)
        sums = []
        for (h, r), values in zip(wanted, units([slot_of(t, h, 0, r) for h, r in wanted])):
            arrived = [recv1[arrival1(t, h, d, r)].astype(f32) for d in range(2)]
            sums.append([values[k] + (arrived[0][k] + arrived[1][k]) for k in range(2)])
        return sums

    def place(t, h, d):
        return (t * 2 + h) * 2 + d

    def copy_a(t, h, d):
        i = place(t, h, d)
        return remote(send_a.at[i], recv_a.at[i], a_send.at[0], a_recv.at[t], neighbour(1 - h, d))

    def copy_b(t, h, d, k):
        i = place(t, h, d)
        return remote(
            send_b.at[i, k], recv_b.at[i, k], b_send.at[0], b_recv.at[t], neighbour(1 - h, d)
        )

    def second_ring_far(t):
        for h, values in enumerate(line_sums(t, [(0, 2), (1, 2)])):
            for d in range(2):
                send_a[place(t, h, d)] = values[d].astype(bf16)
                copy_a(t, h, d).start()

    def second_ring_near(t):
        wanted = [(h, 1 + 2 * d) for d in range(2) for h in range(2)]
        for (h, r), values in zip(wanted, line_sums(t, wanted)):
            d = r // 2
            i = place(t, h, d)
            send_b[i, 1 - d] = values[1 - d].astype(bf16)
            copy_b(t, h, d, 1 - d).start()
            keep[i] = values[d]

    def own_part(t):
        for h, values in enumerate(line_sums(t, [(0, 0), (1, 0)])):
            for k in range(2):
                own_sum[t * 2 + h, k] = values[k]

    def second_ring_close(t):
        wait_all(recv_a, 4, a_recv.at[t])
        for d in range(2):
            for h in range(2):
                i = place(t, h, d)
                send_b[i, d] = (keep[i] + recv_a[i].astype(f32)).astype(bf16)
                copy_b(t, h, d, d).start()

    def copy_g1(t, h, d):
        s = slot_of(t, h, 0, 0)
        return remote(abuf.at[s], abuf.at[s], g_send.at[0], g1_recv.at[t], neighbour(1 - h, d))

    def copy_g1f(t, h, d):
        s = slot_of(t, h, 0, 3 - 2 * d)
        return remote(abuf.at[s, d], abuf.at[s, d], g_send.at[0], g1f_recv.at[t], neighbour(1 - h, d))

    def copy_g2(t, h, d, r):
        s = slot_of(t, h, 0, r)
        return remote(abuf.at[s], abuf.at[s], g_send.at[0], g2_recv.at[t * 4 + r], neighbour(h, d))

    def copy_g2f(t, h, d, j):
        r = lane(d, j)
        s = slot_of(t, h, 3 - 2 * d, r)
        return remote(abuf.at[s], abuf.at[s], g_send.at[0], g2f_recv.at[r], neighbour(h, d))

    ones = jnp.ones((8, block), f32)

    def lane_sum(values):
        return lax.dot_general(
            ones[:, : values.shape[1]], values, (((1,), (1,)), ((), ())),
            precision=lax.Precision.HIGHEST, preferred_element_type=f32,
        )

    def own_adjoint(t, carry):
        wait_all(recv_b, 4, b_recv.at[t])
        for h in range(2):
            s, q = slot_of(t, h, 0, 0), h * 2 + t
            kept = jnp.zeros((block, block), f32)
            for k in range(2):
                value = own_sum[t * 2 + h, k]
                for d in range(2):
                    value = value + recv_b[place(t, h, d), k].astype(f32)
                cross = value * f32(root_scale)
                seen = ohat[q, k]
                abuf[s, k] = (0.5 * cross - seen * f32(1.0 / lags)).astype(bf16)
                kept = kept + cross * (f32(lags / 2) * cross - 2.0 * seen)
            for d in range(2):
                copy_g1(t, h, d).start()
            total[q] = kept
        for h in range(2):
            for d in range(2):
                copy_g2(t, h, d, 0).start()
        return carry

    def gather_1(t):
        wait_all(abuf, 4, g1_recv.at[t])

        for h in range(2):
            for d in range(2):
                copy_g1f(t, h, d).start()
        for d in range(2):
            for h in range(2):
                for side_d in range(2):
                    copy_g2(t, h, side_d, 3 - 2 * d).start()

    def gather_2(t):
        wait_all(abuf, 2, g1f_recv.at[t])
        for h in range(2):
            for d in range(2):
                copy_g2(t, h, d, 2).start()

    def gather_lane(t, r):
        wait_all(abuf, 4, g2_recv.at[t * 4 + r])
        for h in range(2):
            copy_g2f(t, h, r % 2, lane_place(r)).start()

    def gather_end(r):
        wait_all(abuf, 4, g2f_recv.at[r])

    def back(slots, carry, of_block, count):
        for s in slots:
            weights = abuf[s]
            top = jnp.concatenate((weights[0], -weights[1]), axis=1)
            low = jnp.concatenate((weights[1], weights[0]), axis=1)
            right = of_block(ids[1, s])
            moved = jnp.dot(
                jnp.concatenate((top, low), axis=0), right, preferred_element_type=f32
            )
            left = of_block(ids[0, s]).astype(f32)
            carry = carry + jnp.sum((moved * left).reshape(2 * block // 8, 8, count), axis=0)
        return carry

    def project(quarter):
        chunks = block // group // 4

        def body(i, carry):
            first = pl.multiple_of((quarter * chunks + i) * group, group)
            seen = jnp.concatenate(
                [
                    jnp.concatenate([obs[s, first + k] for k in range(group)], axis=1)
                    for s in range(pair_dev)
                ],
                axis=0,
            )
            out = lax.dot_general(
                spread[...], seen, (((1,), (1,)), ((), ())), preferred_element_type=f32
            )
            out = jnp.sum(out.reshape(pieces, 4 * group, pair_dev * block), axis=0)
            for s in range(pair_dev):
                for k in range(2):
                    cols = slice(s * block, (s + 1) * block)
                    ohat[2 * c + s, k, pl.ds(first, group), :] = out[k * group : (k + 1) * group, cols]
                    ohat_send[s, k, pl.ds(first, group), :] = out[(2 + k) * group : (3 + k) * group, cols]
            return carry

        lax.fori_loop(0, chunks, body, 0, unroll=2)

    swap_ohat = remote(
        ohat_send, ohat.at[pl.ds(2 * c, 2)], core_send.at[3], core_recv.at[3], other
    )
    part_rows = block // freq_devices

    def energies():
        def body(i, carry):
            for s in range(pair_dev):
                seen = obs[s, z * part_rows + i].astype(f32)
                energy[pl.ds(s * part_rows + i, 1), :] = jnp.sum(seen * seen, axis=0, keepdims=True)
            return carry

        lax.fori_loop(0, part_rows, body, 0)

    swap_mis = remote(mis_own, mis_other, core_send.at[4], core_recv.at[4], other)

    def copy_z(dz):
        return pltpu.make_async_remote_copy(
            src_ref=mis_pair, dst_ref=mis_freq.at[dz - 1],
            send_sem=z_send.at[0], recv_sem=z_recv.at[0],
            device_id={"freq": (z + dz) % freq_devices}, device_id_type=MESH,
        )

    def misfit_parts():
        for q in range(2 * stages):
            mis_own[pl.ds(q, 1), :] = lane_sum(total[q])[:1]
        swap_mis.start()

    def misfit_sums():
        swap_mis.wait_recv()
        mis_pair[...] = mis_own[...] + mis_other[...]

        @pl.when(z < freq_devices - 1)
        def _():
            pl.semaphore_wait(z_here, freq_devices - 1 - z)

        for dz in range(1, freq_devices):
            copy_z(dz).start()

    def misfit_end():
        wait_all(mis_freq, freq_devices - 1, z_recv.at[0])
        mine = mis_pair[...]
        for dz in range(1, freq_devices):
            mine = mine + mis_freq[dz - 1]
        from_observed = lane_sum(energy[...])[:1]
        picked = jnp.zeros((mine.shape[0], part_rows), f32)
        for part in range(freq_devices):
            picked = jnp.where(z == part, mine[:, part * part_rows : (part + 1) * part_rows], picked)
        for s in range(pair_dev):
            row = jnp.where(c == 0, picked[s : s + 1], picked[2 + s : 3 + s])
            row = row + from_observed[:, s * part_rows : (s + 1) * part_rows]
            misfit_out[pl.ds(s, 1), :] = row * f32(1.0 / (2.0 * block * lags * freq_total))

    lax.fori_loop(len(early), 12, first_ring, 0)
    project(3)
    swap_ohat.start()
    own_part(0)
    second_ring_far(0)
    second_ring_near(0)
    second_ring_far(1)
    second_ring_close(0)
    second_ring_near(1)
    own_part(1)
    second_ring_close(1)
    swap_ohat.wait_recv()
    lax.fori_loop(0, 2, own_adjoint, 0)

    steps = [
        ([], (0, 1), (0, 0), (0, 0)),
        ([(misfit_parts,), (gather_1, 0)], (0, 0), (0, 0), (1, 2)),
        ([(gather_1, 1)], (1, 0), (0, 0), (1, 2)),
        ([(gather_lane, 0, 0), (misfit_sums,)], (0, 0), (1, 2), (0, 0)),
        ([(gather_2, 0), (gather_lane, 1, 0)], (1, 0), (1, 2), (0, 0)),
        ([(gather_2, 1), (gather_lane, 0, 1)], (0, 0), (1, 2), (1, 0)),
        ([(gather_lane, 0, 3)], (0, 0), (1, 2), (3, 0)),
        ([], (0, 1), (0, 0), (2, 0)),
        ([(gather_lane, 1, 1)], (1, 0), (1, 2), (1, 0)),
        ([(gather_lane, 1, 3)], (1, 0), (1, 2), (3, 0)),
        ([(gather_end, 0)], (0, 1), (2, 0), (0, 0)),
        ([(gather_lane, 0, 2)], (0, 0), (1, 2), (2, 0)),
        ([(gather_lane, 1, 2)], (1, 0), (1, 2), (2, 0)),
        ([(gather_end, 1)], (0, 1), (2, 0), (1, 0)),
        ([(gather_end, 3)], (0, 1), (2, 0), (3, 0)),
    ]

    def gather_step(i, carry):
        for n, step in enumerate(steps):
            if step[0]:
                @pl.when(i == n)
                def _(actions=tuple(step[0])):
                    for action in actions:
                        action[0](*action[1:])

        slots = []
        for u in range(4):
            t, o, r = (
                choose(i, [step[part][0] + u // 2 * step[part][1] for step in steps]) for part in (1, 2, 3)
            )
            slots.append(slot_of(t, u % 2, o, r))
        return back(slots, carry, lambda place: both(green_own, green_other, place), 2 * points)

    gsum[...] = lax.fori_loop(0, len(steps), gather_step, gsum[...])

    gather_end(2)
    last = [slot_of(t, h, 2, 2) for t in range(stages) for h in range(2)]
    scale = f32(1.0 / (block * math.sqrt(slot_count)))

    def finish(buffer, first):
        sums = gsum[:, first : first + points]
        sums = back(last, sums, lambda place: buffer[:, place].reshape(2 * block, points), points)
        return jnp.sum(sums, axis=0, keepdims=True) * scale

    gsend[...] = jnp.broadcast_to(finish(green_other, points), gsend.shape)
    swap_sum = remote(gsend, grecv, core_send.at[5], core_recv.at[5], other)
    swap_sum.start()
    own_lines = finish(green_own, 0)
    misfit_end()
    row_ids = lax.broadcasted_iota(jnp.int32, (2, points), 0)
    swap_sum.wait_recv()
    gradient_out[...] = jnp.where(
        row_ids == c, jnp.broadcast_to(own_lines, (2, points)), grecv[:2]
    )

    swap_psd.wait_send()
    wait_all(green_other, 2, green_send.at[0])
    for e in range(len(early)):
        swap_cross(e).wait_send()
    swap_ohat.wait_send()
    swap_mis.wait_send()
    swap_sum.wait_send()
    wait_all(mis_freq, freq_devices - 1, z_send.at[0])
    wait_all(send1, 24 * stages, one_send.at[0])
    wait_all(send_a, 4 * stages, a_send.at[0])
    wait_all(send_b, 4 * stages, b_send.at[0])
    wait_all(abuf, 30 * stages, g_send.at[0])


def hand_on(gradient, misfit, gradient_out, misfit_out):
    gradient_out[...] = gradient[...]
    misfit_out[...] = misfit[...]


def local(green_spectra, source_psd, pair_list, owner_map, observed):
    freq_devices = lax.axis_size("freq")
    planes, freq_dev, stations, points = green_spectra.shape
    pair_dev, block, unused_cols, lags = observed.shape
    slot_count = owner_map.shape[0]
    blocks = stations // block
    freq_total = freq_dev * freq_devices
    table = jnp.asarray(phase_table(freq_total, lags, freq_devices))
    rows = table.shape[1]
    units = stages * 2 * 2
    dma = pltpu.SemaphoreType.DMA
    vmem = pl.BlockSpec(memory_space=pltpu.VMEM)
    hbm = pl.BlockSpec(memory_space=pltpu.HBM)
    pair = (2, block, block)
    gradient, misfit = pl.pallas_call(
        functools.partial(kernel, freq_devices),
        out_shape=(
            jax.ShapeDtypeStruct((freq_dev, points), f32),
            jax.ShapeDtypeStruct((pair_dev, block // freq_devices), f32),
        ),
        in_specs=[hbm] * 6,
        out_specs=(vmem, vmem),
        scratch_shapes=[
            pltpu.VMEM((2, blocks, block, points), bf16),
            pltpu.VMEM((2, blocks, block, points), bf16),
            pltpu.VMEM((2, blocks, block, points), bf16),
            pltpu.VMEM((2, blocks, block, points), bf16),
            pltpu.VMEM((2, blocks, block, points), bf16),
            pltpu.VMEM((8,) + pair, bf16),
            pltpu.VMEM((8,) + pair, bf16),
            pltpu.VMEM((freq_dev, points), f32),
            pltpu.VMEM((freq_dev, points), f32),
            pltpu.VMEM((1, slot_count), jnp.int32),
            pltpu.VMEM((2, slot_count), jnp.int32),
            pltpu.VMEM((8, 128), jnp.int32),
            pltpu.SMEM((8, 128), jnp.int32),
            pltpu.VMEM((pair_dev, block, block, lags), bf16),
            pltpu.VMEM((rows, lags), bf16),
            pltpu.VMEM((rows, group * lags), bf16),
            pltpu.VMEM((2 * pair_dev,) + pair, f32),
            pltpu.VMEM((pair_dev,) + pair, f32),
            pltpu.VMEM((pair_dev * (block // freq_devices), lags), f32),
            pltpu.VMEM((24 * stages,) + pair, bf16),
            pltpu.VMEM((24 * stages + 1,) + pair, bf16),
            pltpu.VMEM((units, block, block), bf16),
            pltpu.VMEM((units, block, block), bf16),
            pltpu.VMEM((units,) + pair, bf16),
            pltpu.VMEM((units,) + pair, bf16),
            pltpu.VMEM((units, block, block), f32),
            pltpu.VMEM((2 * stages,) + pair, f32),
            pltpu.VMEM((slot_count,) + pair, bf16),
            pltpu.VMEM((2 * stages, block, block), f32),
            pltpu.VMEM((8, block), f32),
            pltpu.VMEM((8, block), f32),
            pltpu.VMEM((8, block), f32),
            pltpu.VMEM((freq_devices - 1, 8, block), f32),
            pltpu.VMEM((8, 2 * points), f32),
            pltpu.VMEM((8, points), f32),
            pltpu.VMEM((8, points), f32),
            dma((8,)),
            dma((6,)),
            dma((6,)),
            dma((1,)),
            dma((8,)),
            dma((1,)),
            dma((6 * stages,)),
            dma((1,)),
            dma((stages,)),
            dma((1,)),
            dma((stages,)),
            dma((1,)),
            dma((stages,)),
            dma((stages,)),
            dma((4 * stages,)),
            dma((4,)),
            dma((1,)),
            dma((1,)),
            pltpu.SemaphoreType.REGULAR,
            pltpu.SemaphoreType.REGULAR,
        ],
        compiler_params=pltpu.CompilerParams(
            collective_id=0, has_side_effects=True, vmem_limit_bytes=60 * 1024 * 1024
        ),
        cost_estimate=pl.CostEstimate(
            flops=8 * slot_count * freq_dev * 2 * block * block * points,
            bytes_accessed=12 * 1024 * 1024,
            transcendentals=0,
        ),
        name="misfit_gradient",
    )(
        owner_map.reshape(1, slot_count),
        pair_list.T,
        source_psd,
        table,
        green_spectra.reshape(planes, freq_dev, blocks, block, points),
        observed,
    )
    return pl.pallas_call(
        hand_on,
        out_shape=(
            jax.ShapeDtypeStruct(gradient.shape, f32),
            jax.ShapeDtypeStruct(misfit.shape, f32),
        ),
        in_specs=[vmem, vmem],
        out_specs=(vmem, vmem),
        name="hand_on",
    )(gradient, misfit)


def solution(mesh):
    in_specs = (
        P(None, "freq", None, "grid"),
        P("freq", "grid"),
        P(),
        P(),
        P("grid", None, None, None),
    )
    out_specs = (P("freq", "grid"), P("grid", "freq"))
    return jax.shard_map(local, mesh=mesh, in_specs=in_specs, out_specs=out_specs, check_vma=False)
```

```python
import functools
import math

import jax
import jax.numpy as jnp
import ml_dtypes
import numpy as np
from jax import lax
from jax.experimental import pallas as pl
from jax.experimental.pallas import tpu as pltpu
from jax.sharding import PartitionSpec as P

harmonic_step = 3
side = 4
stages = 2
pieces = 3
group = 8
MESH = pl.DeviceIdType.MESH
f32 = jnp.float32
bf16 = jnp.bfloat16


def phase_table(freq_total, lag_count, freq_devices):
    freq_ids = np.arange(freq_total)[:, None]
    turns = harmonic_step * (freq_ids + 1) * np.arange(lag_count)[None, :] % lag_count
    angles = turns * (2.0 * math.pi / lag_count)
    exact = np.stack((np.cos(angles), -np.sin(angles)), axis=1)
    parts = []
    for unused in range(pieces):
        part = exact.astype(ml_dtypes.bfloat16)
        parts.append(part)
        exact = exact - part.astype(np.float64)
    table = np.stack(parts).reshape(pieces, freq_devices, 2, 2, lag_count)
    both = np.stack((table, table[:, :, ::-1]), axis=2)
    both = both.transpose(1, 2, 0, 3, 4, 5).reshape(freq_devices * 2, pieces * 4, lag_count)
    return np.repeat(both, group, axis=1)


def kernel(
    freq_devices,
    owner,
    pairs,
    psd_hbm,
    table,
    green,
    observed,
    gradient_out,
    misfit_out,
    green_own,
    green_other,
    green_cross,
    weighted_own,
    weighted_other,
    cross_send,
    cross_recv,
    psd,
    psd_other,
    owner_row,
    pair_rows,
    ids_row,
    ids,
    obs,
    phi,
    spread,
    ohat,
    ohat_send,
    energy,
    send1,
    recv1,
    send_a,
    recv_a,
    send_b,
    recv_b,
    keep,
    own_sum,
    abuf,
    total,
    mis_own,
    mis_other,
    mis_pair,
    mis_freq,
    gsum,
    gsend,
    grecv,
    local_sem,
    core_send,
    core_recv,
    green_send,
    green_recv,
    one_send,
    one_recv,
    a_send,
    a_recv,
    b_send,
    b_recv,
    g_send,
    g1_recv,
    g1f_recv,
    g2_recv,
    g2f_recv,
    z_send,
    z_recv,
    z_here,
    near_here,
):
    z = lax.axis_index("freq")
    g = lax.axis_index("grid")
    c = g % 2
    x = (g // 2) % side
    y = g // (2 * side)
    other = g + 1 - 2 * c
    points = psd_hbm.shape[1]
    pair_dev, block, unused_cols, lags = observed.shape
    freq_total = 2 * freq_devices
    slot_count = 2 * side * side * pair_dev
    root_scale = 1.0 / math.sqrt(points * 2 * side * side)

    def neighbour(axis, d):
        step = 1 + 2 * d
        nx = (x + (1 - axis) * step) % side
        ny = (y + axis * step) % side
        return (ny * side + nx) * 2 + c

    def slot_of(t, h, o, r):
        sx = (x + (1 - h) * o + h * r) % side
        sy = (y + h * o + (1 - h) * r) % side
        return (sy * side + sx) * 4 + h * 2 + t

    def lane(d, j):
        return (1 - d) * (2 - 2 * j) + d * (1 + 2 * j)

    def lane_place(r):
        return ((r + 1) // 2 + 1) % 2

    def remote(src, dst, send, recv, device):
        return pltpu.make_async_remote_copy(
            src_ref=src, dst_ref=dst, send_sem=send, recv_sem=recv,
            device_id={"grid": device}, device_id_type=MESH,
        )

    def copy1(n):
        t, role, u = n // 24, (n % 24) // 8, n % 8
        h, d, j = u % 2, (u // 2) % 2, u // 4
        r = jnp.where(role == 1, lane(1 - d, j), lane(d, j))
        i = jnp.where(role == 0, t * 2 + j, 4 + t * 4 + r)
        return remote(send1.at[n], recv1.at[n], one_send.at[0], one_recv.at[i], neighbour(h, d))

    early = [(1, 1), (0, 0)]

    barrier = pltpu.get_barrier_semaphore()
    def distance(p):
        return jnp.minimum(p, side - p)

    lower = distance(x) + distance(y)
    pl.semaphore_signal(barrier, inc=1, device_id={"grid": other}, device_id_type=MESH)

    def greet(semaphore, upward):
        for axis, p in enumerate((x, y)):
            for d in range(2):
                q = (p + 1 + 2 * d) % side
                near, far = (distance(p), distance(q)) if upward else (distance(q), distance(p))

                @pl.when(near < far)
                def _():
                    pl.semaphore_signal(
                        semaphore, inc=1, device_id={"grid": neighbour(axis, d)}, device_id_type=MESH
                    )

    greet(barrier, True)
    for dz in range(1, freq_devices):

        @pl.when(z + dz < freq_devices)
        def _():
            pl.semaphore_signal(barrier, inc=1, device_id={"freq": z + dz}, device_id_type=MESH)

    load_owner = pltpu.make_async_copy(owner, owner_row, local_sem.at[4])
    load_pairs = pltpu.make_async_copy(pairs, pair_rows, local_sem.at[5])
    load_psd = pltpu.make_async_copy(psd_hbm, psd, local_sem.at[6])
    load_green = pltpu.make_async_copy(green.at[:, c], green_own, local_sem.at[0])
    load_cross = pltpu.make_async_copy(green.at[:, 1 - c], green_cross, local_sem.at[1])
    load_table = pltpu.make_async_copy(table.at[z * 2 + c], phi, local_sem.at[2])
    load_obs = pltpu.make_async_copy(observed, obs, local_sem.at[3])
    load_owner.start()
    load_pairs.start()
    load_psd.start()
    load_cross.start()
    load_green.start()
    load_table.start()
    pl.semaphore_wait(barrier, 1 + lower + z)

    swap_psd = remote(psd_hbm, psd_other, core_send.at[2], core_recv.at[2], other)
    parts = 4
    blocks = green.shape[2]

    def swap_green(n):
        k, some = n // parts, pl.ds(n % parts * (blocks // parts), blocks // parts)
        return remote(
            green.at[k, 1 - c, some], green_other.at[k, some], green_send.at[0], green_recv.at[n], other
        )

    swap_psd.start()
    for n in range(3):
        swap_green(n).start()

    greet(near_here, False)
    for dz in range(1, freq_devices):

        @pl.when(z >= dz)
        def _():
            pl.semaphore_signal(z_here, inc=1, device_id={"freq": z - dz}, device_id_type=MESH)

    def weigh(k, first, count, source, result, row):
        def body(b, carry):
            for i in range(4):
                place = first + 4 * b + i
                result[k, place] = (source[k, place].astype(f32) * row).astype(bf16)
            return carry

        lax.fori_loop(0, count // 4, body, 0)

    def cross_parts(left, right):
        acc = lax.dot_general(left, right, (((1,), (1,)), ((), ())), preferred_element_type=f32)
        return acc[:block, :block] + acc[block:, block:], acc[block:, :block] - acc[:block, block:]

    load_owner.wait()
    load_pairs.wait()
    square = (slot_count, slot_count)
    across = lax.broadcasted_iota(jnp.int32, square, 1)
    along = lax.broadcasted_iota(jnp.int32, square, 0)

    def down(row):
        return jnp.sum(jnp.where(across == along, jnp.broadcast_to(row, square), 0), axis=1, keepdims=True)

    their_owner = jnp.broadcast_to(owner_row[...], square)
    my_owner = down(owner_row[...])
    earlier = (their_owner < my_owner) | ((their_owner == my_owner) & (across < along))
    ids_row[...] = jnp.zeros_like(ids_row)
    entry_slot = jnp.sum(jnp.where(earlier, 1, 0), axis=1, keepdims=True)
    hit = entry_slot == across
    for k in range(2):
        chosen = jnp.where(hit, down(pair_rows[pl.ds(k, 1), :]), 0)
        ids_row[pl.ds(k, 1), pl.ds(0, slot_count)] = jnp.sum(chosen, axis=0, keepdims=True)
    move_ids = pltpu.make_async_copy(ids_row, ids, local_sem.at[7])
    move_ids.start()

    def early_slots(t, j):
        return [slot_of(t, u % 2, 2, lane(u // 2, j)) for u in range(4)]

    def swap_cross(e):
        some = pl.ds(4 * e, 4)
        return remote(
            cross_send.at[some], cross_recv.at[some], core_send.at[e], core_recv.at[e], other
        )

    load_psd.wait()
    cross_row = psd[pl.ds(1 - c, 1), :]
    load_cross.wait()
    move_ids.wait()
    for e, (t, j) in enumerate(early):
        for u, slot in enumerate(early_slots(t, j)):
            left = (green_cross[:, ids[0, slot]].astype(f32) * cross_row).astype(bf16)
            right = green_cross[:, ids[1, slot]]
            values = cross_parts(left.reshape(2 * block, points), right.reshape(2 * block, points))
            for k in range(2):
                cross_send[4 * e + u, k] = values[k].astype(bf16)
        swap_cross(e).start()
        if e == 0:
            swap_green(3).start()
    for n in range(4, 2 * parts):
        swap_green(n).start()
    load_obs.start()

    own_row = psd[pl.ds(c, 1), :]
    load_green.wait()
    for k in range(2):
        weigh(k, 0, blocks, green_own, weighted_own, own_row)
    for e, (t, j) in enumerate(early):
        shares = [
            cross_parts(
                weighted_own[:, ids[0, slot]].reshape(2 * block, points),
                green_own[:, ids[1, slot]].reshape(2 * block, points),
            )
            for slot in early_slots(t, j)
        ]
        swap_cross(e).wait_recv()
        first = t * 24 + j * 4
        for u, values in enumerate(shares):
            for k in range(2):
                send1[first + u, k] = (values[k] + cross_recv[4 * e + u, k].astype(f32)).astype(bf16)
        if e == 0:

            @pl.when(lower < side)
            def _():
                pl.semaphore_wait(near_here, side - lower)

        for u in range(4):
            copy1(first + u).start()

    load_table.wait()
    rows = phi.shape[0]
    row_in_group = lax.broadcasted_iota(jnp.int32, (rows, lags), 0) % group
    phi_values = phi[...].astype(f32)
    for i in range(group):
        spread[:, pl.ds(i * lags, lags)] = jnp.where(row_in_group == i, phi_values, 0.0).astype(bf16)

    recv1[48] = jnp.zeros_like(recv1[48])
    gsum[...] = jnp.zeros_like(gsum)
    mis_own[...] = jnp.zeros_like(mis_own)
    swap_psd.wait_recv()
    other_row = psd_other[pl.ds(c, 1), :]
    for n in range(2 * parts):
        swap_green(n).wait_recv()
        weigh(n // parts, n % parts * (blocks // parts), blocks // parts, green_other, weighted_other, other_row)

    def both(own, others, place):
        return jnp.concatenate((own[:, place], others[:, place]), axis=2).reshape(2 * block, 2 * points)

    def units(slots):
        return [
            cross_parts(
                both(weighted_own, weighted_other, ids[0, slot]),
                both(green_own, green_other, ids[1, slot]),
            )
            for slot in slots
        ]

    def wait_all(buffer, count, semaphore):
        some = buffer.at[pl.ds(0, count)]
        pltpu.make_async_copy(some, some, semaphore).wait()

    def wait1(i):
        wait_all(recv1, 4, one_recv.at[i])

    def choose(i, values):
        chosen = values[0]
        for n in range(1, len(values)):
            chosen = jnp.where(i >= n, values[n], chosen) if values[n] != values[n - 1] else chosen
        return chosen

    groups = [
        (0, 1, 1), (0, 0, 0), (0, 0, 1), (0, 1, 0), (2, 0, 0), (2, 0, 1),
        (1, 0, 0), (1, 0, 1), (2, 1, 0), (2, 1, 1), (1, 1, 0), (1, 1, 1),
    ]

    def first_ring(i, carry):
        part, t, j = (choose(i, [values[k] for values in groups]) for k in range(3))
        through = part == 1
        role = jnp.where(through, 2, part // 2)
        first = t * 24 + role * 8 + j * 4

        @pl.when(i == 6)
        def _():
            load_obs.wait()
            energies()

        @pl.when((i == 6) | (i == 8) | (i == 10))
        def _():
            project(jnp.where(i == 6, 0, jnp.where(i == 8, 1, 2)))

        @pl.when(through)
        def _():
            wait1(t * 2 + j)

        slots = []
        for u in range(4):
            h, d = u % 2, u // 2
            o = jnp.where(part == 0, 2, 1 + 2 * d)
            r = jnp.where(part == 2, lane(1 - d, j), lane(d, j))
            slots.append(slot_of(t, h, o, r))
        for u, values in enumerate(units(slots)):
            n = first + u
            with_n = jnp.where(through, n - 16, 48)
            for k in range(2):
                send1[n, k] = (values[k] + recv1[with_n, k].astype(f32)).astype(bf16)
        for u in range(4):
            copy1(first + u).start()
        return carry

    def arrival1(t, h, d, r):
        role = 2 - (r + d) % 2
        return t * 24 + role * 8 + lane_place(r) * 4 + d * 2 + h

    def line_sums(t, wanted):
        for r in sorted({r for h, r in wanted}):
            wait1(4 + t * 4 + r)
        sums = []
        for (h, r), values in zip(wanted, units([slot_of(t, h, 0, r) for h, r in wanted])):
            arrived = [recv1[arrival1(t, h, d, r)].astype(f32) for d in range(2)]
            sums.append([values[k] + (arrived[0][k] + arrived[1][k]) for k in range(2)])
        return sums

    def place(t, h, d):
        return (t * 2 + h) * 2 + d

    def copy_a(t, h, d):
        i = place(t, h, d)
        return remote(send_a.at[i], recv_a.at[i], a_send.at[0], a_recv.at[t], neighbour(1 - h, d))

    def copy_b(t, h, d, k):
        i = place(t, h, d)
        return remote(
            send_b.at[i, k], recv_b.at[i, k], b_send.at[0], b_recv.at[t], neighbour(1 - h, d)
        )

    def second_ring_far(t):
        for h, values in enumerate(line_sums(t, [(0, 2), (1, 2)])):
            for d in range(2):
                send_a[place(t, h, d)] = values[d].astype(bf16)
                copy_a(t, h, d).start()

    def second_ring_near(t):
        wanted = [(h, 1 + 2 * d) for d in range(2) for h in range(2)]
        for (h, r), values in zip(wanted, line_sums(t, wanted)):
            d = r // 2
            i = place(t, h, d)
            send_b[i, 1 - d] = values[1 - d].astype(bf16)
            copy_b(t, h, d, 1 - d).start()
            keep[i] = values[d]

    def own_part(t):
        for h, values in enumerate(line_sums(t, [(0, 0), (1, 0)])):
            for k in range(2):
                own_sum[t * 2 + h, k] = values[k]

    def second_ring_close(t):
        wait_all(recv_a, 4, a_recv.at[t])
        for d in range(2):
            for h in range(2):
                i = place(t, h, d)
                send_b[i, d] = (keep[i] + recv_a[i].astype(f32)).astype(bf16)
                copy_b(t, h, d, d).start()

    def copy_g1(t, h, d):
        s = slot_of(t, h, 0, 0)
        return remote(abuf.at[s], abuf.at[s], g_send.at[0], g1_recv.at[t], neighbour(1 - h, d))

    def copy_g1f(t, h, d):
        s = slot_of(t, h, 0, 3 - 2 * d)
        return remote(abuf.at[s, d], abuf.at[s, d], g_send.at[0], g1f_recv.at[t], neighbour(1 - h, d))

    def copy_g2(t, h, d, r):
        s = slot_of(t, h, 0, r)
        return remote(abuf.at[s], abuf.at[s], g_send.at[0], g2_recv.at[t * 4 + r], neighbour(h, d))

    def copy_g2f(t, h, d, j):
        r = lane(d, j)
        s = slot_of(t, h, 3 - 2 * d, r)
        return remote(abuf.at[s], abuf.at[s], g_send.at[0], g2f_recv.at[r], neighbour(h, d))

    ones = jnp.ones((8, block), f32)

    def lane_sum(values):
        return lax.dot_general(
            ones[:, : values.shape[1]], values, (((1,), (1,)), ((), ())),
            precision=lax.Precision.HIGHEST, preferred_element_type=f32,
        )

    def own_adjoint(t, carry):
        wait_all(recv_b, 4, b_recv.at[t])
        for h in range(2):
            s, q = slot_of(t, h, 0, 0), h * 2 + t
            kept = jnp.zeros((block, block), f32)
            for k in range(2):
                value = own_sum[t * 2 + h, k]
                for d in range(2):
                    value = value + recv_b[place(t, h, d), k].astype(f32)
                cross = value * f32(root_scale)
                seen = ohat[q, k]
                abuf[s, k] = (0.5 * cross - seen * f32(1.0 / lags)).astype(bf16)
                kept = kept + cross * (f32(lags / 2) * cross - 2.0 * seen)
            for d in range(2):
                copy_g1(t, h, d).start()
            total[q] = kept
        for h in range(2):
            for d in range(2):
                copy_g2(t, h, d, 0).start()
        return carry

    def gather_1(t):
        wait_all(abuf, 4, g1_recv.at[t])

        for h in range(2):
            for d in range(2):
                copy_g1f(t, h, d).start()
        for d in range(2):
            for h in range(2):
                for side_d in range(2):
                    copy_g2(t, h, side_d, 3 - 2 * d).start()

    def gather_2(t):
        wait_all(abuf, 2, g1f_recv.at[t])
        for h in range(2):
            for d in range(2):
                copy_g2(t, h, d, 2).start()

    def gather_lane(t, r):
        wait_all(abuf, 4, g2_recv.at[t * 4 + r])
        for h in range(2):
            copy_g2f(t, h, r % 2, lane_place(r)).start()

    def gather_end(r):
        wait_all(abuf, 4, g2f_recv.at[r])

    def back(slots, carry, of_block, count):
        for s in slots:
            weights = abuf[s]
            top = jnp.concatenate((weights[0], -weights[1]), axis=1)
            low = jnp.concatenate((weights[1], weights[0]), axis=1)
            right = of_block(ids[1, s])
            moved = jnp.dot(
                jnp.concatenate((top, low), axis=0), right, preferred_element_type=f32
            )
            left = of_block(ids[0, s]).astype(f32)
            carry = carry + jnp.sum((moved * left).reshape(2 * block // 8, 8, count), axis=0)
        return carry

    def project(quarter):
        chunks = block // group // 4

        def body(i, carry):
            first = pl.multiple_of((quarter * chunks + i) * group, group)
            seen = jnp.concatenate(
                [
                    jnp.concatenate([obs[s, first + k] for k in range(group)], axis=1)
                    for s in range(pair_dev)
                ],
                axis=0,
            )
            out = lax.dot_general(
                spread[...], seen, (((1,), (1,)), ((), ())), preferred_element_type=f32
            )
            out = jnp.sum(out.reshape(pieces, 4 * group, pair_dev * block), axis=0)
            for s in range(pair_dev):
                for k in range(2):
                    cols = slice(s * block, (s + 1) * block)
                    ohat[2 * c + s, k, pl.ds(first, group), :] = out[k * group : (k + 1) * group, cols]
                    ohat_send[s, k, pl.ds(first, group), :] = out[(2 + k) * group : (3 + k) * group, cols]
            return carry

        lax.fori_loop(0, chunks, body, 0, unroll=2)

    swap_ohat = remote(
        ohat_send, ohat.at[pl.ds(2 * c, 2)], core_send.at[3], core_recv.at[3], other
    )
    part_rows = block // freq_devices

    def energies():
        def body(i, carry):
            for s in range(pair_dev):
                seen = obs[s, z * part_rows + i].astype(f32)
                energy[pl.ds(s * part_rows + i, 1), :] = jnp.sum(seen * seen, axis=0, keepdims=True)
            return carry

        lax.fori_loop(0, part_rows, body, 0)

    swap_mis = remote(mis_own, mis_other, core_send.at[4], core_recv.at[4], other)

    def copy_z(dz):
        return pltpu.make_async_remote_copy(
            src_ref=mis_pair, dst_ref=mis_freq.at[dz - 1],
            send_sem=z_send.at[0], recv_sem=z_recv.at[0],
            device_id={"freq": (z + dz) % freq_devices}, device_id_type=MESH,
        )

    def misfit_parts():
        for q in range(2 * stages):
            mis_own[pl.ds(q, 1), :] = lane_sum(total[q])[:1]
        swap_mis.start()

    def misfit_sums():
        swap_mis.wait_recv()
        mis_pair[...] = mis_own[...] + mis_other[...]

        @pl.when(z < freq_devices - 1)
        def _():
            pl.semaphore_wait(z_here, freq_devices - 1 - z)

        for dz in range(1, freq_devices):
            copy_z(dz).start()

    def misfit_end():
        wait_all(mis_freq, freq_devices - 1, z_recv.at[0])
        mine = mis_pair[...]
        for dz in range(1, freq_devices):
            mine = mine + mis_freq[dz - 1]
        from_observed = lane_sum(energy[...])[:1]
        picked = jnp.zeros((mine.shape[0], part_rows), f32)
        for part in range(freq_devices):
            picked = jnp.where(z == part, mine[:, part * part_rows : (part + 1) * part_rows], picked)
        for s in range(pair_dev):
            row = jnp.where(c == 0, picked[s : s + 1], picked[2 + s : 3 + s])
            row = row + from_observed[:, s * part_rows : (s + 1) * part_rows]
            misfit_out[pl.ds(s, 1), :] = row * f32(1.0 / (2.0 * block * lags * freq_total))

    lax.fori_loop(len(early), 12, first_ring, 0)
    project(3)
    swap_ohat.start()
    own_part(0)
    second_ring_far(0)
    second_ring_near(0)
    second_ring_far(1)
    second_ring_close(0)
    second_ring_near(1)
    own_part(1)
    second_ring_close(1)
    swap_ohat.wait_recv()
    lax.fori_loop(0, 2, own_adjoint, 0)

    steps = [
        ([], (0, 1), (0, 0), (0, 0)),
        ([(misfit_parts,), (gather_1, 0)], (0, 0), (0, 0), (1, 2)),
        ([(gather_1, 1)], (1, 0), (0, 0), (1, 2)),
        ([(gather_lane, 0, 0)], (0, 0), (1, 2), (0, 0)),
        ([(gather_2, 0), (gather_lane, 1, 0)], (1, 0), (1, 2), (0, 0)),
        ([(gather_2, 1), (gather_lane, 0, 1)], (0, 0), (1, 2), (1, 0)),
        ([(gather_lane, 0, 3)], (0, 0), (1, 2), (3, 0)),
        ([(misfit_sums,)], (0, 1), (0, 0), (2, 0)),
        ([(gather_lane, 1, 1)], (1, 0), (1, 2), (1, 0)),
        ([(gather_lane, 1, 3)], (1, 0), (1, 2), (3, 0)),
        ([(gather_end, 0)], (0, 1), (2, 0), (0, 0)),
        ([(gather_lane, 0, 2)], (0, 0), (1, 2), (2, 0)),
        ([(gather_lane, 1, 2)], (1, 0), (1, 2), (2, 0)),
        ([(gather_end, 1)], (0, 1), (2, 0), (1, 0)),
        ([(gather_end, 3)], (0, 1), (2, 0), (3, 0)),
    ]

    def gather_step(i, carry):
        for n, step in enumerate(steps):
            if step[0]:
                @pl.when(i == n)
                def _(actions=tuple(step[0])):
                    for action in actions:
                        action[0](*action[1:])

        slots = []
        for u in range(4):
            t, o, r = (
                choose(i, [step[part][0] + u // 2 * step[part][1] for step in steps]) for part in (1, 2, 3)
            )
            slots.append(slot_of(t, u % 2, o, r))
        return back(slots, carry, lambda place: both(green_own, green_other, place), 2 * points)

    gsum[...] = lax.fori_loop(0, len(steps), gather_step, gsum[...])

    gather_end(2)
    last = [slot_of(t, h, 2, 2) for t in range(stages) for h in range(2)]
    scale = f32(1.0 / (block * math.sqrt(slot_count)))

    def finish(buffer, first):
        sums = gsum[:, first : first + points]
        sums = back(last, sums, lambda place: buffer[:, place].reshape(2 * block, points), points)
        return jnp.sum(sums, axis=0, keepdims=True) * scale

    gsend[...] = jnp.broadcast_to(finish(green_other, points), gsend.shape)
    swap_sum = remote(gsend, grecv, core_send.at[5], core_recv.at[5], other)
    swap_sum.start()
    own_lines = finish(green_own, 0)
    misfit_end()
    row_ids = lax.broadcasted_iota(jnp.int32, (2, points), 0)
    swap_sum.wait_recv()
    gradient_out[...] = jnp.where(
        row_ids == c, jnp.broadcast_to(own_lines, (2, points)), grecv[:2]
    )

    swap_psd.wait_send()
    wait_all(green_other, 2, green_send.at[0])
    for e in range(len(early)):
        swap_cross(e).wait_send()
    swap_ohat.wait_send()
    swap_mis.wait_send()
    swap_sum.wait_send()
    wait_all(mis_freq, freq_devices - 1, z_send.at[0])
    wait_all(send1, 24 * stages, one_send.at[0])
    wait_all(send_a, 4 * stages, a_send.at[0])
    wait_all(send_b, 4 * stages, b_send.at[0])
    wait_all(abuf, 30 * stages, g_send.at[0])


def hand_on(gradient, misfit, gradient_out, misfit_out, sems):
    copies = [
        pltpu.make_async_copy(gradient, gradient_out, sems.at[0]),
        pltpu.make_async_copy(misfit, misfit_out, sems.at[1]),
    ]
    for copy in copies:
        copy.start()
    for copy in copies:
        copy.wait()


def local(green_spectra, source_psd, pair_list, owner_map, observed):
    freq_devices = lax.axis_size("freq")
    planes, freq_dev, stations, points = green_spectra.shape
    pair_dev, block, unused_cols, lags = observed.shape
    slot_count = owner_map.shape[0]
    blocks = stations // block
    freq_total = freq_dev * freq_devices
    table = jnp.asarray(phase_table(freq_total, lags, freq_devices))
    rows = table.shape[1]
    units = stages * 2 * 2
    dma = pltpu.SemaphoreType.DMA
    vmem = pl.BlockSpec(memory_space=pltpu.VMEM)
    hbm = pl.BlockSpec(memory_space=pltpu.HBM)
    pair = (2, block, block)
    gradient, misfit = pl.pallas_call(
        functools.partial(kernel, freq_devices),
        out_shape=(
            jax.ShapeDtypeStruct((freq_dev, points), f32),
            jax.ShapeDtypeStruct((pair_dev, block // freq_devices), f32),
        ),
        in_specs=[hbm] * 6,
        out_specs=(vmem, vmem),
        scratch_shapes=[
            pltpu.VMEM((2, blocks, block, points), bf16),
            pltpu.VMEM((2, blocks, block, points), bf16),
            pltpu.VMEM((2, blocks, block, points), bf16),
            pltpu.VMEM((2, blocks, block, points), bf16),
            pltpu.VMEM((2, blocks, block, points), bf16),
            pltpu.VMEM((8,) + pair, bf16),
            pltpu.VMEM((8,) + pair, bf16),
            pltpu.VMEM((freq_dev, points), f32),
            pltpu.VMEM((freq_dev, points), f32),
            pltpu.VMEM((1, slot_count), jnp.int32),
            pltpu.VMEM((2, slot_count), jnp.int32),
            pltpu.VMEM((8, 128), jnp.int32),
            pltpu.SMEM((8, 128), jnp.int32),
            pltpu.VMEM((pair_dev, block, block, lags), bf16),
            pltpu.VMEM((rows, lags), bf16),
            pltpu.VMEM((rows, group * lags), bf16),
            pltpu.VMEM((2 * pair_dev,) + pair, f32),
            pltpu.VMEM((pair_dev,) + pair, f32),
            pltpu.VMEM((pair_dev * (block // freq_devices), lags), f32),
            pltpu.VMEM((24 * stages,) + pair, bf16),
            pltpu.VMEM((24 * stages + 1,) + pair, bf16),
            pltpu.VMEM((units, block, block), bf16),
            pltpu.VMEM((units, block, block), bf16),
            pltpu.VMEM((units,) + pair, bf16),
            pltpu.VMEM((units,) + pair, bf16),
            pltpu.VMEM((units, block, block), f32),
            pltpu.VMEM((2 * stages,) + pair, f32),
            pltpu.VMEM((slot_count,) + pair, bf16),
            pltpu.VMEM((2 * stages, block, block), f32),
            pltpu.VMEM((8, block), f32),
            pltpu.VMEM((8, block), f32),
            pltpu.VMEM((8, block), f32),
            pltpu.VMEM((freq_devices - 1, 8, block), f32),
            pltpu.VMEM((8, 2 * points), f32),
            pltpu.VMEM((8, points), f32),
            pltpu.VMEM((8, points), f32),
            dma((8,)),
            dma((6,)),
            dma((6,)),
            dma((1,)),
            dma((8,)),
            dma((1,)),
            dma((6 * stages,)),
            dma((1,)),
            dma((stages,)),
            dma((1,)),
            dma((stages,)),
            dma((1,)),
            dma((stages,)),
            dma((stages,)),
            dma((4 * stages,)),
            dma((4,)),
            dma((1,)),
            dma((1,)),
            pltpu.SemaphoreType.REGULAR,
            pltpu.SemaphoreType.REGULAR,
        ],
        compiler_params=pltpu.CompilerParams(
            collective_id=0, has_side_effects=True, vmem_limit_bytes=60 * 1024 * 1024
        ),
        cost_estimate=pl.CostEstimate(
            flops=8 * slot_count * freq_dev * 2 * block * block * points,
            bytes_accessed=12 * 1024 * 1024,
            transcendentals=0,
        ),
        name="misfit_gradient",
    )(
        owner_map.reshape(1, slot_count),
        pair_list.T,
        source_psd,
        table,
        green_spectra.reshape(planes, freq_dev, blocks, block, points),
        observed,
    )
    return pl.pallas_call(
        hand_on,
        out_shape=(
            jax.ShapeDtypeStruct(gradient.shape, f32),
            jax.ShapeDtypeStruct(misfit.shape, f32),
        ),
        in_specs=[hbm, hbm],
        out_specs=(hbm, hbm),
        scratch_shapes=[dma((2,))],
        name="hand_on",
    )(gradient, misfit)


def solution(mesh):
    in_specs = (
        P(None, "freq", None, "grid"),
        P("freq", "grid"),
        P(),
        P(),
        P("grid", None, None, None),
    )
    out_specs = (P("freq", "grid"), P("grid", "freq"))
    return jax.shard_map(local, mesh=mesh, in_specs=in_specs, out_specs=out_specs, check_vma=False)
```
